32 devices in a mesh: dp: 8 (over z, core), fsdp: 4 (over y, x).
Axes of the slice: x: 2, y: 2, z: 4, core: 2. Of those that a mesh axis runs over, the one named last changes fastest.
Arguments:
- tokens: bfloat16 [32768, 1024], P(('dp', 'fsdp')), may hold values from -6 to 6
- seq_lengths: int32 [32, 4], P(('dp', 'fsdp')), may hold values from 0 to 1024, as said below
- expert_ids: int32 [32768, 1], P(('dp', 'fsdp')), may hold values from 0 to 1; in each aligned block of 1024 rows (0 to 1023, 1024 to 2047, ...) at most 768 rows name the same one
- grad_out: bfloat16 [32768, 1024], P(('dp', 'fsdp')), may hold values from -6 to 6
- ln1_gain: bfloat16 [1024], P(('dp', 'fsdp')), may hold values from 0.5 to 1.5
- ln1_bias: bfloat16 [1024], P(('dp', 'fsdp')), may hold values from -1.5 to 1.5
- w_qkv: bfloat16 [1024, 3072], P(('dp', 'fsdp')), may hold values from -0.1875 to 0.1875
- w_attn_out: bfloat16 [1024, 1024], P(('dp', 'fsdp')), may hold values from -0.75 to 0.75
- ln2_gain: bfloat16 [1024], P(('dp', 'fsdp')), may hold values from 0.5 to 1.5
- ln2_bias: bfloat16 [1024], P(('dp', 'fsdp')), may hold values from -1.5 to 1.5
- w_expert_in: bfloat16 [2, 1024, 4096], P(None, ('dp', 'fsdp')), may hold values from -0.1875 to 0.1875
- w_expert_out: bfloat16 [2, 4096, 1024], P(None, ('dp', 'fsdp')), may hold values from -0.09375 to 0.09375
Outputs:
- block_out: bfloat16 [32768, 1024], P(('dp', 'fsdp'))
- grad_tokens: float32 [32768, 1024], P(('dp', 'fsdp'))
- grad_ln1_gain: float32 [1024], P(('dp', 'fsdp'))
- grad_ln1_bias: float32 [1024], P(('dp', 'fsdp'))
- grad_w_qkv: float32 [1024, 3072], P(('dp', 'fsdp'))
- grad_w_attn_out: float32 [1024, 1024], P(('dp', 'fsdp'))
- grad_ln2_gain: float32 [1024], P(('dp', 'fsdp'))
- grad_ln2_bias: float32 [1024], P(('dp', 'fsdp'))
- grad_w_expert_in: float32 [2, 1024, 4096], P(None, ('dp', 'fsdp'))
- grad_w_expert_out: float32 [2, 4096, 1024], P(None, ('dp', 'fsdp'))
The draws below stay inside these ranges and needn't reach their ends.
Inputs may be any that keep to these rules, and one draw needn't show every extreme that they name: `seq_lengths`: each row is either one sequence of 1024 tokens followed by zeros, or 4 lengths of at least 128 that sum to 1024; some row is a single sequence in every draw. `expert_ids`: at most 768 of one device's 1024 tokens name the same expert, and that many do on some device.
All inputs are finite; a program needn't handle non-finite values.
Results may differ from the reference program's by a relative error of at most 0.012.
Values may be sent and summed in bfloat16 or wider, within the bound.
A program may use at most 320 MiB of HBM per device.

```python
import math
import jax
import jax.numpy as jnp
import numpy as np
from jax import lax

D = 1024
HEADS = 16
HEAD_DIM = 64
FF = 4096
EXPERTS = 2
SEGS = 4
TOK_DEV = 1024
BLOCKS = 32
TOKENS = 32768
SHORT = 256
CAPACITY = 768


def draw_seq_lengths(key, part):
    key = jax.random.fold_in(key, 7)
    pick_key, spread_key, whole_key = jax.random.split(key, 3)
    half_span = SHORT // 2
    offsets = jax.random.randint(spread_key, (BLOCKS, SEGS // 2), -half_span, half_span + 1)
    paired = jnp.stack([SHORT + offsets, SHORT - offsets], axis=-1).reshape(BLOCKS, SEGS)
    single = jnp.zeros((BLOCKS, SEGS), jnp.int32).at[:, 0].set(TOK_DEV)
    chosen = jax.random.randint(whole_key, (BLOCKS,), 0, 2)
    forced = jax.random.randint(pick_key, (), 0, BLOCKS)
    chosen = jnp.where(jnp.arange(BLOCKS) == forced, 1, chosen)
    return jnp.where(chosen[:, None] == 1, single, paired).astype(jnp.int32)


def level_of(own_key, shape, shards, least, top_value):
    def one(dim, shards_of):
        heights = jax.random.uniform(jax.random.fold_in(jax.random.fold_in(own_key, 6), dim), (shards_of,), jnp.float32, least / len(shards), top_value / len(shards))
        return jnp.repeat(jnp.exp(heights), shape[dim] // shards_of).reshape((-1,) + (1,) * (len(shape) - dim - 1))

    factor_of = one(*shards[0])
    for cut in shards[1:]:
        factor_of = factor_of * one(*cut)
    return factor_of


def assign_block(stream_key, own, number, rows, number_of, top, reach, slope):
    sequence = jax.random.permutation(stream_key, number_of)
    heavy_load, usual = portions_of(number_of, rows * top, reach, slope, True), portions_of(number_of, rows * top, reach, slope, False)
    places = jnp.arange(number_of)

    def named(sizes, rotation):
        used = int((sizes > 0).sum())
        fixed = max(1, used // 4)
        passed = fixed + (places - fixed + rotation * (used - fixed)) % max(1, number_of - fixed)
        return jnp.zeros((number_of,), jnp.int32).at[sequence[jnp.where(places < fixed, places, passed)]].set(jnp.asarray(sizes, jnp.int32))

    sizes = jnp.where(number % 4 == 0, named(heavy_load, number // 4), named(usual, number - number // 4 - 1))
    mixed = jax.random.permutation(jax.random.fold_in(own, 3), number_of)
    donor, receiver = mixed[0:number_of // 2 * 2:2], mixed[1:number_of // 2 * 2:2]
    margin = jnp.minimum(sizes[donor] - 1, reach - sizes[receiver]) // 2
    margin = jnp.where((donor == sequence[0]) | (receiver == sequence[0]) | (sizes[receiver] == 0), 0, jnp.maximum(margin, 0))
    passed = jax.random.randint(jax.random.fold_in(own, 4), (number_of // 2,), 0, 1 << 20) % (margin + 1)
    sizes = sizes.at[donor].add(-passed).at[receiver].add(passed)
    members = jnp.searchsorted(jnp.cumsum(sizes), jnp.arange(rows * top), side="right").astype(jnp.int32)
    grid = members.reshape(top, rows).T
    grid = grid[jax.random.permutation(jax.random.fold_in(own, 1), rows)]
    rotation = jax.random.randint(jax.random.fold_in(own, 2), (rows, 1), 0, top)
    return jnp.take_along_axis(grid, (jnp.arange(top)[None, :] + rotation) % top, axis=1)


def portions_of(number_of, total, limit, lean, full):
    weights = [(1 << 20) // math.isqrt(standing ** lean) + 1 for standing in range(1, number_of + 1)]
    largest = limit if full else min(limit, max(-(-total // number_of), total * weights[0] // sum(weights)))
    least = 1 if total - largest >= number_of - 1 else 0
    holding, rest = [largest] + [least] * (number_of - 1), total - largest - least * (number_of - 1)
    while rest > 0:
        free = [i for i in range(1, number_of) if holding[i] < largest] or [i for i in range(1, number_of) if holding[i] < limit]
        pool, left = sum([weights[i] for i in free]), rest
        for i in free:
            extra = min(limit - holding[i], max(1, left * weights[i] // pool), rest)
            holding[i] = holding[i] + extra
            rest = rest - extra
    return np.array(holding)


def noise(own_key, shape, deviation, reach, cuts=(), kind=jnp.bfloat16):
    loudness = level_of(own_key, shape, cuts, -0.22, 0.18) if cuts else 1.0
    entries = jax.random.normal(own_key, shape, jnp.float32) * deviation * loudness
    return jnp.minimum(jnp.maximum(entries, -reach), reach).astype(kind)


def setup_inputs(seed: int = 0) -> dict:
    key_list = jax.random.split(jax.random.key(seed), 13)
    tokens = noise(key_list[0], (TOKENS, D), 1.0, 6.0, ((0, 32),))
    seq_lengths = draw_seq_lengths(jax.random.fold_in(key_list[12], 71), 0)
    expert_ids_keys = jax.random.split(jax.random.fold_in(key_list[2], 1), TOKENS // TOK_DEV)
    expert_ids_turns = jax.random.permutation(jax.random.fold_in(key_list[2], 3), TOKENS // TOK_DEV)
    expert_ids = jax.vmap(lambda own, number: assign_block(jax.random.fold_in(key_list[2], 2), own, number, TOK_DEV, EXPERTS, 1, CAPACITY, 1))(expert_ids_keys, expert_ids_turns).reshape((TOKENS, 1))
    grad_out = noise(key_list[3], (TOKENS, D), 1.0, 6.0, ((0, 32),))
    ln1_gain = jnp.clip(1.0 + 0.1 * jax.random.normal(key_list[4], (D,), jnp.float32), 0.5, 1.5).astype(jnp.bfloat16)
    ln1_bias = noise(key_list[5], (D,), 0.3, 1.5, ((0, 32),))
    w_qkv = noise(key_list[6], (D, 3 * D), D ** -0.5, 0.1875, ((0, 32),))
    w_attn_out = noise(key_list[7], (D, D), (D // 16) ** -0.5, 0.75, ((0, 32),))
    ln2_gain = jnp.clip(1.0 + 0.1 * jax.random.normal(key_list[8], (D,), jnp.float32), 0.5, 1.5).astype(jnp.bfloat16)
    ln2_bias = noise(key_list[9], (D,), 0.3, 1.5, ((0, 32),))
    w_expert_in = noise(key_list[10], (EXPERTS, D, FF), D ** -0.5, 0.1875, ((1, 32),))
    w_expert_out = noise(key_list[11], (EXPERTS, FF, D), FF ** -0.5, 0.09375, ((1, 32),))
    return dict(tokens=tokens, seq_lengths=seq_lengths, expert_ids=expert_ids, grad_out=grad_out, ln1_gain=ln1_gain, ln1_bias=ln1_bias, w_qkv=w_qkv, w_attn_out=w_attn_out, ln2_gain=ln2_gain, ln2_bias=ln2_bias, w_expert_in=w_expert_in, w_expert_out=w_expert_out)


@jax.custom_vjp
def low(v):
    return lax.optimization_barrier(v.astype(jnp.bfloat16)).astype(jnp.float32)

@jax.custom_vjp
def low_back(v):
    return v

def low_keep(v):
    return (low(v), None)

def low_pass(kept, grad):
    return (grad,)

def back_keep(v):
    return (v, None)

def back_low(kept, grad):
    return (low(grad),)
low.defvjp(low_keep, low_pass)
low_back.defvjp(back_keep, back_low)
EPSILON = 1e-05
MASKED = -1000000000.0
HIGHEST = lax.Precision.HIGHEST

def layer_norm(values, gain, shift):
    average = lax.optimization_barrier(jnp.mean(values, axis=-1, keepdims=True))
    centred = values - average
    variance = lax.optimization_barrier(jnp.mean(centred * centred, axis=-1, keepdims=True))
    return centred * lax.rsqrt(variance + EPSILON) * gain + shift

def allowed_pairs(lengths_row, row_count):
    bounds = jnp.cumsum(lengths_row).astype(jnp.int32)
    positions = jnp.arange(row_count, dtype=jnp.int32)
    segment = lax.optimization_barrier(jnp.sum((positions[:, None] >= bounds[None, :]).astype(jnp.int32), axis=1))
    return (segment[:, None] == segment[None, :]) & (positions[None, :] <= positions[:, None])

def block_forward(params, tokens_blk, lengths_row, routes_row):
    gain_one, bias_one, qkv_weight, attn_weight, gain_two, bias_two, in_weight, out_weight = params
    row_count = tokens_blk.shape[0]
    normed_one = low(layer_norm(tokens_blk, gain_one, bias_one))
    projected = low(low_back(jnp.dot(normed_one, qkv_weight, precision=HIGHEST)))
    queries = projected[:, :D].reshape(row_count, HEADS, HEAD_DIM)
    keys_all = projected[:, D:2 * D].reshape(row_count, HEADS, HEAD_DIM)
    values_all = projected[:, 2 * D:].reshape(row_count, HEADS, HEAD_DIM)
    raw_scores = low_back(jnp.einsum('qhd,khd->hqk', queries, keys_all, precision=HIGHEST) * HEAD_DIM ** (-0.5))
    scores = jnp.where(allowed_pairs(lengths_row, row_count)[None], raw_scores, MASKED)
    attend = low(jax.nn.softmax(scores, axis=-1))
    mixed_rows = jnp.einsum('hqk,khd->qhd', attend, values_all, precision=HIGHEST).reshape(row_count, D)
    mixed_rows = low(low_back(mixed_rows))
    hidden_one = tokens_blk + low_back(jnp.dot(mixed_rows, attn_weight, precision=HIGHEST))
    normed_two = low(layer_norm(hidden_one, gain_two, bias_two))
    result = hidden_one
    for expert in range(EXPERTS):
        inner_sums = low_back(jnp.dot(normed_two, in_weight[expert], precision=HIGHEST))
        active = low(jax.nn.gelu(inner_sums))
        branch = low_back(jnp.dot(active, out_weight[expert], precision=HIGHEST))
        result = result + jnp.where((routes_row[:, 0] == expert)[:, None], branch, 0.0)
    return result

def reference(tokens, seq_lengths, expert_ids, grad_out, ln1_gain, ln1_bias, w_qkv, w_attn_out, ln2_gain, ln2_bias, w_expert_in, w_expert_out):
    params = tuple((weight.astype(jnp.float32) for weight in (ln1_gain, ln1_bias, w_qkv, w_attn_out, ln2_gain, ln2_bias, w_expert_in, w_expert_out)))
    tokens_all = tokens.astype(jnp.float32).reshape(BLOCKS, TOK_DEV, D)
    routes_all = expert_ids.reshape(BLOCKS, TOK_DEV, 1)

    def forward(tokens_in, weights):

        def one_block(inputs):
            return block_forward(weights, inputs[0], inputs[1], inputs[2])
        return lax.map(jax.checkpoint(one_block), (tokens_in, seq_lengths, routes_all))
    outputs, pullback = jax.vjp(forward, tokens_all, params)
    grad_input, grad_params = pullback(grad_out.astype(jnp.float32).reshape(BLOCKS, TOK_DEV, D))
    return (outputs.reshape(TOKENS, D).astype(jnp.bfloat16), grad_input.reshape(TOKENS, D), grad_params[0], grad_params[1], grad_params[2], grad_params[3], grad_params[4], grad_params[5], grad_params[6], grad_params[7])
```

```python
import functools

import jax
import jax.numpy as jnp
from jax import lax
from jax.experimental import pallas as pl
from jax.experimental.pallas import tpu as pltpu
from jax.sharding import PartitionSpec as P

HEADS = 16
HEAD_DIM = 64
EXPERTS = 2
EPSILON = 1e-05
MASKED = -1000000000.0
AXES = ("dp", "fsdp")
BLOCK = 128
TILE = 256
MIB = 1024 * 1024
F32 = jnp.float32
BF16 = jnp.bfloat16
NT = (((1,), (1,)), ((), ()))
TN = (((0,), (0,)), ((), ()))
ROOT_2_PI = 0.7978845608028654
CUBIC = 0.044715


def dot(a, b):
    return jnp.dot(a, b, preferred_element_type=F32)


def dot_nt(a, b):
    return lax.dot_general(a, b, NT, preferred_element_type=F32)


def dot_tn(a, b):
    return lax.dot_general(a, b, TN, preferred_element_type=F32)


def norm_parts(values):
    average = jnp.mean(values, axis=-1, keepdims=True)
    centred = values - average
    variance = jnp.mean(centred * centred, axis=-1, keepdims=True)
    inverse = lax.rsqrt(variance + EPSILON)
    return (centred * inverse, inverse)


def norm_back(grad_normed, scaled, inverse, gain):
    grad_scaled = grad_normed * gain
    middle = jnp.mean(grad_scaled, axis=-1, keepdims=True)
    along = jnp.mean(grad_scaled * scaled, axis=-1, keepdims=True)
    return inverse * (grad_scaled - middle - scaled * along)


class Moves:
    def __init__(self, nd, nf):
        self.nz, self.nf = nd // 2, nf
        bits = []
        bit = 1
        while bit < nf:
            bits.append(bit)
            bit *= 2
        self.orders = (tuple(bits), tuple(reversed(bits)))

    def send(self, value, where):
        pairs = []
        for zed in range(self.nz):
            for core in range(2):
                for flat in range(self.nf):
                    z_to, core_to, f_to = where(zed, core, flat)
                    pairs.append(
                        (
                            (zed * 2 + core) * self.nf + flat,
                            (z_to * 2 + core_to) * self.nf + f_to,
                        )
                    )
        return lax.ppermute(value, AXES, pairs)

    def core(self, value):
        return self.send(value, lambda z, c, f: (z, 1 - c, f))

    def flat(self, value, bit):
        return self.send(value, lambda z, c, f: (z, c, f ^ bit))

    def along(self, value, steps):
        return self.send(value, lambda z, c, f: ((z + steps) % self.nz, c, f))

    def near(self, value, bit):
        return self.send(value, lambda z, c, f: (z ^ bit, c, f))

    def relative(self, stream):
        offsets = [0]
        for bit in reversed(self.orders[stream]):
            offsets = offsets + [one ^ bit for one in offsets]
        return tuple(offsets)

    def gather_z(self, value):
        return [value] + [self.along(value, k) for k in range(1, self.nz)]

    def gather_z_pair(self, value):
        held, bit = value[:, None], 1
        while 2 * bit < self.nz:
            held = jnp.concatenate([held, self.near(held, bit)], axis=1)
            bit *= 2
        got = self.near(held, bit)
        return [jnp.concatenate([held[n], got[n]], axis=0) for n in range(2)], got

    def gather_first(self, value, stream):
        held = value[None]
        for bit in tuple(reversed(self.orders[stream]))[:-1]:
            held = jnp.concatenate([held, self.flat(held, bit)], axis=0)
        return held

    def gather_last(self, held, stream):
        return self.flat(held, self.orders[stream][0])

    def reduce_flat(self, keep, sent, stream):
        order = self.orders[stream]
        now = add_low(keep, self.flat(sent, order[0]))
        for bit in order[1:]:
            half = now.shape[0] // 2
            now = add_low(now[:half], self.flat(now[half:], bit))
        return now[0]

    def reduce_z(self, value):
        total = value[0].astype(F32)
        for k in range(1, self.nz):
            total = total + self.along(value[k], k).astype(F32)
        return total

    def reduce_z_pair(self, value):
        bit = self.nz // 2
        while bit > 1:
            value = add_low(value[:bit], self.near(value[bit:], bit))
            bit //= 2
        return value[0].astype(F32) + self.near(value[1], 1).astype(F32)


def after(value, *others):
    return lax.optimization_barrier((value,) + others)[0]


def add_low(a, b):
    return (a.astype(F32) + b.astype(F32)).astype(BF16)


def attention_forward_kernel(seg_row, seg_col, q, k, v, out, stats, bias):
    rows = q.shape[0]
    pair = pl.program_id(0)
    lane = lax.broadcasted_iota(jnp.int32, (1, BLOCK), 1)

    @pl.when(pair == 0)
    def _():
        stats[...] = jnp.zeros_like(stats)
        for i in range(rows // TILE):
            span = (i + 1) * TILE
            place = slice(i * TILE, span)
            query = lax.broadcasted_iota(jnp.int32, (TILE, span), 0) + i * TILE
            key = lax.broadcasted_iota(jnp.int32, (TILE, span), 1)
            same = seg_col[place, 0:1] == seg_row[0:1, :span]
            bias[place, :span] = jnp.where(same & (key <= query), 0.0, MASKED)

    for i in range(rows // TILE):
        span = (i + 1) * TILE
        place = slice(i * TILE, span)
        query = q[place, :] * jnp.asarray(HEAD_DIM**-0.5, BF16)
        mixed = jnp.zeros((TILE, BLOCK), F32)
        held = stats[place, :]
        for side in range(2):
            mine = (lane // HEAD_DIM) == side
            part = jnp.where(mine, query, jnp.zeros_like(query))
            scores = dot_nt(part, k[:span, :]) + bias[place, :span]
            highest = jnp.max(scores, axis=1, keepdims=True)
            terms = jnp.exp(scores - highest)
            total = jnp.sum(terms, axis=1, keepdims=True)
            attend = (terms * (1.0 / total)).astype(BF16)
            mixed = jnp.where(mine, dot(attend, v[:span, :]), mixed)
            held = jnp.where(lane == 2 * pair + side, highest + jnp.log(total), held)
        stats[place, :] = held
        out[place, :] = mixed.astype(BF16)


def attention_forward(projected, seg_row, seg_col, first, count):
    rows, width = projected.shape[0], projected.shape[1] // 3
    pairs = width // BLOCK
    column = lambda start: pl.BlockSpec((rows, BLOCK), lambda h: (0, start + h))
    whole = lambda shape: pl.BlockSpec(shape, lambda h: (0, 0))
    return pl.pallas_call(
        attention_forward_kernel,
        grid=(count,),
        in_specs=[
            whole((8, rows)),
            whole((rows, BLOCK)),
            column(first),
            column(first + pairs),
            column(first + 2 * pairs),
        ],
        out_specs=[column(0), whole((rows, BLOCK))],
        out_shape=[
            jax.ShapeDtypeStruct((rows, count * BLOCK), BF16),
            jax.ShapeDtypeStruct((rows, BLOCK), F32),
        ],
        scratch_shapes=[pltpu.VMEM((rows, rows), F32)],
        compiler_params=pltpu.CompilerParams(vmem_limit_bytes=40 * MIB),
        cost_estimate=pl.CostEstimate(
            flops=4 * rows * rows * count * BLOCK,
            bytes_accessed=8 * rows * count * BLOCK,
            transcendentals=2 * count * rows * rows,
        ),
        name="attention_forward",
    )(seg_row, seg_col, projected, projected, projected)


def attention_backward_kernel(first, seg_row, seg_col, stats, q, k, v, g, dq, dk, dv, bias, dks, dvs):
    rows = q.shape[0]
    pair = pl.program_id(0)
    lane = lax.broadcasted_iota(jnp.int32, (1, BLOCK), 1)
    row = lax.broadcasted_iota(jnp.int32, (BLOCK, 1), 0)

    @pl.when(pair == 0)
    def _():
        for i in range(rows // TILE):
            span = (i + 1) * TILE
            place = slice(i * TILE, span)
            query = lax.broadcasted_iota(jnp.int32, (span, TILE), 1) + i * TILE
            key = lax.broadcasted_iota(jnp.int32, (span, TILE), 0)
            same = seg_col[:span, 0:1] == seg_row[0:1, place]
            bias[:span, place] = jnp.where(same & (key <= query), 0.0, MASKED)

    dks[...] = jnp.zeros_like(dks)
    dvs[...] = jnp.zeros_like(dvs)
    k_turned = k[...].T
    for i in range(rows // TILE):
        span = (i + 1) * TILE
        place = slice(i * TILE, span)
        query = q[place, :] * jnp.asarray(HEAD_DIM**-0.5, BF16)
        grad = g[place, :]
        turned = jnp.zeros((BLOCK, TILE), F32)
        for side in range(2):
            mine = (lane // HEAD_DIM) == side
            part = jnp.where(mine, query, jnp.zeros_like(query))
            grad_part = jnp.where(mine, grad, jnp.zeros_like(grad))
            level = stats[pl.ds(2 * (first + pair) + side, 1), place]
            scores = dot_nt(k[:span, :], part) + bias[:span, place]
            attend = jnp.exp(scores - level)
            grad_attend = dot_nt(v[:span, :], grad_part)
            inner = jnp.sum(attend * grad_attend, axis=0, keepdims=True)
            grad_scores = (attend * (grad_attend - inner)).astype(BF16)
            dks[:span, :] += dot(grad_scores, part)
            dvs[:span, :] += dot(attend.astype(BF16), grad_part)
            turned = jnp.where(
                (row // HEAD_DIM) == side, dot(k_turned[:, :span], grad_scores), turned
            )
        dq[place, :] = (turned.T * HEAD_DIM**-0.5).astype(BF16)
    dk[...] = dks[...].astype(BF16)
    dv[...] = dvs[...].astype(BF16)


def attention_backward(projected, grad_mixed, stats, seg_row, seg_col, first, count):
    rows, width = projected.shape[0], projected.shape[1] // 3
    pairs = width // BLOCK
    column = lambda start: pl.BlockSpec((rows, BLOCK), lambda h: (0, start + h))
    whole = lambda shape: pl.BlockSpec(shape, lambda h: (0, 0))
    share = jax.ShapeDtypeStruct((rows, count * BLOCK), BF16)
    return pl.pallas_call(
        functools.partial(attention_backward_kernel, first),
        grid=(count,),
        in_specs=[
            whole((8, rows)),
            whole((rows, BLOCK)),
            whole((BLOCK, rows)),
            column(first),
            column(first + pairs),
            column(first + 2 * pairs),
            column(first),
        ],
        out_specs=[column(0), column(0), column(0)],
        out_shape=[share, share, share],
        scratch_shapes=[
            pltpu.VMEM((rows, rows), F32),
            pltpu.VMEM((rows, BLOCK), F32),
            pltpu.VMEM((rows, BLOCK), F32),
        ],
        compiler_params=pltpu.CompilerParams(vmem_limit_bytes=40 * MIB),
        cost_estimate=pl.CostEstimate(
            flops=10 * rows * rows * count * BLOCK,
            bytes_accessed=14 * rows * count * BLOCK,
            transcendentals=2 * count * rows * rows,
        ),
        name="attention_backward",
    )(seg_row, seg_col, stats, projected, projected, projected, grad_mixed)


class Copies:
    def __init__(self, send_sems, recv_sems):
        self.send_sems, self.recv_sems, self.made = send_sems, recv_sems, []

    def start(self, source, target, device):
        n = len(self.made)
        one = pltpu.make_async_remote_copy(
            src_ref=source,
            dst_ref=target,
            send_sem=self.send_sems.at[n],
            recv_sem=self.recv_sems.at[n],
            device_id=device,
            device_id_type=pl.DeviceIdType.MESH,
        )
        one.start()
        self.made.append(one)
        return one


def wait_in(copies):
    for one in copies:
        one.wait_recv()


def forward_kernel(
    moves,
    tokens,
    mine,
    own_in,
    their_in,
    own_out,
    seg_row,
    seg_col,
    out_qkv,
    out_attn,
    out_params,
    first_in,
    first_out,
    column_in,
    column_out,
    normed,
    projected,
    mixed,
    stats,
    weights,
    bias,
    send_sems,
    recv_sems,
    local_sems,
):
    nz, nf = moves.nz, moves.nf
    dp, flat = lax.axis_index("dp"), lax.axis_index("fsdp")
    zed, core = dp // 2, lax.rem(dp, 2)
    rows, wide = tokens.shape
    sibling = (zed * 2 + 1 - core, flat)
    others = [(lax.rem(zed + k, nz) * 2 + core, flat) for k in range(1, nz)]
    hops = {bit: (dp, flat ^ bit) for bit in moves.orders[0]}

    barrier = pltpu.get_barrier_semaphore()
    for device in [sibling] + others + list(hops.values()):
        pl.semaphore_signal(barrier, inc=1, device_id=device, device_id_type=pl.DeviceIdType.MESH)
    pl.semaphore_wait(barrier, 1 + len(others) + len(hops))

    remote = Copies(send_sems, recv_sems)
    local = []

    def local_start(source, target):
        one = pltpu.make_async_copy(source, target, local_sems.at[len(local)])
        one.start()
        local.append(one)
        return one

    own = local_start(mine, weights.at[zed, core, flat])
    column = [remote.start(mine, weights.at[zed, core, flat], device) for device in others]
    crossed = [
        remote.start(their_in.at[0], first_in.at[zed, core, flat], sibling),
        remote.start(their_in.at[1], column_in.at[zed, core], sibling),
    ]
    blocks = [
        local_start(own_in.at[0], first_in.at[zed, core, flat]),
        local_start(own_out.at[0], first_out.at[zed, flat]),
        local_start(own_in.at[1], column_in.at[zed, core]),
        local_start(own_out.at[1], column_out.at[zed]),
    ]

    for i in range(rows // TILE):
        span = (i + 1) * TILE
        place = slice(i * TILE, span)
        query = lax.broadcasted_iota(jnp.int32, (TILE, span), 0) + i * TILE
        key = lax.broadcasted_iota(jnp.int32, (TILE, span), 1)
        same = seg_col[place, 0:1] == seg_row[0:1, :span]
        bias[place, :span] = jnp.where(same & (key <= query), 0.0, MASKED)
    stats[...] = jnp.zeros_like(stats)

    def stream_columns(stream):
        return slice(0, 2 * wide) if stream == 0 else slice(2 * wide, 4 * wide + BLOCK)

    def send_weights(stream, owner, device):
        place = weights.at[:, core, owner, :, stream_columns(stream)]
        return remote.start(place, place, device)

    own.wait()
    wait_in(column)
    near = [tuple(reversed(moves.orders[n]))[0] for n in range(2)]
    far = [moves.orders[n][0] for n in range(2)]
    hop_near = [send_weights(n, flat, hops[near[n]]) for n in range(2)]
    hop_far = [send_weights(n, flat, hops[far[n]]) for n in range(2)]
    place = weights.at[:, core, flat]
    across = [remote.start(place, place, sibling)]

    wait_in(crossed)
    for one in blocks:
        one.wait()
    first_column = []
    for device in others:
        place = first_in.at[zed, :, flat]
        first_column.append(remote.start(place, place, device))
        first_column.append(remote.start(own_out.at[0], first_out.at[zed, flat], device))

    wait_in(hop_near)
    hop_last = [send_weights(n, flat ^ near[n], hops[far[n]]) for n in range(2)]
    across += [send_weights(n, flat ^ near[n], sibling) for n in range(2)]
    wait_in(hop_far)
    across += [send_weights(n, flat ^ far[n], sibling) for n in range(2)]
    wait_in(hop_last)
    across += [send_weights(n, flat ^ near[n] ^ far[n], sibling) for n in range(2)]

    def send_first(stream, owner, device):
        place = first_in.at[:, :, owner] if stream == 0 else first_out.at[:, owner]
        return remote.start(place, place, device)

    wait_in(first_column)
    first_near = [send_first(n, flat, hops[near[n]]) for n in range(2)]
    first_far = [send_first(n, flat, hops[far[n]]) for n in range(2)]
    second_column = []
    for device in others:
        place = column_in.at[zed]
        second_column.append(remote.start(place, place, device))
        second_column.append(remote.start(own_out.at[1], column_out.at[zed], device))

    wait_in(across)
    whole = 2 * nz * nf * mine.shape[0]
    writes = [
        local_start(weights.at[:, :, :, :, pl.ds(0, 3 * wide)], out_qkv),
        local_start(weights.at[:, :, :, :, pl.ds(3 * wide, wide)], out_attn),
        local_start(weights.at[:, :, :, :, pl.ds(4 * wide, BLOCK)], out_params),
    ]
    turned = weights[:, :, :, :, pl.ds(4 * wide, BLOCK)].reshape(whole, BLOCK).astype(F32).T
    gain, shift = turned[0:1, :], turned[1:2, :]

    @pl.loop(0, rows // TILE)
    def _(t):
        place = pl.ds(pl.multiple_of(t * TILE, TILE), TILE)
        scaled, _ = norm_parts(tokens[place, :].astype(F32))
        normed[place, :] = (scaled * gain + shift).astype(BF16)
        for part in range(3):
            columns = pl.ds(part * wide, wide)
            matrix = weights[:, :, :, :, columns].reshape(whole, wide)
            projected[place, columns] = dot(normed[place, :], matrix).astype(BF16)

    lane = lax.broadcasted_iota(jnp.int32, (1, BLOCK), 1)
    pairs = wide // BLOCK

    def attend_pair(pair):
        columns = [
            pl.ds(pl.multiple_of(n * wide + pair * BLOCK, BLOCK), BLOCK) for n in range(3)
        ]
        for i in range(rows // TILE):
            span = (i + 1) * TILE
            place = slice(i * TILE, span)
            query = projected[place, columns[0]] * jnp.asarray(HEAD_DIM**-0.5, BF16)
            result = jnp.zeros((TILE, BLOCK), F32)
            held = stats[place, :]
            for side in range(2):
                ours = (lane // HEAD_DIM) == side
                part = jnp.where(ours, query, jnp.zeros_like(query))
                scores = dot_nt(part, projected[:span, columns[1]]) + bias[place, :span]
                highest = jnp.max(scores, axis=1, keepdims=True)
                terms = jnp.exp(scores - highest)
                total = jnp.sum(terms, axis=1, keepdims=True)
                attend = (terms * (1.0 / total)).astype(BF16)
                result = jnp.where(ours, dot(attend, projected[:span, columns[2]]), result)
                held = jnp.where(lane == 2 * pair + side, highest + jnp.log(total), held)
            stats[place, :] = held
            mixed[place, columns[0]] = result.astype(BF16)

    @pl.loop(0, pairs // 4)
    def _(pair):
        attend_pair(pair)

    wait_in(first_near)
    first_last = [send_first(n, flat ^ near[n], hops[far[n]]) for n in range(2)]

    @pl.loop(pairs // 4, pairs)
    def _(pair):
        attend_pair(pair)

    wait_in(first_far)
    wait_in(first_last)
    wait_in(second_column)
    for one in remote.made:
        one.wait_send()
    for one in writes:
        one.wait()


def forward_pass(moves, tokens, mine, own_in, their_in, own_out, seg_row, seg_col):
    nz, nf = moves.nz, moves.nf
    rows, wide = tokens.shape
    deep, half = own_in.shape[1:]
    part = own_out.shape[1]
    anywhere = pl.BlockSpec(memory_space=pl.ANY)
    inside = pl.BlockSpec(memory_space=pltpu.VMEM)
    shape = jax.ShapeDtypeStruct
    remote = 3 * (nz - 1) + 2 + 2 * 3 + 7 + 2 * (nz - 1) + 2 * 3
    return pl.pallas_call(
        functools.partial(forward_kernel, moves),
        in_specs=[inside] * 7,
        out_specs=[anywhere] * 7 + [inside] * 4,
        out_shape=[
            shape((nz, 2, nf, deep, 3 * wide), BF16),
            shape((nz, 2, nf, deep, wide), BF16),
            shape((nz, 2, nf, deep, BLOCK), BF16),
            shape((nz, 2, nf, deep, half), BF16),
            shape((nz, nf, part, wide), BF16),
            shape((nz, 2, deep, half), BF16),
            shape((nz, part, wide), BF16),
            shape((rows, wide), BF16),
            shape((rows, 3 * wide), BF16),
            shape((rows, wide), BF16),
            shape((rows, BLOCK), F32),
        ],
        scratch_shapes=[
            pltpu.VMEM((nz, 2, nf, deep, 4 * wide + BLOCK), BF16),
            pltpu.VMEM((rows, rows), F32),
            pltpu.SemaphoreType.DMA((remote,)),
            pltpu.SemaphoreType.DMA((remote,)),
            pltpu.SemaphoreType.DMA((8,)),
        ],
        compiler_params=pltpu.CompilerParams(
            collective_id=0, has_side_effects=True, vmem_limit_bytes=56 * MIB
        ),
        cost_estimate=pl.CostEstimate(
            flops=10 * rows * wide * wide, bytes_accessed=80 * wide * wide, transcendentals=0
        ),
        name="forward_pass",
    )(tokens, mine, own_in, their_in, own_out, seg_row, seg_col)


def attention_grads_kernel(
    moves, stream, deep, share, place, normed, mixed, dq, dk, dv, branch, near, far, low, sems
):
    zed, core, flat = place[0], place[1], place[2]
    for d in range(normed.shape[1] // TILE):
        rows = pl.ds(d * TILE, TILE)
        turned = normed[:, rows].T
        for n, part in enumerate((dq, dk, dv)):
            low[rows, pl.ds(n * share, share)] = dot(turned, part[...]).astype(BF16)
        low[rows, pl.ds(3 * share, share)] = dot(mixed[:, rows].T, branch[...]).astype(BF16)
    begun = []
    for number, offset in enumerate(moves.relative(stream)):
        for k in range(moves.nz):
            z_of = lax.rem(zed + k, moves.nz)
            for other in range(2):
                owner = core if other == 0 else 1 - core
                start = ((z_of * 2 + owner) * moves.nf + (flat ^ offset)) * deep
                rows = pl.ds(pl.multiple_of(start, deep), deep)
                target = (far if other else near).at[number, k]
                begun.append(
                    pltpu.make_async_copy(low.at[rows], target, sems.at[len(begun)])
                )
    for one in begun:
        one.start()
    for one in begun:
        one.wait()


def attention_grads(moves, stream, place, normed, mixed, dq, dk, dv, branch, deep):
    rows, wide = normed.shape
    share = dq.shape[1]
    anywhere = pl.BlockSpec(memory_space=pl.ANY)
    inside = pl.BlockSpec(memory_space=pltpu.VMEM)
    piece = jax.ShapeDtypeStruct((moves.nf, moves.nz, deep, 4 * share), BF16)
    return pl.pallas_call(
        functools.partial(attention_grads_kernel, moves, stream, deep, share),
        in_specs=[pl.BlockSpec(memory_space=pltpu.SMEM)] + [inside] * 6,
        out_specs=[anywhere] * 2,
        out_shape=[piece, piece],
        scratch_shapes=[
            pltpu.VMEM((wide, 4 * share), BF16),
            pltpu.SemaphoreType.DMA((2 * moves.nz * moves.nf,)),
        ],
        compiler_params=pltpu.CompilerParams(vmem_limit_bytes=40 * MIB),
        cost_estimate=pl.CostEstimate(
            flops=8 * rows * wide * share, bytes_accessed=20 * wide * share, transcendentals=0
        ),
        name="attention_grads",
    )(place, normed, mixed, dq, dk, dv, branch)


def gelu_both(value):
    square = value * value
    bent = jnp.tanh(ROOT_2_PI * value * (1.0 + CUBIC * square))
    half = 0.5 + 0.5 * bent
    slope = half + (0.5 * ROOT_2_PI) * value * (1.0 - bent * bent) * (1.0 + 3.0 * CUBIC * square)
    return (value * half, slope)


def expert_kernel(plan, *refs):
    moves, deep, chunk, chunks = plan[:4]
    expert, place, x_own, x_other, g_own, g_other = (plan[4],) + refs[:5]
    x_own, x_other, g_own, g_other = [
        one.at[expert] for one in (x_own, x_other, g_own, g_other)
    ]
    loaded = plan[5]
    weights, refs = refs[5 : 5 + loaded], refs[5 + loaded :]
    count = 4 if moves is not None else 2
    rows_out, refs = [refs[n // 2].at[n % 2] for n in range(4)], refs[2:]
    grads, refs = refs[:count], refs[count:]
    (win, wout, x, x_turned, g, branch, back, sum_in, sum_out, low_in, low_out, empty) = refs[:12]
    w_sems, x_sem, out_sems, row_sem = refs[12:]
    width = x.shape[1]
    most = x_own.shape[0] // BLOCK
    zed, flat, own_n, other_n = place[0], place[1], place[2], place[3]
    blocks = own_n + other_n
    tiles = (blocks + 1) // 2

    def block_rows(i):
        return pl.ds(pl.multiple_of(i * BLOCK, BLOCK), BLOCK)

    def each_block(act):
        for n, skip, a, b in ((own_n, 0, x_own, g_own), (other_n, own_n, x_other, g_other)):

            @pl.loop(0, n)
            def _(i):
                for outer, inner in ((a, x), (b, g)):
                    act(
                        pltpu.make_async_copy(
                            outer.at[block_rows(i)], inner.at[block_rows(skip + i)], x_sem
                        )
                    )

    each_block(lambda one: one.start())

    copies = []
    if loaded == 2:
        copies = [(weights[0], win), (weights[1], wout)]
    else:
        part_rows = chunk // moves.nf
        for stream in range(2):
            offsets = moves.relative(stream)
            half = len(offsets) // 2
            for number, offset in enumerate(offsets):
                piece = weights[stream * 2 + number // half].at[number % half]
                owner = flat ^ offset
                for k in range(moves.nz):
                    if stream == 0:
                        for part in range(2):
                            start = ((k * 2 + part) * moves.nf + owner) * deep
                            rows = pl.ds(pl.multiple_of(start, deep), deep)
                            copies.append((piece.at[k, part], win.at[rows]))
                    else:
                        start = (k * moves.nf + owner) * part_rows
                        rows = pl.ds(pl.multiple_of(start, part_rows), part_rows)
                        copies.append((piece.at[k], wout.at[rows]))
    begun = [
        pltpu.make_async_copy(source, target, w_sems.at[n])
        for n, (source, target) in enumerate(copies)
    ]
    for one in begun:
        one.start()
    empty[...] = jnp.zeros_like(empty)
    branch[...] = jnp.zeros_like(branch)
    back[...] = jnp.zeros_like(back)
    each_block(lambda one: one.wait())

    @pl.when(lax.rem(blocks, 2) == 1)
    def _():
        x[block_rows(blocks), :] = jnp.zeros((BLOCK, width), BF16)
        g[block_rows(blocks), :] = jnp.zeros((BLOCK, width), BF16)

    @pl.loop(0, tiles)
    def _(t):
        rows = pl.ds(pl.multiple_of(t * TILE, TILE), TILE)
        x_turned[:, rows] = x[rows, :].T

    for one in begun:
        one.wait()

    def grad_copies(j):
        columns = pl.ds(pl.multiple_of(j * chunk, chunk), chunk)
        if moves is None:
            made = [(low_in, grads[0].at[:, columns]), (low_out, grads[1].at[columns])]
        else:
            made = []
            k_of = zed ^ j
            half_deep = chunk // moves.nf // 2
            for stream in range(2):
                offsets = moves.relative(stream)
                half = len(offsets) // 2
                for number, offset in enumerate(offsets):
                    target = grads[stream * 2 + number // half].at[number % half]
                    owner = flat ^ offset
                    for part in range(2):
                        if stream == 0:
                            for k in range(moves.nz):
                                start = (((zed ^ k) * 2 + part) * moves.nf + owner) * deep
                                rows = pl.ds(pl.multiple_of(start, deep), deep)
                                place_of = target.at[k, pl.ds(part * deep, deep), columns]
                                made.append((low_in.at[rows], place_of))
                        else:
                            start = (owner * 2 + part) * half_deep
                            rows = pl.ds(pl.multiple_of(start, half_deep), half_deep)
                            place_of = target.at[k_of, :, pl.ds(part * width, width)]
                            made.append((low_out.at[rows], place_of))
        return [
            pltpu.make_async_copy(source, target, out_sems.at[n])
            for n, (source, target) in enumerate(made)
        ]

    @pl.loop(0, chunks)
    def _(j):
        columns = pl.ds(pl.multiple_of(j * chunk, chunk), chunk)
        sum_in[...] = jnp.zeros_like(sum_in)
        sum_out[...] = jnp.zeros_like(sum_out)

        @pl.loop(0, tiles)
        def _(t):
            rows = pl.ds(pl.multiple_of(t * TILE, TILE), TILE)
            g_tile = g[rows, :]
            inner = dot(x[rows, :], win[:, columns])
            grad_active = dot_nt(g_tile, wout[columns, :])
            active, slope = gelu_both(inner)
            active_low = active.astype(BF16)
            grad_inner = (grad_active * slope).astype(BF16)
            branch[rows, :] += dot(active_low, wout[columns, :])
            back[rows, :] += dot_nt(grad_inner, win[:, columns])
            sum_in[...] += dot(x_turned[:, rows], grad_inner)
            sum_out[...] += dot_tn(active_low, g_tile)

        @pl.when(j > 0)
        def _():
            for one in grad_copies(j - 1):
                one.wait()

        low_in[...] = sum_in[...].astype(BF16)
        low_out[...] = sum_out[...].astype(BF16)
        for one in grad_copies(j):
            one.start()

    @pl.loop(0, tiles)
    def _(t):
        rows = pl.ds(pl.multiple_of(t * TILE, TILE), TILE)
        x[rows, :] = branch[rows, :].astype(BF16)
        g[rows, :] = back[rows, :].astype(BF16)

    def each_result(act):
        for n, skip, a, b in (
            (own_n, 0, rows_out[0], rows_out[1]),
            (other_n, own_n, rows_out[2], rows_out[3]),
        ):

            @pl.loop(0, n)
            def _(i):
                for outer, inner in ((a, x), (b, g)):
                    act(
                        pltpu.make_async_copy(
                            inner.at[block_rows(skip + i)], outer.at[block_rows(i)], row_sem
                        )
                    )

            @pl.loop(n, most)
            def _(i):
                for outer in (a, b):
                    act(pltpu.make_async_copy(empty, outer.at[block_rows(i)], row_sem))

    each_result(lambda one: one.start())
    each_result(lambda one: one.wait())
    for one in grad_copies(chunks - 1):
        one.wait()


def expert_block(moves, expert, place, sorted_rows, weights, deep, half_hidden):
    capacity, width = sorted_rows[0].shape[1:]
    most = 2 * capacity
    if moves is not None:
        chunks = moves.nz
        copies = 4 * moves.nz * moves.nf
    else:
        chunks = 4
        copies = 2
    chunk = half_hidden // chunks
    anywhere = pl.BlockSpec(memory_space=pl.ANY)
    row_shape = jax.ShapeDtypeStruct((2, capacity, width), BF16)
    if moves is not None:
        block = (moves.nf // 2, moves.nz, 2 * deep, half_hidden)
        grads = [jax.ShapeDtypeStruct(block, BF16)] * 4
    else:
        grads = [jax.ShapeDtypeStruct(w.shape, BF16) for w in weights]
    return pl.pallas_call(
        functools.partial(expert_kernel, (moves, deep, chunk, chunks, expert, len(weights))),
        in_specs=[pl.BlockSpec(memory_space=pltpu.SMEM)] + [anywhere] * (4 + len(weights)),
        out_specs=[anywhere] * (2 + len(grads)),
        out_shape=[row_shape] * 2 + grads,
        scratch_shapes=[
            pltpu.VMEM((width, half_hidden), BF16),
            pltpu.VMEM((half_hidden, width), BF16),
            pltpu.VMEM((most, width), BF16),
            pltpu.VMEM((width, most), BF16),
            pltpu.VMEM((most, width), BF16),
            pltpu.VMEM((most, width), F32),
            pltpu.VMEM((most, width), F32),
            pltpu.VMEM((width, chunk), F32),
            pltpu.VMEM((chunk, width), F32),
            pltpu.VMEM((width, chunk), BF16),
            pltpu.VMEM((chunk, width), BF16),
            pltpu.VMEM((BLOCK, width), BF16),
            pltpu.SemaphoreType.DMA((copies,)),
            pltpu.SemaphoreType.DMA,
            pltpu.SemaphoreType.DMA((copies,)),
            pltpu.SemaphoreType.DMA,
        ],
        compiler_params=pltpu.CompilerParams(vmem_limit_bytes=56 * MIB),
        cost_estimate=pl.CostEstimate(
            flops=12 * 1024 * width * half_hidden,
            bytes_accessed=8 * width * half_hidden + 32 * 1024 * width,
            transcendentals=1024 * half_hidden,
        ),
        name="expert_block",
    )(place, *sorted_rows, *weights)


def gather_experts_whole(w_expert_in, w_expert_out, core, nz):
    width, hidden = w_expert_out.shape[2], w_expert_in.shape[2]
    all_in = lax.all_gather(w_expert_in, AXES, axis=1, tiled=True)
    all_out = lax.all_gather(w_expert_out, AXES, axis=1, tiled=True)
    all_in = all_in.reshape(EXPERTS, width, nz, 2, hidden // (2 * nz))
    all_in = lax.dynamic_index_in_dim(all_in, core, 3, False)
    all_in = all_in.reshape(EXPERTS, width, hidden // 2)
    all_out = all_out.reshape(EXPERTS, nz, 2, hidden // (2 * nz), width)
    all_out = lax.dynamic_index_in_dim(all_out, core, 2, False)
    all_out = all_out.reshape(EXPERTS, hidden // 2, width)
    return [[all_in[e], all_out[e]] for e in range(EXPERTS)]


def reduce_expert(moves, pieces):
    sum_in = moves.reduce_flat(pieces[0], pieces[1], 0)
    sum_out = moves.reduce_flat(pieces[2], pieces[3], 1)
    sums = moves.reduce_z_pair(jnp.stack([sum_in, sum_out], axis=1))
    wide = sums.shape[2] // 2
    return sums[0], jnp.concatenate([sums[1, :, :wide], sums[1, :, wide:]], axis=0)


def join_cores(moves, shares_in, core, deep):
    both = jnp.stack(shares_in)
    both = both.reshape(EXPERTS, 2, deep, both.shape[2])
    ours = lax.dynamic_index_in_dim(both, core, 1, False)
    theirs = moves.core(lax.dynamic_index_in_dim(both, 1 - core, 1, False))
    low_core = jnp.where(core == 0, ours, theirs).reshape(EXPERTS, deep, moves.nz, 1, -1)
    high_core = jnp.where(core == 0, theirs, ours).reshape(EXPERTS, deep, moves.nz, 1, -1)
    return jnp.concatenate([low_core, high_core], axis=3).reshape(EXPERTS, deep, -1)


def reduce_vectors(moves, vectors, place, deep):
    zed, core, flat = place
    held = vectors.reshape(4, moves.nz, 2, moves.nf, deep)
    held = lax.dynamic_index_in_dim(held, core, 2, False) + moves.core(
        lax.dynamic_index_in_dim(held, 1 - core, 2, False)
    )
    held = jnp.moveaxis(held, 2, 0)
    bit = moves.nf // 2
    while bit:
        pair = held.reshape((2, bit) + held.shape[1:])
        side = lax.rem(flat // bit, 2)
        held = lax.dynamic_index_in_dim(pair, side, 0, False) + moves.flat(
            lax.dynamic_index_in_dim(pair, 1 - side, 0, False), bit
        )
        bit //= 2
    held = held[0]
    total = lax.dynamic_index_in_dim(held, zed, 1, False)
    for k in range(1, moves.nz):
        other = lax.dynamic_index_in_dim(held, lax.rem(zed + k, moves.nz), 1, False)
        total = total + moves.along(other, k)
    return total


def local(
    nd,
    nf,
    tokens,
    seq_lengths,
    expert_ids,
    grad_out,
    ln1_gain,
    ln1_bias,
    w_qkv,
    w_attn_out,
    ln2_gain,
    ln2_bias,
    w_expert_in,
    w_expert_out,
):
    rows, width = tokens.shape
    deep = w_qkv.shape[0]
    hidden = w_expert_in.shape[2]
    half_hidden = hidden // 2
    half = width // 2
    moves = Moves(nd, nf)
    nz = moves.nz
    staged = deep % 32 == 0
    core = lax.rem(lax.axis_index("dp"), 2)
    zed = lax.axis_index("dp") // 2
    flat = lax.axis_index("fsdp")
    place = jnp.stack([zed, core, flat]).astype(jnp.int32)

    params = jnp.stack([ln1_gain, ln1_bias, ln2_gain, ln2_bias], axis=1)
    params = jnp.pad(params, ((0, 0), (0, BLOCK - 4)))
    mine = jnp.concatenate([w_qkv, w_attn_out, params], axis=1)
    tokens_wide = tokens.astype(F32)
    positions = jnp.arange(rows, dtype=jnp.int32)
    bounds = jnp.cumsum(seq_lengths[0])
    segment = jnp.sum((positions[:, None] >= bounds[None, :]).astype(jnp.int32), axis=1)
    seg_row = jnp.broadcast_to(segment[None, :], (8, rows))
    seg_col = jnp.broadcast_to(segment[:, None], (rows, BLOCK))
    if staged:
        by_core = w_expert_in.reshape(EXPERTS, deep, nz, 2, hidden // (2 * nz))
        own_in, their_in = [
            lax.dynamic_index_in_dim(by_core, which, 3, False).reshape(EXPERTS, deep, half_hidden)
            for which in (core, 1 - core)
        ]
        outs = forward_pass(moves, tokens, mine, own_in, their_in, w_expert_out, seg_row, seg_col)
        whole_qkv, whole_attn, params, first_in = [
            one.reshape(-1, one.shape[-1]) for one in outs[:4]
        ]
        first_out = outs[4].reshape(half_hidden, width)
        column_in, column_out, normed_one, projected, mixed, stats = outs[5:]
        held = [moves.gather_first(column_in, 0), moves.gather_first(column_out, 1)]
        last = [moves.gather_last(held[0], 0), moves.gather_last(held[1], 1)]
        expert_weights = [[first_in, first_out], [held[0], last[0], held[1], last[1]]]
    else:
        whole = lax.all_gather(mine, AXES, axis=0, tiled=True)
        whole_qkv, whole_attn = whole[:, : 3 * width], whole[:, 3 * width : 4 * width]
        params = whole[:, 4 * width :]
        expert_weights = gather_experts_whole(w_expert_in, w_expert_out, core, nz)
    gain_one, bias_one, gain_two, bias_two = [
        params[:, n].astype(F32)[None, :] for n in range(4)
    ]
    scaled_one, inverse_one = norm_parts(tokens_wide)
    if not staged:
        normed_one = (scaled_one * gain_one + bias_one).astype(BF16)
        projected = dot(normed_one, whole_qkv).astype(BF16)
        mixed, stats = attention_forward(projected, seg_row, seg_col, 0, width // BLOCK)

    routed = expert_ids[:, 0]
    second = (routed == 1).astype(jnp.int32)
    rank_second = jnp.cumsum(second) - second
    second_n = jnp.sum(second)
    rank = jnp.where(routed == 1, rank_second, positions - rank_second)
    capacity = 3 * rows // 4
    slots = jnp.arange(capacity, dtype=jnp.int32)[:, None]
    spread = [
        ((rank[None, :] == slots) & (routed[None, :] == e)).astype(BF16) for e in range(EXPERTS)
    ]
    split = jnp.stack([rows - second_n, second_n]).astype(jnp.int32)
    split = (split + BLOCK - 1) // BLOCK
    spread_all = jnp.concatenate(spread, axis=0)
    grad_sorted = dot(spread_all, grad_out).astype(BF16)
    grad_sorted = after(grad_sorted, projected)
    note = jnp.broadcast_to(split[:, None].astype(BF16), (2, width))
    note = jnp.pad(note, ((0, 14), (0, 0)))
    noted = moves.core(jnp.concatenate([grad_sorted, note], axis=0))
    split_other = noted[2 * capacity : 2 * capacity + 2, 0].astype(jnp.int32)
    grad_sorted = grad_sorted.reshape(EXPERTS, capacity, width)
    grad_sorted_other = noted[: 2 * capacity].reshape(EXPERTS, capacity, width)

    pairs = width // BLOCK
    parts = [(0, pairs // 2), (pairs // 2, pairs // 2)]
    stats_turned = stats.T
    hidden_one = tokens_wide + dot(mixed, whole_attn)
    scaled_two, inverse_two = norm_parts(hidden_one)
    normed_two = (scaled_two * gain_two + bias_two).astype(BF16)

    sorted_rows = dot(spread_all, normed_two).astype(BF16)
    sorted_other = moves.core(sorted_rows).reshape(EXPERTS, capacity, width)
    sorted_rows = sorted_rows.reshape(EXPERTS, capacity, width)
    results, grad_pieces = [], []
    for e in range(EXPERTS):
        table = jnp.stack([zed, flat, split[e], split_other[e]]).astype(jnp.int32)
        outs = expert_block(
            moves if staged else None,
            e,
            table,
            [sorted_rows, sorted_other, grad_sorted, grad_sorted_other],
            list(expert_weights[e]),
            deep,
            half_hidden,
        )
        results.append(add_low(outs[0], moves.core(outs[1])))
        grad_pieces.append(outs[2:])
    both = jnp.concatenate(results, axis=1)
    grad_normed_two = dot_tn(spread_all, both[1])
    branch = dot_tn(spread_all, both[0])
    block_result = (hidden_one + branch).astype(BF16)

    grad_gain_two = jnp.sum(grad_normed_two * scaled_two, axis=0)
    grad_bias_two = jnp.sum(grad_normed_two, axis=0)
    grad_hidden = grad_out.astype(F32) + norm_back(
        grad_normed_two, scaled_two, inverse_two, gain_two
    )
    grad_branch = grad_hidden.astype(BF16)
    grad_mixed = dot_nt(grad_branch, whole_attn).astype(BF16)

    grad_parts, shares = [], []
    for n, (first, count) in enumerate(parts):
        trio = attention_backward(
            projected, grad_mixed, stats_turned, seg_row, seg_col, first, count
        )
        grad_parts.append(trio)
        if staged:
            near, far = attention_grads(
                moves,
                n,
                place,
                normed_one,
                mixed,
                *trio,
                grad_branch[:, first * BLOCK : (first + count) * BLOCK],
                deep,
            )
            pieces = add_low(near, moves.core(far))
            shares.append(moves.reduce_flat(pieces[: nf // 2], pieces[nf // 2 :], n))
    grad_projected = jnp.concatenate(
        [grad_parts[n][m] for m in range(3) for n in range(2)], axis=1
    )
    grad_normed_one = dot_nt(grad_projected, whole_qkv)
    grad_gain_one = jnp.sum(grad_normed_one * scaled_one, axis=0)
    grad_bias_one = jnp.sum(grad_normed_one, axis=0)
    grad_input = grad_hidden + norm_back(grad_normed_one, scaled_one, inverse_one, gain_one)
    vectors = jnp.stack([grad_gain_one, grad_bias_one, grad_gain_two, grad_bias_two])

    if staged:
        sums = [reduce_expert(moves, pieces) for pieces in grad_pieces]
        share_in = join_cores(moves, [one[0] for one in sums], core, deep)
        share_out = jnp.stack([one[1] for one in sums])
        vectors = reduce_vectors(moves, vectors, (zed, core, flat), deep)
        share = moves.reduce_z(jnp.stack(shares, axis=1)).reshape(2, deep, 4, half)
        share = jnp.moveaxis(share, 0, 2).reshape(deep, 4 * width)
        share_qkv, share_attn = share[:, : 3 * width], share[:, 3 * width :]
    else:
        share_qkv = lax.psum_scatter(
            dot_tn(normed_one, grad_projected), AXES, scatter_dimension=0, tiled=True
        )
        share_attn = lax.psum_scatter(
            dot_tn(mixed, grad_branch), AXES, scatter_dimension=0, tiled=True
        )
        vectors = lax.psum_scatter(vectors, AXES, scatter_dimension=1, tiled=True)
        full_in = jnp.stack([pieces[0] for pieces in grad_pieces])
        full_out = jnp.stack([pieces[1] for pieces in grad_pieces])
        full_in = full_in.reshape(EXPERTS, width, nz, 1, -1).astype(F32)
        full_out = full_out.reshape(EXPERTS, nz, 1, -1, width).astype(F32)
        chosen = jnp.arange(2) == core
        full_in = jnp.where(chosen[None, None, None, :, None], full_in, 0.0)
        full_out = jnp.where(chosen[None, None, :, None, None], full_out, 0.0)
        share_in = lax.psum_scatter(
            full_in.reshape(EXPERTS, width, hidden), AXES, scatter_dimension=1, tiled=True
        )
        share_out = lax.psum_scatter(
            full_out.reshape(EXPERTS, hidden, width), AXES, scatter_dimension=1, tiled=True
        )
    return (
        block_result,
        grad_input,
        vectors[0],
        vectors[1],
        share_qkv,
        share_attn,
        vectors[2],
        vectors[3],
        share_in,
        share_out,
    )


def solution(mesh):
    rows = P(AXES, None)
    vector = P(AXES)
    expert = P(None, AXES, None)
    return jax.shard_map(
        functools.partial(local, mesh.shape["dp"], mesh.shape["fsdp"]),
        mesh=mesh,
        in_specs=(
            rows, rows, rows, rows, vector, vector, rows, rows, vector, vector, expert, expert
        ),
        out_specs=(
            rows, rows, vector, vector, rows, rows, vector, vector, expert, expert
        ),
        check_vma=False,
    )
```

```python
import functools

import jax
import jax.numpy as jnp
from jax import lax
from jax.experimental import pallas as pl
from jax.experimental.pallas import tpu as pltpu
from jax.sharding import PartitionSpec as P

HEADS = 16
HEAD_DIM = 64
EXPERTS = 2
EPSILON = 1e-05
MASKED = -1000000000.0
AXES = ("dp", "fsdp")
BLOCK = 128
TILE = 256
MIB = 1024 * 1024
F32 = jnp.float32
BF16 = jnp.bfloat16
NT = (((1,), (1,)), ((), ()))
TN = (((0,), (0,)), ((), ()))
ROOT_2_PI = 0.7978845608028654
CUBIC = 0.044715


def dot(a, b):
    return jnp.dot(a, b, preferred_element_type=F32)


def dot_nt(a, b):
    return lax.dot_general(a, b, NT, preferred_element_type=F32)


def dot_tn(a, b):
    return lax.dot_general(a, b, TN, preferred_element_type=F32)


def norm_parts(values):
    average = jnp.mean(values, axis=-1, keepdims=True)
    centred = values - average
    variance = jnp.mean(centred * centred, axis=-1, keepdims=True)
    inverse = lax.rsqrt(variance + EPSILON)
    return (centred * inverse, inverse)


def norm_back(grad_normed, scaled, inverse, gain):
    grad_scaled = grad_normed * gain
    middle = jnp.mean(grad_scaled, axis=-1, keepdims=True)
    along = jnp.mean(grad_scaled * scaled, axis=-1, keepdims=True)
    return inverse * (grad_scaled - middle - scaled * along)


class Moves:
    def __init__(self, nd, nf):
        self.nz, self.nf = nd // 2, nf
        bits = []
        bit = 1
        while bit < nf:
            bits.append(bit)
            bit *= 2
        self.orders = (tuple(bits), tuple(reversed(bits)))

    def send(self, value, where):
        pairs = []
        for zed in range(self.nz):
            for core in range(2):
                for flat in range(self.nf):
                    z_to, core_to, f_to = where(zed, core, flat)
                    pairs.append(
                        (
                            (zed * 2 + core) * self.nf + flat,
                            (z_to * 2 + core_to) * self.nf + f_to,
                        )
                    )
        return lax.ppermute(value, AXES, pairs)

    def core(self, value):
        return self.send(value, lambda z, c, f: (z, 1 - c, f))

    def flat(self, value, bit):
        return self.send(value, lambda z, c, f: (z, c, f ^ bit))

    def along(self, value, steps):
        return self.send(value, lambda z, c, f: ((z + steps) % self.nz, c, f))

    def near(self, value, bit):
        return self.send(value, lambda z, c, f: (z ^ bit, c, f))

    def relative(self, stream):
        offsets = [0]
        for bit in reversed(self.orders[stream]):
            offsets = offsets + [one ^ bit for one in offsets]
        return tuple(offsets)

    def gather_z(self, value):
        return [value] + [self.along(value, k) for k in range(1, self.nz)]

    def gather_z_pair(self, value):
        held, bit = value[:, None], 1
        while 2 * bit < self.nz:
            held = jnp.concatenate([held, self.near(held, bit)], axis=1)
            bit *= 2
        got = self.near(held, bit)
        return [jnp.concatenate([held[n], got[n]], axis=0) for n in range(2)], got

    def gather_first(self, value, stream):
        held = value[None]
        for bit in tuple(reversed(self.orders[stream]))[:-1]:
            held = jnp.concatenate([held, self.flat(held, bit)], axis=0)
        return held

    def gather_last(self, held, stream):
        return self.flat(held, self.orders[stream][0])

    def reduce_flat(self, keep, sent, stream):
        order = self.orders[stream]
        now = add_low(keep, self.flat(sent, order[0]))
        for bit in order[1:]:
            half = now.shape[0] // 2
            now = add_low(now[:half], self.flat(now[half:], bit))
        return now[0]

    def reduce_z(self, value):
        total = value[0].astype(F32)
        for k in range(1, self.nz):
            total = total + self.along(value[k], k).astype(F32)
        return total

    def reduce_z_pair(self, value):
        bit = self.nz // 2
        while bit > 1:
            value = add_low(value[:bit], self.near(value[bit:], bit))
            bit //= 2
        return value[0].astype(F32) + self.near(value[1], 1).astype(F32)


def after(value, *others):
    return lax.optimization_barrier((value,) + others)[0]


def add_low(a, b):
    return (a.astype(F32) + b.astype(F32)).astype(BF16)


def attention_forward_kernel(seg_row, seg_col, q, k, v, out, stats, bias):
    rows = q.shape[0]
    pair = pl.program_id(0)
    lane = lax.broadcasted_iota(jnp.int32, (1, BLOCK), 1)

    @pl.when(pair == 0)
    def _():
        stats[...] = jnp.zeros_like(stats)
        for i in range(rows // TILE):
            span = (i + 1) * TILE
            place = slice(i * TILE, span)
            query = lax.broadcasted_iota(jnp.int32, (TILE, span), 0) + i * TILE
            key = lax.broadcasted_iota(jnp.int32, (TILE, span), 1)
            same = seg_col[place, 0:1] == seg_row[0:1, :span]
            bias[place, :span] = jnp.where(same & (key <= query), 0.0, MASKED)

    for i in range(rows // TILE):
        span = (i + 1) * TILE
        place = slice(i * TILE, span)
        query = q[place, :] * jnp.asarray(HEAD_DIM**-0.5, BF16)
        mixed = jnp.zeros((TILE, BLOCK), F32)
        held = stats[place, :]
        for side in range(2):
            mine = (lane // HEAD_DIM) == side
            part = jnp.where(mine, query, jnp.zeros_like(query))
            scores = dot_nt(part, k[:span, :]) + bias[place, :span]
            highest = jnp.max(scores, axis=1, keepdims=True)
            terms = jnp.exp(scores - highest)
            total = jnp.sum(terms, axis=1, keepdims=True)
            attend = (terms * (1.0 / total)).astype(BF16)
            mixed = jnp.where(mine, dot(attend, v[:span, :]), mixed)
            held = jnp.where(lane == 2 * pair + side, highest + jnp.log(total), held)
        stats[place, :] = held
        out[place, :] = mixed.astype(BF16)


def attention_forward(projected, seg_row, seg_col, first, count):
    rows, width = projected.shape[0], projected.shape[1] // 3
    pairs = width // BLOCK
    column = lambda start: pl.BlockSpec((rows, BLOCK), lambda h: (0, start + h))
    whole = lambda shape: pl.BlockSpec(shape, lambda h: (0, 0))
    return pl.pallas_call(
        attention_forward_kernel,
        grid=(count,),
        in_specs=[
            whole((8, rows)),
            whole((rows, BLOCK)),
            column(first),
            column(first + pairs),
            column(first + 2 * pairs),
        ],
        out_specs=[column(0), whole((rows, BLOCK))],
        out_shape=[
            jax.ShapeDtypeStruct((rows, count * BLOCK), BF16),
            jax.ShapeDtypeStruct((rows, BLOCK), F32),
        ],
        scratch_shapes=[pltpu.VMEM((rows, rows), F32)],
        compiler_params=pltpu.CompilerParams(vmem_limit_bytes=40 * MIB),
        cost_estimate=pl.CostEstimate(
            flops=4 * rows * rows * count * BLOCK,
            bytes_accessed=8 * rows * count * BLOCK,
            transcendentals=2 * count * rows * rows,
        ),
        name="attention_forward",
    )(seg_row, seg_col, projected, projected, projected)


def attention_backward_kernel(first, seg_row, seg_col, stats, q, k, v, g, dq, dk, dv, bias, dks, dvs):
    rows = q.shape[0]
    pair = pl.program_id(0)
    lane = lax.broadcasted_iota(jnp.int32, (1, BLOCK), 1)
    row = lax.broadcasted_iota(jnp.int32, (BLOCK, 1), 0)

    @pl.when(pair == 0)
    def _():
        for i in range(rows // TILE):
            span = (i + 1) * TILE
            place = slice(i * TILE, span)
            query = lax.broadcasted_iota(jnp.int32, (span, TILE), 1) + i * TILE
            key = lax.broadcasted_iota(jnp.int32, (span, TILE), 0)
            same = seg_col[:span, 0:1] == seg_row[0:1, place]
            bias[:span, place] = jnp.where(same & (key <= query), 0.0, MASKED)

    dks[...] = jnp.zeros_like(dks)
    dvs[...] = jnp.zeros_like(dvs)
    k_turned = k[...].T
    for i in range(rows // TILE):
        span = (i + 1) * TILE
        place = slice(i * TILE, span)
        query = q[place, :] * jnp.asarray(HEAD_DIM**-0.5, BF16)
        grad = g[place, :]
        turned = jnp.zeros((BLOCK, TILE), F32)
        for side in range(2):
            mine = (lane // HEAD_DIM) == side
            part = jnp.where(mine, query, jnp.zeros_like(query))
            grad_part = jnp.where(mine, grad, jnp.zeros_like(grad))
            level = stats[pl.ds(2 * (first + pair) + side, 1), place]
            scores = dot_nt(k[:span, :], part) + bias[:span, place]
            attend = jnp.exp(scores - level)
            grad_attend = dot_nt(v[:span, :], grad_part)
            inner = jnp.sum(attend * grad_attend, axis=0, keepdims=True)
            grad_scores = (attend * (grad_attend - inner)).astype(BF16)
            dks[:span, :] += dot(grad_scores, part)
            dvs[:span, :] += dot(attend.astype(BF16), grad_part)
            turned = jnp.where(
                (row // HEAD_DIM) == side, dot(k_turned[:, :span], grad_scores), turned
            )
        dq[place, :] = (turned.T * HEAD_DIM**-0.5).astype(BF16)
    dk[...] = dks[...].astype(BF16)
    dv[...] = dvs[...].astype(BF16)


def attention_backward(projected, grad_mixed, stats, seg_row, seg_col, first, count):
    rows, width = projected.shape[0], projected.shape[1] // 3
    pairs = width // BLOCK
    column = lambda start: pl.BlockSpec((rows, BLOCK), lambda h: (0, start + h))
    whole = lambda shape: pl.BlockSpec(shape, lambda h: (0, 0))
    share = jax.ShapeDtypeStruct((rows, count * BLOCK), BF16)
    return pl.pallas_call(
        functools.partial(attention_backward_kernel, first),
        grid=(count,),
        in_specs=[
            whole((8, rows)),
            whole((rows, BLOCK)),
            whole((BLOCK, rows)),
            column(first),
            column(first + pairs),
            column(first + 2 * pairs),
            column(first),
        ],
        out_specs=[column(0), column(0), column(0)],
        out_shape=[share, share, share],
        scratch_shapes=[
            pltpu.VMEM((rows, rows), F32),
            pltpu.VMEM((rows, BLOCK), F32),
            pltpu.VMEM((rows, BLOCK), F32),
        ],
        compiler_params=pltpu.CompilerParams(vmem_limit_bytes=40 * MIB),
        cost_estimate=pl.CostEstimate(
            flops=10 * rows * rows * count * BLOCK,
            bytes_accessed=14 * rows * count * BLOCK,
            transcendentals=2 * count * rows * rows,
        ),
        name="attention_backward",
    )(seg_row, seg_col, stats, projected, projected, projected, grad_mixed)


class Copies:
    def __init__(self, send_sems, recv_sems):
        self.send_sems, self.recv_sems, self.made = send_sems, recv_sems, []

    def start(self, source, target, device):
        n = len(self.made)
        one = pltpu.make_async_remote_copy(
            src_ref=source,
            dst_ref=target,
            send_sem=self.send_sems.at[n],
            recv_sem=self.recv_sems.at[n],
            device_id=device,
            device_id_type=pl.DeviceIdType.MESH,
        )
        one.start()
        self.made.append(one)
        return one


def wait_in(copies):
    for one in copies:
        one.wait_recv()


def forward_kernel(
    moves,
    tokens,
    mine,
    own_in,
    own_out,
    seg_row,
    seg_col,
    slot_row,
    grad_out,
    note,
    out_qkv,
    out_attn,
    out_params,
    first_in,
    first_out,
    held_in,
    held_out,
    sorted_other,
    grad_other,
    noted,
    normed,
    projected,
    mixed,
    stats,
    hidden,
    sorted_rows,
    grad_sorted,
    weights,
    bias,
    normed_two,
    send_sems,
    recv_sems,
    local_sems,
):
    nz, nf = moves.nz, moves.nf
    dp, flat = lax.axis_index("dp"), lax.axis_index("fsdp")
    zed, core = dp // 2, lax.rem(dp, 2)
    rows, wide = tokens.shape
    sibling = (zed * 2 + 1 - core, flat)
    others = [(lax.rem(zed + k, nz) * 2 + core, flat) for k in range(1, nz)]
    hops = {bit: (dp, flat ^ bit) for bit in moves.orders[0]}

    barrier = pltpu.get_barrier_semaphore()
    for device in [sibling] + others + list(hops.values()):
        pl.semaphore_signal(barrier, inc=1, device_id=device, device_id_type=pl.DeviceIdType.MESH)
    pl.semaphore_wait(barrier, 1 + len(others) + len(hops))

    remote = Copies(send_sems, recv_sems)
    local = []

    def local_start(source, target):
        one = pltpu.make_async_copy(source, target, local_sems.at[len(local)])
        one.start()
        local.append(one)
        return one

    own = local_start(mine, weights.at[zed, core, flat])
    column = [remote.start(mine, weights.at[zed, core, flat], device) for device in others]
    column_in, column_out = held_in.at[0], held_out.at[0]
    targets = (first_in.at[zed, core, flat], column_in.at[zed, core])
    cut = own_in.shape[2] // (2 * nz)
    crossed, blocks = [remote.start(note, noted, sibling)], []
    for e in range(EXPERTS):
        for z_of in range(nz):
            target = targets[e].at[:, pl.ds(z_of * cut, cut)]
            theirs, ours = [
                own_in.at[e, :, pl.ds(pl.multiple_of((2 * z_of + which) * cut, cut), cut)]
                for which in (1 - core, core)
            ]
            crossed.append(remote.start(theirs, target, sibling))
            blocks.append(local_start(ours, target))
    blocks.append(local_start(own_out.at[0], first_out.at[zed, flat]))
    blocks.append(local_start(own_out.at[1], column_out.at[zed]))

    def sort_rows(source, target):
        @pl.loop(0, target.shape[0] // TILE)
        def _(t):
            place = pl.ds(pl.multiple_of(t * TILE, TILE), TILE)
            slot = lax.broadcasted_iota(jnp.int32, (TILE, rows), 0) + t * TILE
            chosen = (slot == slot_row[0:1, :]).astype(F32).astype(BF16)
            target[place, :] = dot(chosen, source[...]).astype(BF16)

    sort_rows(grad_out, grad_sorted)
    for i in range(rows // TILE):
        span = (i + 1) * TILE
        place = slice(i * TILE, span)
        query = lax.broadcasted_iota(jnp.int32, (TILE, span), 0) + i * TILE
        key = lax.broadcasted_iota(jnp.int32, (TILE, span), 1)
        same = seg_col[place, 0:1] == seg_row[0:1, :span]
        bias[place, :span] = jnp.where(same & (key <= query), 0.0, MASKED)
    stats[...] = jnp.zeros_like(stats)

    def stream_columns(stream):
        return slice(0, 2 * wide) if stream == 0 else slice(2 * wide, 4 * wide + BLOCK)

    def send_weights(stream, owner, device):
        place = weights.at[:, core, owner, :, stream_columns(stream)]
        return remote.start(place, place, device)

    own.wait()
    wait_in(column)
    exchanged = [remote.start(grad_sorted, grad_other, sibling)]
    near = [tuple(reversed(moves.orders[n]))[0] for n in range(2)]
    far = [moves.orders[n][0] for n in range(2)]
    hop_near = [send_weights(n, flat, hops[near[n]]) for n in range(2)]
    hop_far = [send_weights(n, flat, hops[far[n]]) for n in range(2)]
    place = weights.at[:, core, flat]
    across = [remote.start(place, place, sibling)]

    wait_in(crossed)
    for one in blocks:
        one.wait()
    first_column = []
    for device in others:
        place = first_in.at[zed, :, flat]
        first_column.append(remote.start(place, place, device))
        first_column.append(remote.start(own_out.at[0], first_out.at[zed, flat], device))

    wait_in(hop_near)
    hop_last = [send_weights(n, flat ^ near[n], hops[far[n]]) for n in range(2)]
    across += [send_weights(n, flat ^ near[n], sibling) for n in range(2)]
    wait_in(hop_far)
    across += [send_weights(n, flat ^ far[n], sibling) for n in range(2)]
    wait_in(hop_last)
    across += [send_weights(n, flat ^ near[n] ^ far[n], sibling) for n in range(2)]

    def send_first(stream, owner, device):
        place = first_in.at[:, :, owner] if stream == 0 else first_out.at[:, owner]
        return remote.start(place, place, device)

    wait_in(first_column)
    first_near = [send_first(n, flat, hops[near[n]]) for n in range(2)]
    first_far = [send_first(n, flat, hops[far[n]]) for n in range(2)]
    second_column = []
    for device in others:
        place = column_in.at[zed]
        second_column.append(remote.start(place, place, device))
        second_column.append(remote.start(own_out.at[1], column_out.at[zed], device))

    wait_in(across)
    whole = 2 * nz * nf * mine.shape[0]
    writes = [
        local_start(weights.at[:, :, :, :, pl.ds(0, 3 * wide)], out_qkv),
        local_start(weights.at[:, :, :, :, pl.ds(3 * wide, wide)], out_attn),
        local_start(weights.at[:, :, :, :, pl.ds(4 * wide, BLOCK)], out_params),
    ]
    turned = weights[:, :, :, :, pl.ds(4 * wide, BLOCK)].reshape(whole, BLOCK).astype(F32).T
    gain, shift = turned[0:1, :], turned[1:2, :]

    @pl.loop(0, rows // TILE)
    def _(t):
        place = pl.ds(pl.multiple_of(t * TILE, TILE), TILE)
        scaled, _ = norm_parts(tokens[place, :].astype(F32))
        normed[place, :] = (scaled * gain + shift).astype(BF16)
        for part in range(3):
            columns = pl.ds(part * wide, wide)
            matrix = weights[:, :, :, :, columns].reshape(whole, wide)
            projected[place, columns] = dot(normed[place, :], matrix).astype(BF16)

    lane = lax.broadcasted_iota(jnp.int32, (1, BLOCK), 1)
    pairs = wide // BLOCK

    def attend_pair(pair):
        columns = [
            pl.ds(pl.multiple_of(n * wide + pair * BLOCK, BLOCK), BLOCK) for n in range(3)
        ]
        for i in range(rows // TILE):
            span = (i + 1) * TILE
            place = slice(i * TILE, span)
            query = projected[place, columns[0]] * jnp.asarray(HEAD_DIM**-0.5, BF16)
            result = jnp.zeros((TILE, BLOCK), F32)
            held = stats[place, :]
            for side in range(2):
                ours = (lane // HEAD_DIM) == side
                part = jnp.where(ours, query, jnp.zeros_like(query))
                scores = dot_nt(part, projected[:span, columns[1]]) + bias[place, :span]
                highest = jnp.max(scores, axis=1, keepdims=True)
                terms = jnp.exp(scores - highest)
                total = jnp.sum(terms, axis=1, keepdims=True)
                attend = (terms * (1.0 / total)).astype(BF16)
                result = jnp.where(ours, dot(attend, projected[:span, columns[2]]), result)
                held = jnp.where(lane == 2 * pair + side, highest + jnp.log(total), held)
            stats[place, :] = held
            mixed[place, columns[0]] = result.astype(BF16)

    @pl.loop(0, pairs // 4)
    def _(pair):
        attend_pair(pair)

    wait_in(first_near)
    first_last = [send_first(n, flat ^ near[n], hops[far[n]]) for n in range(2)]

    @pl.loop(pairs // 4, pairs)
    def _(pair):
        attend_pair(pair)

    wait_in(second_column)
    second_near = [
        remote.start(held.at[0], held.at[1], hops[near[n]])
        for n, held in enumerate((held_in, held_out))
    ]

    gain_two, shift_two = turned[2:3, :], turned[3:4, :]

    @pl.loop(0, rows // TILE)
    def _(t):
        place = pl.ds(pl.multiple_of(t * TILE, TILE), TILE)
        matrix = weights[:, :, :, :, pl.ds(3 * wide, wide)].reshape(whole, wide)
        total = tokens[place, :].astype(F32) + dot(mixed[place, :], matrix)
        hidden[place, :] = total
        scaled, _ = norm_parts(total)
        normed_two[place, :] = (scaled * gain_two + shift_two).astype(BF16)

    sort_rows(normed_two, sorted_rows)
    exchanged.append(remote.start(sorted_rows, sorted_other, sibling))
    wait_in(first_far)
    wait_in(first_last)
    wait_in(second_near)
    wait_in(exchanged)
    for one in remote.made:
        one.wait_send()
    for one in writes:
        one.wait()


def forward_pass(moves, tokens, mine, own_in, own_out, seg_row, seg_col, slot_row, grad_out, note):
    nz, nf = moves.nz, moves.nf
    rows, wide = tokens.shape
    deep, half = own_in.shape[1], own_in.shape[2] // 2
    part = own_out.shape[1]
    capacity = 3 * rows // 4
    anywhere = pl.BlockSpec(memory_space=pl.ANY)
    inside = pl.BlockSpec(memory_space=pltpu.VMEM)
    shape = jax.ShapeDtypeStruct
    remote = 7 * (nz - 1) + 2 * nz + 24
    return pl.pallas_call(
        functools.partial(forward_kernel, moves),
        in_specs=[inside] * 9,
        out_specs=[anywhere] * 10 + [inside] * 7,
        out_shape=[
            shape((nz, 2, nf, deep, 3 * wide), BF16),
            shape((nz, 2, nf, deep, wide), BF16),
            shape((nz, 2, nf, deep, BLOCK), BF16),
            shape((nz, 2, nf, deep, half), BF16),
            shape((nz, nf, part, wide), BF16),
            shape((2, nz, 2, deep, half), BF16),
            shape((2, nz, part, wide), BF16),
            shape((EXPERTS * capacity, wide), BF16),
            shape((EXPERTS * capacity, wide), BF16),
            shape(note.shape, BF16),
            shape((rows, wide), BF16),
            shape((rows, 3 * wide), BF16),
            shape((rows, wide), BF16),
            shape((rows, BLOCK), F32),
            shape((rows, wide), F32),
            shape((EXPERTS * capacity, wide), BF16),
            shape((EXPERTS * capacity, wide), BF16),
        ],
        scratch_shapes=[
            pltpu.VMEM((nz, 2, nf, deep, 4 * wide + BLOCK), BF16),
            pltpu.VMEM((rows, rows), F32),
            pltpu.VMEM((rows, wide), BF16),
            pltpu.SemaphoreType.DMA((remote,)),
            pltpu.SemaphoreType.DMA((remote,)),
            pltpu.SemaphoreType.DMA((2 * nz + 6,)),
        ],
        compiler_params=pltpu.CompilerParams(
            collective_id=0, has_side_effects=True, vmem_limit_bytes=60 * MIB
        ),
        cost_estimate=pl.CostEstimate(
            flops=10 * rows * wide * wide, bytes_accessed=80 * wide * wide, transcendentals=0
        ),
        name="forward_pass",
    )(tokens, mine, own_in, own_out, seg_row, seg_col, slot_row, grad_out, note)


def sum_low(*values):
    total = values[0].astype(F32)
    for one in values[1:]:
        total = total + one.astype(F32)
    return total


def backward_kernel(
    moves,
    deep,
    projected,
    whole_qkv,
    whole_attn,
    hidden,
    normed_out,
    tokens_in,
    grad_out,
    rows_first,
    rows_second,
    other_first,
    other_second,
    keep_first_in,
    keep_first_out,
    arrived_in,
    arrived_out,
    keep_in,
    sent_in,
    keep_out,
    sent_out,
    stats,
    seg_row,
    seg_col,
    slot_col,
    mixed,
    params,
    block_out,
    grad_tokens,
    share_in,
    share_out,
    share_qkv,
    share_attn,
    share_vectors,
    got_in,
    got_out,
    hop_in,
    hop_out,
    first_hop_in,
    first_hop_out,
    landed,
    wide_low,
    wide_f32,
    grad_projected,
    grad_mixed,
    branch,
    normed,
    tokens,
    key_sums,
    value_sums,
    low,
    cross,
    got_q,
    hop_q,
    z_q,
    up_q,
    vec,
    cross_vec,
    got_vec,
    hop_vec,
    z_vec,
    up,
    spare,
    up_first,
    z_first,
    z_second,
    final,
    send_sems,
    recv_sems,
    local_sems,
):
    nz, nf = moves.nz, moves.nf
    dp, flat = lax.axis_index("dp"), lax.axis_index("fsdp")
    zed, core = dp // 2, lax.rem(dp, 2)
    rows, wide = tokens.shape
    half = wide // 2
    sibling = (zed * 2 + 1 - core, flat)
    others = [((zed ^ k) * 2 + core, flat) for k in range(1, nz)]
    hops = {bit: (dp, flat ^ bit) for bit in moves.orders[0]}

    barrier = pltpu.get_barrier_semaphore()
    for device in [sibling] + others + list(hops.values()):
        pl.semaphore_signal(barrier, inc=1, device_id=device, device_id_type=pl.DeviceIdType.MESH)
    pl.semaphore_wait(barrier, 1 + len(others) + len(hops))

    remote = Copies(send_sems, recv_sems)
    local = []

    def local_start(source, target):
        one = pltpu.make_async_copy(source, target, local_sems.at[len(local)])
        one.start()
        local.append(one)
        return one

    def load(*pairs):
        for one in [local_start(source, target) for source, target in pairs]:
            one.wait()

    capacity = rows_first.shape[1]
    crossed_rows = [
        remote.start(other_first.at[1], grad_projected.at[pl.ds(0, capacity), pl.ds(2 * wide, wide)], sibling),
        remote.start(other_second.at[1], grad_mixed.at[pl.ds(0, capacity)], sibling),
    ]
    crossed_late = [
        remote.start(other.at[0], landed.at[e], sibling)
        for e, other in enumerate((other_first, other_second))
    ]
    row_loads = [
        local_start(source.at[1], grad_projected.at[pl.ds(0, capacity), pl.ds(e * wide, wide)])
        for e, source in enumerate((rows_first, rows_second))
    ]
    loaded = local_start(projected, wide_low)
    phase_loads = [
        local_start(hidden, wide_f32),
        local_start(whole_attn, normed),
        local_start(grad_out, tokens),
    ]
    one_way = [moves.orders[n][0] for n in range(2)]
    other_way = [moves.orders[n][1] for n in range(2)]
    keep_first, arrived = (keep_first_in, keep_first_out), (arrived_in, arrived_out)
    first_hop = (first_hop_in, first_hop_out)

    def first_next(n):
        load((keep_first[n].at[1], up_first.at[n]), (arrived[n].at[1], spare.at[0]))

        @pl.loop(0, nz)
        def _(k):
            up_first[n, k] = sum_low(up_first[n, k], spare[0, k]).astype(BF16)

        return remote.start(up_first.at[n], first_hop[n], hops[other_way[n]])

    first_hops = [first_next(n) for n in range(2)]
    keep, sent = (keep_in, keep_out), (sent_in, sent_out)
    got, hop = (got_in, got_out), (hop_in, hop_out)
    second_got = {}
    for index in (1, 0):
        for n in range(2):
            second_got[n, index] = remote.start(
                sent[n].at[index], got[n].at[index], hops[one_way[n]]
            )

    for one in row_loads + phase_loads:
        one.wait()
    wait_in(crossed_rows)

    def add_rows(target, source, columns):
        @pl.loop(0, capacity // TILE)
        def _(t):
            place = pl.ds(pl.multiple_of(t * TILE, TILE), TILE)
            total = sum_low(grad_projected[place, target], source[place, columns])
            grad_projected[place, target] = total.astype(BF16)

    first_columns, second_columns = pl.ds(0, wide), pl.ds(wide, wide)
    add_rows(first_columns, grad_projected, pl.ds(2 * wide, wide))
    add_rows(second_columns, grad_mixed, first_columns)

    def tokens_order(place):
        total = jnp.zeros((TILE, wide), F32)
        for e in range(EXPERTS):
            slot = lax.broadcasted_iota(jnp.int32, (TILE, capacity), 1) + e * capacity
            chosen = (slot == slot_col[place, 0:1]).astype(F32).astype(BF16)
            total = total + dot(chosen, grad_projected[pl.ds(0, capacity), pl.ds(e * wide, wide)])
        return total

    turned = params[...].astype(F32).T
    gain_one, gain_two = turned[0:1, :], turned[2:3, :]
    empty = jnp.zeros((1, wide), F32)

    def second_norm_tile(t, sums):
        place = pl.ds(pl.multiple_of(t * TILE, TILE), TILE)
        grad = tokens_order(place)
        scaled, inverse = norm_parts(wide_f32[place, :])
        total = tokens[place, :].astype(F32) + norm_back(grad, scaled, inverse, gain_two)
        wide_f32[place, :] = total
        low_total = total.astype(BF16)
        branch[place, :] = low_total
        grad_mixed[place, :] = dot_nt(low_total, normed[...]).astype(BF16)
        return (
            sums[0] + jnp.sum(grad * scaled, axis=0, keepdims=True),
            sums[1] + jnp.sum(grad, axis=0, keepdims=True),
        )

    sums_two = lax.fori_loop(0, rows // TILE, second_norm_tile, (empty, empty))
    load((wide_f32, grad_tokens), (normed_out, normed), (tokens_in, tokens))

    def first_sums(n):
        load(
            (keep_first[n].at[0], up_first.at[n]),
            (arrived[n].at[0], spare.at[0]),
            (first_hop[n], spare.at[1]),
        )

        @pl.loop(0, nz)
        def _(k):
            total = sum_low(up_first[n, k], spare[0, k], spare[1, k])
            up_first[n, k] = total.astype(BF16)

        return [
            remote.start(up_first.at[n, k], z_first.at[n, k - 1], others[k - 1])
            for k in range(1, nz)
        ]

    wait_in(first_hops)
    for one in first_hops:
        one.wait_send()
    first_z = first_sums(0) + first_sums(1)

    lane = lax.broadcasted_iota(jnp.int32, (1, BLOCK), 1)
    row = lax.broadcasted_iota(jnp.int32, (BLOCK, 1), 0)
    for i in range(rows // TILE):
        span = (i + 1) * TILE
        place = slice(i * TILE, span)
        query = lax.broadcasted_iota(jnp.int32, (span, TILE), 1) + i * TILE
        key = lax.broadcasted_iota(jnp.int32, (span, TILE), 0)
        same = seg_col[:span, 0:1] == seg_row[0:1, place]
        wide_f32[:span, place] = jnp.where(same & (key <= query), 0.0, MASKED)
    loaded.wait()
    pairs = wide // BLOCK

    def attend_pair(pair):
        columns = [
            pl.ds(pl.multiple_of(n * wide + pair * BLOCK, BLOCK), BLOCK) for n in range(3)
        ]
        key_sums[...] = jnp.zeros_like(key_sums)
        value_sums[...] = jnp.zeros_like(value_sums)
        keys_turned = wide_low[:, columns[1]].T
        for i in range(rows // TILE):
            span = (i + 1) * TILE
            place = slice(i * TILE, span)
            query = wide_low[place, columns[0]] * jnp.asarray(HEAD_DIM**-0.5, BF16)
            grad = grad_mixed[place, columns[0]]
            turned = jnp.zeros((BLOCK, TILE), F32)
            for side in range(2):
                ours = (lane // HEAD_DIM) == side
                part = jnp.where(ours, query, jnp.zeros_like(query))
                grad_part = jnp.where(ours, grad, jnp.zeros_like(grad))
                level = stats[pl.ds(2 * pair + side, 1), place]
                scores = dot_nt(wide_low[:span, columns[1]], part) + wide_f32[:span, place]
                attend = jnp.exp(scores - level)
                grad_attend = dot_nt(wide_low[:span, columns[2]], grad_part)
                inner = jnp.sum(attend * grad_attend, axis=0, keepdims=True)
                grad_scores = (attend * (grad_attend - inner)).astype(BF16)
                key_sums[:span, :] += dot(grad_scores, part)
                value_sums[:span, :] += dot(attend.astype(BF16), grad_part)
                turned = jnp.where(
                    (row // HEAD_DIM) == side, dot(keys_turned[:, :span], grad_scores), turned
                )
            grad_projected[place, columns[0]] = (turned.T * HEAD_DIM**-0.5).astype(BF16)
        grad_projected[:, columns[1]] = key_sums[...].astype(BF16)
        grad_projected[:, columns[2]] = value_sums[...].astype(BF16)

    def attend_pairs(start, stop):
        @pl.loop(start, stop)
        def _(pair):
            attend_pair(pair)

    def weight_grads(n):
        @pl.loop(0, nz)
        def _(z_of):
            span = 2 * nf * deep
            place = pl.ds(pl.multiple_of(z_of * span, span), span)
            turned = normed[:, place].T
            mixed_turned = mixed[:, place].T
            for part in range(4):
                if part < 3:
                    columns = pl.ds(part * wide + n * half, half)
                    made = dot(turned, grad_projected[:, columns])
                else:
                    made = dot(mixed_turned, branch[:, pl.ds(n * half, half)])
                made = made.astype(BF16).reshape(2, nf, deep, half)
                low[n, z_of, :, :, :, pl.ds(part * half, half)] = made

    def cross_start(source, target):
        return remote.start(source.at[:, 1 - core], target, sibling)

    def cross_add(source, target):
        @pl.loop(0, nz)
        def _(k):
            source[k, core] = sum_low(source[k, core], target[k]).astype(source.dtype)

    def hop_start(source, target, n):
        bits = one_way[n], other_way[n]
        return [
            remote.start(
                source.at[:, core, flat ^ bits[0] ^ (bits[1] * index)],
                target.at[index],
                hops[bits[0]],
            )
            for index in (1, 0)
        ]

    def hop_next(source, arrived, target, landing, n):
        @pl.loop(0, nz)
        def _(k):
            mine = source[k, core, flat ^ other_way[n]]
            target[k] = sum_low(mine, arrived[1, k]).astype(target.dtype)

        return remote.start(target, landing, hops[other_way[n]])

    def z_start(source, arrived, landing, z_landing):
        @pl.loop(0, nz)
        def _(k):
            total = sum_low(source[k, core, flat], arrived[0, k], landing[k])
            source[k, core, flat] = total.astype(source.dtype)

        return [
            remote.start(source.at[zed ^ k, core, flat], z_landing.at[k - 1], others[k - 1])
            for k in range(1, nz)
        ]

    def z_total(source, z_landing):
        return sum_low(source[zed, core, flat], *[z_landing[k] for k in range(nz - 1)])

    def second_next(n):
        load((keep[n].at[1], up.at[n]), (got[n].at[1], spare.at[0]))

        @pl.loop(0, nz)
        def _(k):
            up[n, k] = sum_low(up[n, k], spare[0, k]).astype(BF16)

        return remote.start(up.at[n], hop[n], hops[other_way[n]])

    def second_z(n):
        load((keep[n].at[0], up.at[n]), (got[n].at[0], spare.at[0]), (hop[n], spare.at[1]))

        @pl.loop(0, nz)
        def _(k):
            up[n, k] = sum_low(up[n, k], spare[0, k], spare[1, k]).astype(BF16)

        return [
            remote.start(up.at[n, k], z_second.at[n, k - 1], others[k - 1]) for k in range(1, nz)
        ]

    def finish_expert(e, own, z_landing, writes):
        for n in range(2):
            final[2 * e + n] = sum_low(own[n], *[z_landing[n, k] for k in range(nz - 1)])
        cut = share_in.shape[2] // (2 * nz)
        for z_of in range(nz):
            place = pl.ds(pl.multiple_of((z_of * 2 + core) * cut, cut), cut)
            target = share_in.at[e, :, place]
            source = final.at[2 * e]
            there = source.at[pl.ds(pl.multiple_of((1 - core) * deep, deep), deep)]
            here = source.at[pl.ds(pl.multiple_of(core * deep, deep), deep)]
            writes.append(remote.start(there.at[:, pl.ds(z_of * cut, cut)], target, sibling))
            stored.append(local_start(here.at[:, pl.ds(z_of * cut, cut)], target))
        part = share_out.shape[1] // 2
        for index in range(2):
            stored.append(
                local_start(
                    final.at[2 * e + 1, :, pl.ds(index * wide, wide)],
                    share_out.at[e, pl.ds(index * part, part)],
                )
            )

    def put_share(n, total):
        for part in range(4):
            piece = total[:, part * half : (part + 1) * half]
            if part < 3:
                share_qkv[:, pl.ds(part * wide + n * half, half)] = piece
            else:
                share_attn[:, pl.ds(n * half, half)] = piece

    stored = []
    attend_pairs(0, pairs // 2)
    weight_grads(0)
    crossed = [cross_start(low.at[0], cross.at[0])]
    wait_in([second_got[n, 1] for n in range(2)])
    second_hop = [second_next(n) for n in range(2)]
    attend_pairs(pairs // 2, 3 * pairs // 4)
    wait_in(crossed)
    cross_add(low.at[0], cross.at[0])
    hops_a = hop_start(low.at[0], got_q.at[0], 0)
    attend_pairs(3 * pairs // 4, pairs)
    reload = local_start(whole_qkv, wide_low)
    restore = local_start(grad_tokens, wide_f32)
    weight_grads(1)
    crossed = [cross_start(low.at[1], cross.at[1])]
    wait_in(hops_a)
    next_a = hop_next(low.at[0], got_q.at[0], up_q.at[0], hop_q.at[0], 0)
    wait_in([second_got[n, 0] for n in range(2)] + second_hop)
    for one in second_hop:
        one.wait_send()
    second_zs = second_z(0) + second_z(1)
    wait_in(crossed)
    cross_add(low.at[1], cross.at[1])
    hops_b = hop_start(low.at[1], got_q.at[1], 1)

    reload.wait()
    restore.wait()
    def norm_tile(t, sums):
        place = pl.ds(pl.multiple_of(t * TILE, TILE), TILE)
        grad = dot_nt(grad_projected[place, :], wide_low[...])
        scaled, inverse = norm_parts(tokens[place, :].astype(F32))
        wide_f32[place, :] += norm_back(grad, scaled, inverse, gain_one)
        return (
            sums[0] + jnp.sum(grad * scaled, axis=0, keepdims=True),
            sums[1] + jnp.sum(grad, axis=0, keepdims=True),
        )

    sums = lax.fori_loop(0, rows // TILE, norm_tile, (empty, empty))
    result = local_start(wide_f32, grad_tokens)
    index = lax.broadcasted_iota(jnp.int32, (BLOCK, 1), 0)
    stacked = jnp.zeros((BLOCK, wide), F32)
    for n, one in enumerate(sums + sums_two):
        stacked = jnp.where(index == n, one, stacked)
    vec[...] = stacked.T.reshape(nz, 2, nf, deep, BLOCK)
    crossed = [cross_start(vec, cross_vec)]

    wait_in([next_a])
    z_a = z_start(low.at[0], got_q.at[0], hop_q.at[0], z_q.at[0])
    wait_in(crossed)
    cross_add(vec, cross_vec)
    hops_v = hop_start(vec, got_vec, 0)
    writes = []
    wait_in(first_z)
    finish_expert(0, [up_first[n, 0] for n in range(2)], z_first, writes)
    wait_in(hops_v)
    next_v = hop_next(vec, got_vec, hop_vec.at[1], hop_vec.at[0], 0)
    wait_in(hops_b)
    next_b = hop_next(low.at[1], got_q.at[1], up_q.at[1], hop_q.at[1], 1)
    wait_in([next_v])
    z_v = z_start(vec, got_vec, hop_vec.at[0], z_vec)
    wait_in([next_b])
    z_b = z_start(low.at[1], got_q.at[1], hop_q.at[1], z_q.at[1])

    result.wait()
    wait_in(crossed_late)
    load(
        (hidden, wide_f32),
        *[
            (source.at[0], grad_projected.at[pl.ds(0, capacity), pl.ds(e * wide, wide)])
            for e, source in enumerate((rows_first, rows_second))
        ],
        (landed.at[0], grad_projected.at[pl.ds(0, capacity), pl.ds(2 * wide, wide)]),
        (landed.at[1], grad_mixed.at[pl.ds(0, capacity)]),
    )
    add_rows(first_columns, grad_projected, pl.ds(2 * wide, wide))
    add_rows(second_columns, grad_mixed, first_columns)

    @pl.loop(0, rows // TILE)
    def _(t):
        place = pl.ds(pl.multiple_of(t * TILE, TILE), TILE)
        branch[place, :] = (wide_f32[place, :] + tokens_order(place)).astype(BF16)

    stored.append(local_start(branch, block_out))
    wait_in(z_a)
    put_share(0, z_total(low.at[0], z_q.at[0]))
    wait_in(z_v)
    share_vectors[...] = z_total(vec, z_vec)
    wait_in(second_zs)
    finish_expert(1, [up[n, 0] for n in range(2)], z_second, writes)
    wait_in(z_b)
    put_share(1, z_total(low.at[1], z_q.at[1]))
    wait_in(writes)
    for one in remote.made:
        if not any(one is other for other in second_hop + first_hops):
            one.wait_send()
    for one in stored:
        one.wait()


def backward_pass(moves, deep, big, row_parts, sums, stats, seg, slot_col, mixed, params):
    nz, nf = moves.nz, moves.nf
    rows, wide = mixed.shape
    half = wide // 2
    block = sums[0].shape[2:]
    capacity = row_parts[0].shape[1]
    anywhere = pl.BlockSpec(memory_space=pl.ANY)
    inside = pl.BlockSpec(memory_space=pltpu.VMEM)
    shape = jax.ShapeDtypeStruct
    landing = (2, nz) + block
    remote = 24 + 7 * (nz - 1) + 2 * nz
    inputs = list(big) + list(row_parts) + list(sums)
    return pl.pallas_call(
        functools.partial(backward_kernel, moves, deep),
        in_specs=[anywhere] * len(inputs) + [inside] * 6,
        out_specs=[anywhere] * 4 + [inside] * 3 + [anywhere] * 7,
        out_shape=[
            shape((rows, wide), BF16),
            shape((rows, wide), F32),
            shape((EXPERTS, deep, 2 * block[1]), F32),
            shape((EXPERTS, block[0] * block[1] // wide, wide), F32),
            shape((deep, 3 * wide), F32),
            shape((deep, wide), F32),
            shape((deep, BLOCK), F32),
            shape(landing, BF16),
            shape(landing, BF16),
            shape(landing[1:], BF16),
            shape(landing[1:], BF16),
            shape(landing[1:], BF16),
            shape(landing[1:], BF16),
            shape((EXPERTS, capacity, wide), BF16),
        ],
        scratch_shapes=[
            pltpu.VMEM((rows, 3 * wide), BF16),
            pltpu.VMEM((rows, rows), F32),
            pltpu.VMEM((rows, 3 * wide), BF16),
            pltpu.VMEM((rows, wide), BF16),
            pltpu.VMEM((rows, wide), BF16),
            pltpu.VMEM((rows, wide), BF16),
            pltpu.VMEM((rows, wide), BF16),
            pltpu.VMEM((rows, BLOCK), F32),
            pltpu.VMEM((rows, BLOCK), F32),
            pltpu.VMEM((2, nz, 2, nf, deep, 4 * half), BF16),
            pltpu.VMEM((2, nz, nf, deep, 4 * half), BF16),
            pltpu.VMEM((2, 2, nz, deep, 4 * half), BF16),
            pltpu.VMEM((2, nz, deep, 4 * half), BF16),
            pltpu.VMEM((2, nz - 1, deep, 4 * half), BF16),
            pltpu.VMEM((2, nz, deep, 4 * half), BF16),
            pltpu.VMEM((nz, 2, nf, deep, BLOCK), F32),
            pltpu.VMEM((nz, nf, deep, BLOCK), F32),
            pltpu.VMEM((2, nz, deep, BLOCK), F32),
            pltpu.VMEM((2, nz, deep, BLOCK), F32),
            pltpu.VMEM((nz - 1, deep, BLOCK), F32),
            pltpu.VMEM((2, nz) + block, BF16),
            pltpu.VMEM((2, nz) + block, BF16),
            pltpu.VMEM((2, nz) + block, BF16),
            pltpu.VMEM((2, nz - 1) + block, BF16),
            pltpu.VMEM((2, nz - 1) + block, BF16),
            pltpu.VMEM((4,) + block, F32),
            pltpu.SemaphoreType.DMA((remote,)),
            pltpu.SemaphoreType.DMA((remote,)),
            pltpu.SemaphoreType.DMA((44 + 2 * nz,)),
        ],
        compiler_params=pltpu.CompilerParams(
            collective_id=1, has_side_effects=True, vmem_limit_bytes=62 * MIB
        ),
        cost_estimate=pl.CostEstimate(
            flops=30 * rows * wide * wide, bytes_accessed=80 * wide * wide, transcendentals=0
        ),
        name="backward_pass",
    )(*inputs, stats, *seg, slot_col, mixed, params)


def gelu_both(value):
    square = value * value
    bent = jnp.tanh(ROOT_2_PI * value * (1.0 + CUBIC * square))
    half = 0.5 + 0.5 * bent
    slope = half + (0.5 * ROOT_2_PI) * value * (1.0 - bent * bent) * (1.0 + 3.0 * CUBIC * square)
    return (value * half, slope)


def expert_kernel(plan, *refs):
    moves, deep, chunk, chunks = plan[:4]
    expert, place, x_own, x_other, g_own, g_other = (plan[4],) + refs[:5]
    x_own, x_other, g_own, g_other = [
        one.at[expert] for one in (x_own, x_other, g_own, g_other)
    ]
    loaded = plan[5]
    weights, refs = refs[5 : 5 + loaded], refs[5 + loaded :]
    count = 4 if moves is not None else 2
    rows_out, refs = [refs[n // 2].at[n % 2] for n in range(4)], refs[2:]
    grads, refs = refs[:count], refs[count:]
    (win, wout, x, x_turned, g, branch, back, sum_in, sum_out, low_in, low_out, empty) = refs[:12]
    w_sems, x_sem, out_sems, row_sem = refs[12:]
    width = x.shape[1]
    most = x_own.shape[0] // BLOCK
    zed, flat, own_n, other_n = place[0], place[1], place[2], place[3]
    blocks = own_n + other_n
    tiles = (blocks + 1) // 2

    def block_rows(i):
        return pl.ds(pl.multiple_of(i * BLOCK, BLOCK), BLOCK)

    def each_block(act):
        for n, skip, a, b in ((own_n, 0, x_own, g_own), (other_n, own_n, x_other, g_other)):

            @pl.loop(0, n)
            def _(i):
                for outer, inner in ((a, x), (b, g)):
                    act(
                        pltpu.make_async_copy(
                            outer.at[block_rows(i)], inner.at[block_rows(skip + i)], x_sem
                        )
                    )

    each_block(lambda one: one.start())

    copies = []
    if loaded == 2:
        copies = [(weights[0], win), (weights[1], wout)]
    else:
        part_rows = chunk // moves.nf
        for stream in range(2):
            offsets = moves.relative(stream)
            half = len(offsets) // 2
            for number, offset in enumerate(offsets):
                piece = weights[stream * 2 + number // half].at[number % half]
                owner = flat ^ offset
                for k in range(moves.nz):
                    if stream == 0:
                        for part in range(2):
                            start = ((k * 2 + part) * moves.nf + owner) * deep
                            rows = pl.ds(pl.multiple_of(start, deep), deep)
                            copies.append((piece.at[k, part], win.at[rows]))
                    else:
                        start = (k * moves.nf + owner) * part_rows
                        rows = pl.ds(pl.multiple_of(start, part_rows), part_rows)
                        copies.append((piece.at[k], wout.at[rows]))
    begun = [
        pltpu.make_async_copy(source, target, w_sems.at[n])
        for n, (source, target) in enumerate(copies)
    ]
    for one in begun:
        one.start()
    empty[...] = jnp.zeros_like(empty)
    branch[...] = jnp.zeros_like(branch)
    back[...] = jnp.zeros_like(back)
    each_block(lambda one: one.wait())

    @pl.when(lax.rem(blocks, 2) == 1)
    def _():
        x[block_rows(blocks), :] = jnp.zeros((BLOCK, width), BF16)
        g[block_rows(blocks), :] = jnp.zeros((BLOCK, width), BF16)

    @pl.loop(0, tiles)
    def _(t):
        rows = pl.ds(pl.multiple_of(t * TILE, TILE), TILE)
        x_turned[:, rows] = x[rows, :].T

    for one in begun:
        one.wait()

    def grad_copies(j):
        columns = pl.ds(pl.multiple_of(j * chunk, chunk), chunk)
        if moves is None:
            made = [(low_in, grads[0].at[:, columns]), (low_out, grads[1].at[columns])]
        else:
            made = []
            k_of = zed ^ j
            half_deep = chunk // moves.nf // 2
            for stream in range(2):
                offsets = moves.relative(stream)
                half = len(offsets) // 2
                for number, offset in enumerate(offsets):
                    target = grads[stream * 2 + number // half].at[number % half]
                    owner = flat ^ offset
                    for part in range(2):
                        if stream == 0:
                            for k in range(moves.nz):
                                start = (((zed ^ k) * 2 + part) * moves.nf + owner) * deep
                                rows = pl.ds(pl.multiple_of(start, deep), deep)
                                place_of = target.at[k, pl.ds(part * deep, deep), columns]
                                made.append((low_in.at[rows], place_of))
                        else:
                            start = (owner * 2 + part) * half_deep
                            rows = pl.ds(pl.multiple_of(start, half_deep), half_deep)
                            place_of = target.at[k_of, :, pl.ds(part * width, width)]
                            made.append((low_out.at[rows], place_of))
        return [
            pltpu.make_async_copy(source, target, out_sems.at[n])
            for n, (source, target) in enumerate(made)
        ]

    @pl.loop(0, chunks)
    def _(j):
        columns = pl.ds(pl.multiple_of(j * chunk, chunk), chunk)
        sum_in[...] = jnp.zeros_like(sum_in)
        sum_out[...] = jnp.zeros_like(sum_out)

        @pl.loop(0, tiles)
        def _(t):
            rows = pl.ds(pl.multiple_of(t * TILE, TILE), TILE)
            g_tile = g[rows, :]
            inner = dot(x[rows, :], win[:, columns])
            grad_active = dot_nt(g_tile, wout[columns, :])
            active, slope = gelu_both(inner)
            active_low = active.astype(BF16)
            grad_inner = (grad_active * slope).astype(BF16)
            branch[rows, :] += dot(active_low, wout[columns, :])
            back[rows, :] += dot_nt(grad_inner, win[:, columns])
            sum_in[...] += dot(x_turned[:, rows], grad_inner)
            sum_out[...] += dot_tn(active_low, g_tile)

        @pl.when(j > 0)
        def _():
            for one in grad_copies(j - 1):
                one.wait()

        low_in[...] = sum_in[...].astype(BF16)
        low_out[...] = sum_out[...].astype(BF16)
        for one in grad_copies(j):
            one.start()

    @pl.loop(0, tiles)
    def _(t):
        rows = pl.ds(pl.multiple_of(t * TILE, TILE), TILE)
        x[rows, :] = branch[rows, :].astype(BF16)
        g[rows, :] = back[rows, :].astype(BF16)

    def each_result(act):
        for n, skip, a, b in (
            (own_n, 0, rows_out[0], rows_out[1]),
            (other_n, own_n, rows_out[2], rows_out[3]),
        ):

            @pl.loop(0, n)
            def _(i):
                for outer, inner in ((a, x), (b, g)):
                    act(
                        pltpu.make_async_copy(
                            inner.at[block_rows(skip + i)], outer.at[block_rows(i)], row_sem
                        )
                    )

            @pl.loop(n, most)
            def _(i):
                for outer in (a, b):
                    act(pltpu.make_async_copy(empty, outer.at[block_rows(i)], row_sem))

    each_result(lambda one: one.start())
    each_result(lambda one: one.wait())
    for one in grad_copies(chunks - 1):
        one.wait()


def expert_block(moves, expert, place, sorted_rows, weights, deep, half_hidden):
    capacity, width = sorted_rows[0].shape[1:]
    most = 2 * capacity
    if moves is not None:
        chunks = moves.nz
        copies = 4 * moves.nz * moves.nf
    else:
        chunks = 4
        copies = 2
    chunk = half_hidden // chunks
    anywhere = pl.BlockSpec(memory_space=pl.ANY)
    row_shape = jax.ShapeDtypeStruct((2, capacity, width), BF16)
    if moves is not None:
        block = (moves.nf // 2, moves.nz, 2 * deep, half_hidden)
        grads = [jax.ShapeDtypeStruct(block, BF16)] * 4
    else:
        grads = [jax.ShapeDtypeStruct(w.shape, BF16) for w in weights]
    return pl.pallas_call(
        functools.partial(expert_kernel, (moves, deep, chunk, chunks, expert, len(weights))),
        in_specs=[pl.BlockSpec(memory_space=pltpu.SMEM)] + [anywhere] * (4 + len(weights)),
        out_specs=[anywhere] * (2 + len(grads)),
        out_shape=[row_shape] * 2 + grads,
        scratch_shapes=[
            pltpu.VMEM((width, half_hidden), BF16),
            pltpu.VMEM((half_hidden, width), BF16),
            pltpu.VMEM((most, width), BF16),
            pltpu.VMEM((width, most), BF16),
            pltpu.VMEM((most, width), BF16),
            pltpu.VMEM((most, width), F32),
            pltpu.VMEM((most, width), F32),
            pltpu.VMEM((width, chunk), F32),
            pltpu.VMEM((chunk, width), F32),
            pltpu.VMEM((width, chunk), BF16),
            pltpu.VMEM((chunk, width), BF16),
            pltpu.VMEM((BLOCK, width), BF16),
            pltpu.SemaphoreType.DMA((copies,)),
            pltpu.SemaphoreType.DMA,
            pltpu.SemaphoreType.DMA((copies,)),
            pltpu.SemaphoreType.DMA,
        ],
        compiler_params=pltpu.CompilerParams(vmem_limit_bytes=56 * MIB),
        cost_estimate=pl.CostEstimate(
            flops=12 * 1024 * width * half_hidden,
            bytes_accessed=8 * width * half_hidden + 32 * 1024 * width,
            transcendentals=1024 * half_hidden,
        ),
        name="expert_block",
    )(place, *sorted_rows, *weights)


def gather_experts_whole(w_expert_in, w_expert_out, core, nz):
    width, hidden = w_expert_out.shape[2], w_expert_in.shape[2]
    all_in = lax.all_gather(w_expert_in, AXES, axis=1, tiled=True)
    all_out = lax.all_gather(w_expert_out, AXES, axis=1, tiled=True)
    all_in = all_in.reshape(EXPERTS, width, nz, 2, hidden // (2 * nz))
    all_in = lax.dynamic_index_in_dim(all_in, core, 3, False)
    all_in = all_in.reshape(EXPERTS, width, hidden // 2)
    all_out = all_out.reshape(EXPERTS, nz, 2, hidden // (2 * nz), width)
    all_out = lax.dynamic_index_in_dim(all_out, core, 2, False)
    all_out = all_out.reshape(EXPERTS, hidden // 2, width)
    return [[all_in[e], all_out[e]] for e in range(EXPERTS)]


def local(
    nd,
    nf,
    tokens,
    seq_lengths,
    expert_ids,
    grad_out,
    ln1_gain,
    ln1_bias,
    w_qkv,
    w_attn_out,
    ln2_gain,
    ln2_bias,
    w_expert_in,
    w_expert_out,
):
    rows, width = tokens.shape
    deep = w_qkv.shape[0]
    hidden = w_expert_in.shape[2]
    half_hidden = hidden // 2
    half = width // 2
    moves = Moves(nd, nf)
    nz = moves.nz
    staged = deep % 32 == 0
    core = lax.rem(lax.axis_index("dp"), 2)
    zed = lax.axis_index("dp") // 2
    flat = lax.axis_index("fsdp")
    place = jnp.stack([zed, core, flat]).astype(jnp.int32)

    positions = jnp.arange(rows, dtype=jnp.int32)
    bounds = jnp.cumsum(seq_lengths[0])
    segment = jnp.sum((positions[:, None] >= bounds[None, :]).astype(jnp.int32), axis=1)
    seg_row = jnp.broadcast_to(segment[None, :], (8, rows))
    seg_col = jnp.broadcast_to(segment[:, None], (rows, BLOCK))
    routed = expert_ids[:, 0]
    rank_second = jnp.cumsum(routed) - routed
    second_n = jnp.sum(routed)
    capacity = 3 * rows // 4
    slot = jnp.where(routed == 1, capacity + rank_second, positions - rank_second)
    split = jnp.stack([rows - second_n, second_n]).astype(jnp.int32)
    split = (split + BLOCK - 1) // BLOCK

    params = jnp.stack([ln1_gain, ln1_bias, ln2_gain, ln2_bias], axis=1)
    params = jnp.pad(params, ((0, 0), (0, BLOCK - 4)))
    mine = jnp.concatenate([w_qkv, w_attn_out, params], axis=1)
    arguments = (tokens, grad_out, mine, w_expert_in, w_expert_out)
    if staged:
        return staged_block(moves, arguments, seg_row, seg_col, slot, split, (zed, core, flat))
    return plain_block(moves, arguments, seg_row, seg_col, slot, split, (zed, core, flat))


def staged_block(moves, arguments, seg_row, seg_col, slot, split, place):
    tokens, grad_out, mine, w_expert_in, w_expert_out = arguments
    rows, width = tokens.shape
    deep, hidden = w_expert_in.shape[1:]
    half_hidden = hidden // 2
    capacity = 3 * rows // 4
    zed, core, flat = place
    note = jnp.broadcast_to(split[:, None].astype(BF16), (2, BLOCK))
    note = jnp.pad(note, ((0, 14), (0, 0)))
    slot_row = jnp.broadcast_to(slot[None, :], (8, rows))
    slot_col = jnp.broadcast_to(slot[:, None], (rows, BLOCK))
    outs = forward_pass(
        moves, tokens, mine, w_expert_in, w_expert_out, seg_row, seg_col, slot_row, grad_out, note
    )
    whole_qkv, whole_attn, params, first_in = [one.reshape(-1, one.shape[-1]) for one in outs[:4]]
    first_out = outs[4].reshape(half_hidden, width)
    held = outs[5:7]
    sorted_other, grad_other, noted = outs[7:10]
    normed_one, projected, mixed, stats, hidden_one, sorted_rows, grad_sorted = outs[10:]
    last = [moves.gather_last(held[0], 0), moves.gather_last(held[1], 1)]
    weights = [[first_in, first_out], [held[0], last[0], held[1], last[1]]]
    by_expert = lambda value: value.reshape(EXPERTS, capacity, width)
    row_inputs = [by_expert(one) for one in (sorted_rows, sorted_other, grad_sorted, grad_other)]
    split_other = noted[:2, 0].astype(jnp.int32)
    made = []
    for e in range(EXPERTS):
        table = jnp.stack([zed, flat, split[e], split_other[e]]).astype(jnp.int32)
        made.append(expert_block(moves, e, table, row_inputs, weights[e], deep, half_hidden))
        if e == 0:
            arrived = [moves.flat(made[0][3 + 2 * n], moves.orders[n][0]) for n in range(2)]
    results = backward_pass(
        moves,
        deep,
        [projected, whole_qkv, whole_attn, hidden_one, normed_one, tokens, grad_out],
        [made[0][0], made[1][0], made[0][1], made[1][1]],
        [made[0][2], made[0][4]] + arrived + list(made[1][2:]),
        stats.T,
        [seg_row, seg_col],
        slot_col,
        mixed,
        params,
    )
    block_result, grad_input, share_in, share_out, share_qkv, share_attn, vectors = results[:7]
    vectors = vectors[:, :4].T
    return (
        block_result,
        grad_input,
        vectors[0],
        vectors[1],
        share_qkv,
        share_attn,
        vectors[2],
        vectors[3],
        share_in,
        share_out,
    )


def plain_block(moves, arguments, seg_row, seg_col, slot, split, place):
    tokens, grad_out, mine, w_expert_in, w_expert_out = arguments
    rows, width = tokens.shape
    hidden = w_expert_in.shape[2]
    deep = mine.shape[0]
    nz = moves.nz
    zed, core, flat = place
    capacity = 3 * rows // 4
    whole = lax.all_gather(mine, AXES, axis=0, tiled=True)
    whole_qkv, whole_attn = whole[:, : 3 * width], whole[:, 3 * width : 4 * width]
    params = whole[:, 4 * width :]
    expert_weights = gather_experts_whole(w_expert_in, w_expert_out, core, nz)
    gain_one, bias_one, gain_two, bias_two = [
        params[:, n].astype(F32)[None, :] for n in range(4)
    ]
    tokens_wide = tokens.astype(F32)
    scaled_one, inverse_one = norm_parts(tokens_wide)
    normed_one = (scaled_one * gain_one + bias_one).astype(BF16)
    projected = dot(normed_one, whole_qkv).astype(BF16)
    mixed, stats = attention_forward(projected, seg_row, seg_col, 0, width // BLOCK)
    hidden_one = tokens_wide + dot(mixed, whole_attn)
    scaled_two, inverse_two = norm_parts(hidden_one)
    normed_two = (scaled_two * gain_two + bias_two).astype(BF16)
    slots = jnp.arange(EXPERTS * capacity, dtype=jnp.int32)[:, None]
    spread = (slots == slot[None, :]).astype(BF16)
    by_expert = lambda value: value.reshape(EXPERTS, capacity, width)
    row_inputs = []
    for value in (normed_two, grad_out):
        ordered = dot(spread, value).astype(BF16)
        row_inputs += [by_expert(ordered), by_expert(moves.core(ordered))]
    split_other = moves.core(jnp.broadcast_to(split[:, None], (2, BLOCK)))[:, 0]
    results, grad_pieces = [], []
    for e in range(EXPERTS):
        table = jnp.stack([zed, flat, split[e], split_other[e]]).astype(jnp.int32)
        outs = expert_block(None, e, table, row_inputs, expert_weights[e], deep, hidden // 2)
        results.append(add_low(outs[0], moves.core(outs[1])))
        grad_pieces.append(outs[2:])
    both = jnp.concatenate(results, axis=1)
    grad_normed_two = dot_tn(spread, both[1])
    block_result = (hidden_one + dot_tn(spread, both[0])).astype(BF16)
    grad_hidden = grad_out.astype(F32) + norm_back(
        grad_normed_two, scaled_two, inverse_two, gain_two
    )
    grad_branch = grad_hidden.astype(BF16)
    grad_mixed = dot_nt(grad_branch, whole_attn).astype(BF16)
    trio = attention_backward(
        projected, grad_mixed, stats.T, seg_row, seg_col, 0, width // BLOCK
    )
    grad_projected = jnp.concatenate(trio, axis=1)
    grad_normed_one = dot_nt(grad_projected, whole_qkv)
    grad_input = grad_hidden + norm_back(grad_normed_one, scaled_one, inverse_one, gain_one)
    vectors = jnp.stack(
        [
            jnp.sum(grad_normed_one * scaled_one, axis=0),
            jnp.sum(grad_normed_one, axis=0),
            jnp.sum(grad_normed_two * scaled_two, axis=0),
            jnp.sum(grad_normed_two, axis=0),
        ]
    )
    own = lambda value, dim: lax.psum_scatter(value, AXES, scatter_dimension=dim, tiled=True)
    vectors = own(vectors, 1)
    full_in = jnp.stack([pieces[0] for pieces in grad_pieces])
    full_out = jnp.stack([pieces[1] for pieces in grad_pieces])
    full_in = full_in.reshape(EXPERTS, width, nz, 1, -1).astype(F32)
    full_out = full_out.reshape(EXPERTS, nz, 1, -1, width).astype(F32)
    chosen = jnp.arange(2) == core
    full_in = jnp.where(chosen[None, None, None, :, None], full_in, 0.0)
    full_out = jnp.where(chosen[None, None, :, None, None], full_out, 0.0)
    return (
        block_result,
        grad_input,
        vectors[0],
        vectors[1],
        own(dot_tn(normed_one, grad_projected), 0),
        own(dot_tn(mixed, grad_branch), 0),
        vectors[2],
        vectors[3],
        own(full_in.reshape(EXPERTS, width, hidden), 1),
        own(full_out.reshape(EXPERTS, hidden, width), 1),
    )


def solution(mesh):
    rows = P(AXES, None)
    vector = P(AXES)
    expert = P(None, AXES, None)
    return jax.shard_map(
        functools.partial(local, mesh.shape["dp"], mesh.shape["fsdp"]),
        mesh=mesh,
        in_specs=(
            rows, rows, rows, rows, vector, vector, rows, rows, vector, vector, expert, expert
        ),
        out_specs=(
            rows, rows, vector, vector, rows, rows, vector, vector, expert, expert
        ),
        check_vma=False,
    )
```

```python
import functools

import jax
import jax.numpy as jnp
from jax import lax
from jax.experimental import pallas as pl
from jax.experimental.pallas import tpu as pltpu
from jax.sharding import PartitionSpec as P

HEADS = 16
HEAD_DIM = 64
EXPERTS = 2
EPSILON = 1e-05
MASKED = -1000000000.0
AXES = ("dp", "fsdp")
BLOCK = 128
TILE = 256
MIB = 1024 * 1024
PARTS = 4
F32 = jnp.float32
BF16 = jnp.bfloat16
NT = (((1,), (1,)), ((), ()))
TN = (((0,), (0,)), ((), ()))
ROOT_2_PI = 0.7978845608028654
CUBIC = 0.044715


def dot(a, b):
    return jnp.dot(a, b, preferred_element_type=F32)


def dot_nt(a, b):
    return lax.dot_general(a, b, NT, preferred_element_type=F32)


def dot_tn(a, b):
    return lax.dot_general(a, b, TN, preferred_element_type=F32)


def norm_parts(values):
    average = jnp.mean(values, axis=-1, keepdims=True)
    centred = values - average
    variance = jnp.mean(centred * centred, axis=-1, keepdims=True)
    inverse = lax.rsqrt(variance + EPSILON)
    return (centred * inverse, inverse)


def norm_back(grad_normed, scaled, inverse, gain):
    grad_scaled = grad_normed * gain
    middle = jnp.mean(grad_scaled, axis=-1, keepdims=True)
    along = jnp.mean(grad_scaled * scaled, axis=-1, keepdims=True)
    return inverse * (grad_scaled - middle - scaled * along)


class Moves:
    def __init__(self, nd, nf):
        self.nz, self.nf = nd // 2, nf
        bits = []
        bit = 1
        while bit < nf:
            bits.append(bit)
            bit *= 2
        self.orders = (tuple(bits), tuple(reversed(bits)))

    def send(self, value, where):
        pairs = []
        for zed in range(self.nz):
            for core in range(2):
                for flat in range(self.nf):
                    z_to, core_to, f_to = where(zed, core, flat)
                    pairs.append(
                        (
                            (zed * 2 + core) * self.nf + flat,
                            (z_to * 2 + core_to) * self.nf + f_to,
                        )
                    )
        return lax.ppermute(value, AXES, pairs)

    def core(self, value):
        return self.send(value, lambda z, c, f: (z, 1 - c, f))

    def flat(self, value, bit):
        return self.send(value, lambda z, c, f: (z, c, f ^ bit))

    def along(self, value, steps):
        return self.send(value, lambda z, c, f: ((z + steps) % self.nz, c, f))

    def near(self, value, bit):
        return self.send(value, lambda z, c, f: (z ^ bit, c, f))

    def relative(self, stream):
        offsets = [0]
        for bit in reversed(self.orders[stream]):
            offsets = offsets + [one ^ bit for one in offsets]
        return tuple(offsets)

    def gather_z(self, value):
        return [value] + [self.along(value, k) for k in range(1, self.nz)]

    def gather_z_pair(self, value):
        held, bit = value[:, None], 1
        while 2 * bit < self.nz:
            held = jnp.concatenate([held, self.near(held, bit)], axis=1)
            bit *= 2
        got = self.near(held, bit)
        return [jnp.concatenate([held[n], got[n]], axis=0) for n in range(2)], got

    def gather_first(self, value, stream):
        held = value[None]
        for bit in tuple(reversed(self.orders[stream]))[:-1]:
            held = jnp.concatenate([held, self.flat(held, bit)], axis=0)
        return held

    def gather_last(self, held, stream):
        return self.flat(held, self.orders[stream][0])

    def reduce_flat(self, keep, sent, stream):
        order = self.orders[stream]
        now = add_low(keep, self.flat(sent, order[0]))
        for bit in order[1:]:
            half = now.shape[0] // 2
            now = add_low(now[:half], self.flat(now[half:], bit))
        return now[0]

    def reduce_z(self, value):
        total = value[0].astype(F32)
        for k in range(1, self.nz):
            total = total + self.along(value[k], k).astype(F32)
        return total

    def reduce_z_pair(self, value):
        bit = self.nz // 2
        while bit > 1:
            value = add_low(value[:bit], self.near(value[bit:], bit))
            bit //= 2
        return value[0].astype(F32) + self.near(value[1], 1).astype(F32)


def after(value, *others):
    return lax.optimization_barrier((value,) + others)[0]


def add_low(a, b):
    return (a.astype(F32) + b.astype(F32)).astype(BF16)


def attention_forward_kernel(seg_row, seg_col, q, k, v, out, stats, bias):
    rows = q.shape[0]
    pair = pl.program_id(0)
    lane = lax.broadcasted_iota(jnp.int32, (1, BLOCK), 1)

    @pl.when(pair == 0)
    def _():
        stats[...] = jnp.zeros_like(stats)
        for i in range(rows // TILE):
            span = (i + 1) * TILE
            place = slice(i * TILE, span)
            query = lax.broadcasted_iota(jnp.int32, (TILE, span), 0) + i * TILE
            key = lax.broadcasted_iota(jnp.int32, (TILE, span), 1)
            same = seg_col[place, 0:1] == seg_row[0:1, :span]
            bias[place, :span] = jnp.where(same & (key <= query), 0.0, MASKED)

    for i in range(rows // TILE):
        span = (i + 1) * TILE
        place = slice(i * TILE, span)
        query = q[place, :] * jnp.asarray(HEAD_DIM**-0.5, BF16)
        mixed = jnp.zeros((TILE, BLOCK), F32)
        held = stats[place, :]
        for side in range(2):
            mine = (lane // HEAD_DIM) == side
            part = jnp.where(mine, query, jnp.zeros_like(query))
            scores = dot_nt(part, k[:span, :]) + bias[place, :span]
            highest = jnp.max(scores, axis=1, keepdims=True)
            terms = jnp.exp(scores - highest)
            total = jnp.sum(terms, axis=1, keepdims=True)
            attend = (terms * (1.0 / total)).astype(BF16)
            mixed = jnp.where(mine, dot(attend, v[:span, :]), mixed)
            held = jnp.where(lane == 2 * pair + side, highest + jnp.log(total), held)
        stats[place, :] = held
        out[place, :] = mixed.astype(BF16)


def attention_forward(projected, seg_row, seg_col, first, count):
    rows, width = projected.shape[0], projected.shape[1] // 3
    pairs = width // BLOCK
    column = lambda start: pl.BlockSpec((rows, BLOCK), lambda h: (0, start + h))
    whole = lambda shape: pl.BlockSpec(shape, lambda h: (0, 0))
    return pl.pallas_call(
        attention_forward_kernel,
        grid=(count,),
        in_specs=[
            whole((8, rows)),
            whole((rows, BLOCK)),
            column(first),
            column(first + pairs),
            column(first + 2 * pairs),
        ],
        out_specs=[column(0), whole((rows, BLOCK))],
        out_shape=[
            jax.ShapeDtypeStruct((rows, count * BLOCK), BF16),
            jax.ShapeDtypeStruct((rows, BLOCK), F32),
        ],
        scratch_shapes=[pltpu.VMEM((rows, rows), F32)],
        compiler_params=pltpu.CompilerParams(vmem_limit_bytes=40 * MIB),
        cost_estimate=pl.CostEstimate(
            flops=4 * rows * rows * count * BLOCK,
            bytes_accessed=8 * rows * count * BLOCK,
            transcendentals=2 * count * rows * rows,
        ),
        name="attention_forward",
    )(seg_row, seg_col, projected, projected, projected)


def attention_backward_kernel(first, seg_row, seg_col, stats, q, k, v, g, dq, dk, dv, bias, dks, dvs):
    rows = q.shape[0]
    pair = pl.program_id(0)
    lane = lax.broadcasted_iota(jnp.int32, (1, BLOCK), 1)
    row = lax.broadcasted_iota(jnp.int32, (BLOCK, 1), 0)

    @pl.when(pair == 0)
    def _():
        for i in range(rows // TILE):
            span = (i + 1) * TILE
            place = slice(i * TILE, span)
            query = lax.broadcasted_iota(jnp.int32, (span, TILE), 1) + i * TILE
            key = lax.broadcasted_iota(jnp.int32, (span, TILE), 0)
            same = seg_col[:span, 0:1] == seg_row[0:1, place]
            bias[:span, place] = jnp.where(same & (key <= query), 0.0, MASKED)

    dks[...] = jnp.zeros_like(dks)
    dvs[...] = jnp.zeros_like(dvs)
    k_turned = k[...].T
    for i in range(rows // TILE):
        span = (i + 1) * TILE
        place = slice(i * TILE, span)
        query = q[place, :] * jnp.asarray(HEAD_DIM**-0.5, BF16)
        grad = g[place, :]
        turned = jnp.zeros((BLOCK, TILE), F32)
        for side in range(2):
            mine = (lane // HEAD_DIM) == side
            part = jnp.where(mine, query, jnp.zeros_like(query))
            grad_part = jnp.where(mine, grad, jnp.zeros_like(grad))
            level = stats[pl.ds(2 * (first + pair) + side, 1), place]
            scores = dot_nt(k[:span, :], part) + bias[:span, place]
            attend = jnp.exp(scores - level)
            grad_attend = dot_nt(v[:span, :], grad_part)
            inner = jnp.sum(attend * grad_attend, axis=0, keepdims=True)
            grad_scores = (attend * (grad_attend - inner)).astype(BF16)
            dks[:span, :] += dot(grad_scores, part)
            dvs[:span, :] += dot(attend.astype(BF16), grad_part)
            turned = jnp.where(
                (row // HEAD_DIM) == side, dot(k_turned[:, :span], grad_scores), turned
            )
        dq[place, :] = (turned.T * HEAD_DIM**-0.5).astype(BF16)
    dk[...] = dks[...].astype(BF16)
    dv[...] = dvs[...].astype(BF16)


def attention_backward(projected, grad_mixed, stats, seg_row, seg_col, first, count):
    rows, width = projected.shape[0], projected.shape[1] // 3
    pairs = width // BLOCK
    column = lambda start: pl.BlockSpec((rows, BLOCK), lambda h: (0, start + h))
    whole = lambda shape: pl.BlockSpec(shape, lambda h: (0, 0))
    share = jax.ShapeDtypeStruct((rows, count * BLOCK), BF16)
    return pl.pallas_call(
        functools.partial(attention_backward_kernel, first),
        grid=(count,),
        in_specs=[
            whole((8, rows)),
            whole((rows, BLOCK)),
            whole((BLOCK, rows)),
            column(first),
            column(first + pairs),
            column(first + 2 * pairs),
            column(first),
        ],
        out_specs=[column(0), column(0), column(0)],
        out_shape=[share, share, share],
        scratch_shapes=[
            pltpu.VMEM((rows, rows), F32),
            pltpu.VMEM((rows, BLOCK), F32),
            pltpu.VMEM((rows, BLOCK), F32),
        ],
        compiler_params=pltpu.CompilerParams(vmem_limit_bytes=40 * MIB),
        cost_estimate=pl.CostEstimate(
            flops=10 * rows * rows * count * BLOCK,
            bytes_accessed=14 * rows * count * BLOCK,
            transcendentals=2 * count * rows * rows,
        ),
        name="attention_backward",
    )(seg_row, seg_col, stats, projected, projected, projected, grad_mixed)


class Copies:
    def __init__(self, send_sems, recv_sems):
        self.send_sems, self.recv_sems, self.made = send_sems, recv_sems, []

    def start(self, source, target, device):
        n = len(self.made)
        one = pltpu.make_async_remote_copy(
            src_ref=source,
            dst_ref=target,
            send_sem=self.send_sems.at[n],
            recv_sem=self.recv_sems.at[n],
            device_id=device,
            device_id_type=pl.DeviceIdType.MESH,
        )
        one.start()
        self.made.append(one)
        return one


def wait_in(copies):
    for one in copies:
        one.wait_recv()


def forward_kernel(
    moves,
    tokens,
    mine,
    own_in,
    own_out,
    seg_row,
    seg_col,
    slot_row,
    grad_out,
    out_qkv,
    out_attn,
    out_params,
    first_in,
    first_out,
    column_in,
    column_out,
    sorted_other,
    grad_other,
    normed,
    projected,
    mixed,
    stats,
    hidden,
    sorted_rows,
    grad_sorted,
    weights,
    bias,
    normed_two,
    send_sems,
    recv_sems,
    local_sems,
):
    nz, nf = moves.nz, moves.nf
    dp, flat = lax.axis_index("dp"), lax.axis_index("fsdp")
    zed, core = dp // 2, lax.rem(dp, 2)
    rows, wide = tokens.shape
    sibling = (zed * 2 + 1 - core, flat)
    others = [(lax.rem(zed + k, nz) * 2 + core, flat) for k in range(1, nz)]
    hops = {bit: (dp, flat ^ bit) for bit in moves.orders[0]}

    barrier = pltpu.get_barrier_semaphore()
    for device in [sibling] + others + list(hops.values()):
        pl.semaphore_signal(barrier, inc=1, device_id=device, device_id_type=pl.DeviceIdType.MESH)
    pl.semaphore_wait(barrier, 1 + len(others) + len(hops))

    remote = Copies(send_sems, recv_sems)
    local = []

    def local_start(source, target):
        one = pltpu.make_async_copy(source, target, local_sems.at[len(local)])
        one.start()
        local.append(one)
        return one

    own = local_start(mine, weights.at[zed, core, flat])
    stream_columns = (slice(0, 2 * wide), slice(2 * wide, 4 * wide + BLOCK))

    def send_column(stream):
        columns = stream_columns[stream]
        return [
            remote.start(
                mine.at[:, columns], weights.at[zed, core, flat, :, columns], device
            )
            for device in others
        ]

    column = [send_column(0)]
    targets = (first_in.at[zed, core, flat], column_in.at[zed, core])
    cut = own_in.shape[2] // (2 * nz)
    crossed, blocks = [], []
    for e in range(EXPERTS):
        for z_of in range(nz):
            target = targets[e].at[:, pl.ds(z_of * cut, cut)]
            theirs, ours = [
                own_in.at[e, :, pl.ds(pl.multiple_of((2 * z_of + which) * cut, cut), cut)]
                for which in (1 - core, core)
            ]
            crossed.append(remote.start(theirs, target, sibling))
            blocks.append(local_start(ours, target))
    blocks.append(local_start(own_out.at[0], first_out.at[zed, flat]))
    blocks.append(local_start(own_out.at[1], column_out.at[zed]))

    def sort_rows(source, target):
        @pl.loop(0, target.shape[0] // TILE)
        def _(t):
            place = pl.ds(pl.multiple_of(t * TILE, TILE), TILE)
            slot = lax.broadcasted_iota(jnp.int32, (TILE, rows), 0) + t * TILE
            chosen = (slot == slot_row[0:1, :]).astype(F32).astype(BF16)
            target[place, :] = dot(chosen, source[...]).astype(BF16)

    sort_rows(grad_out, grad_sorted)
    for i in range(rows // TILE):
        span = (i + 1) * TILE
        place = slice(i * TILE, span)
        query = lax.broadcasted_iota(jnp.int32, (TILE, span), 0) + i * TILE
        key = lax.broadcasted_iota(jnp.int32, (TILE, span), 1)
        same = seg_col[place, 0:1] == seg_row[0:1, :span]
        bias[place, :span] = jnp.where(same & (key <= query), 0.0, MASKED)
    stats[...] = jnp.zeros_like(stats)

    def send_weights(stream, owner, device):
        place = weights.at[:, core, owner, :, stream_columns[stream]]
        return remote.start(place, place, device)

    near = [tuple(reversed(moves.orders[n]))[0] for n in range(2)]
    far = [moves.orders[n][0] for n in range(2)]
    hop_near, hop_far, across = [], [], []
    own.wait()
    wait_in(column[0])
    column.append(send_column(1))
    hop_near.append(send_weights(0, flat, hops[near[0]]))
    hop_far.append(send_weights(0, flat, hops[far[0]]))
    across.append(send_weights(0, flat, sibling))

    wait_in(crossed)
    for one in blocks:
        one.wait()
    wait_in(column[1])
    place = first_in.at[zed, :, flat]
    first_column = [[remote.start(place, place, device) for device in others]]
    hop_near.append(send_weights(1, flat, hops[near[1]]))
    hop_far.append(send_weights(1, flat, hops[far[1]]))
    across.append(send_weights(1, flat, sibling))
    wait_in(hop_near)
    hop_last = [send_weights(n, flat ^ near[n], hops[far[n]]) for n in range(2)]
    across += [send_weights(n, flat ^ near[n], sibling) for n in range(2)]
    exchanged = [remote.start(grad_sorted, grad_other, sibling)]

    def send_first(stream, owner, device):
        place = first_in.at[:, :, owner] if stream == 0 else first_out.at[:, owner]
        return remote.start(place, place, device)

    first_near, first_far = [], []
    wait_in(first_column[0])
    first_column.append(
        [
            remote.start(own_out.at[0], first_out.at[zed, flat], device)
            for device in others
        ]
    )
    first_near.append(send_first(0, flat, hops[near[0]]))
    first_far.append(send_first(0, flat, hops[far[0]]))
    wait_in(hop_far)
    across += [send_weights(n, flat ^ far[n], sibling) for n in range(2)]
    wait_in(hop_last)
    across += [send_weights(n, flat ^ near[n] ^ far[n], sibling) for n in range(2)]
    wait_in(across)
    whole = 2 * nz * nf * mine.shape[0]
    writes = [
        local_start(weights.at[:, :, :, :, pl.ds(0, 3 * wide)], out_qkv),
        local_start(weights.at[:, :, :, :, pl.ds(3 * wide, wide)], out_attn),
        local_start(weights.at[:, :, :, :, pl.ds(4 * wide, BLOCK)], out_params),
    ]
    turned = weights[:, :, :, :, pl.ds(4 * wide, BLOCK)].reshape(whole, BLOCK).astype(F32).T
    gain, shift = turned[0:1, :], turned[1:2, :]

    @pl.loop(0, rows // TILE)
    def _(t):
        place = pl.ds(pl.multiple_of(t * TILE, TILE), TILE)
        scaled, _ = norm_parts(tokens[place, :].astype(F32))
        normed[place, :] = (scaled * gain + shift).astype(BF16)
        for part in range(3):
            columns = pl.ds(part * wide, wide)
            matrix = weights[:, :, :, :, columns].reshape(whole, wide)
            projected[place, columns] = dot(normed[place, :], matrix).astype(BF16)

    wait_in(first_column[1])
    first_near.append(send_first(1, flat, hops[near[1]]))
    first_far.append(send_first(1, flat, hops[far[1]]))
    second_column = []
    for device in others:
        place = column_in.at[zed]
        second_column.append(remote.start(place, place, device))
        second_column.append(remote.start(own_out.at[1], column_out.at[zed], device))

    lane = lax.broadcasted_iota(jnp.int32, (1, BLOCK), 1)
    pairs = wide // BLOCK

    def attend_pair(pair):
        columns = [
            pl.ds(pl.multiple_of(n * wide + pair * BLOCK, BLOCK), BLOCK) for n in range(3)
        ]
        for i in range(rows // TILE):
            span = (i + 1) * TILE
            place = slice(i * TILE, span)
            query = projected[place, columns[0]] * jnp.asarray(HEAD_DIM**-0.5, BF16)
            result = jnp.zeros((TILE, BLOCK), F32)
            held = stats[place, :]
            for side in range(2):
                ours = (lane // HEAD_DIM) == side
                part = jnp.where(ours, query, jnp.zeros_like(query))
                scores = dot_nt(part, projected[:span, columns[1]]) + bias[place, :span]
                highest = jnp.max(scores, axis=1, keepdims=True)
                terms = jnp.exp(scores - highest)
                total = jnp.sum(terms, axis=1, keepdims=True)
                attend = (terms * (1.0 / total)).astype(BF16)
                result = jnp.where(ours, dot(attend, projected[:span, columns[2]]), result)
                held = jnp.where(lane == 2 * pair + side, highest + jnp.log(total), held)
            stats[place, :] = held
            mixed[place, columns[0]] = result.astype(BF16)

    wait_in([first_near[0]])
    first_last = [send_first(0, flat ^ near[0], hops[far[0]])]

    @pl.loop(0, pairs // 2)
    def _(pair):
        attend_pair(pair)

    wait_in([first_near[1]])
    first_last.append(send_first(1, flat ^ near[1], hops[far[1]]))

    @pl.loop(pairs // 2, pairs)
    def _(pair):
        attend_pair(pair)

    gain_two, shift_two = turned[2:3, :], turned[3:4, :]

    @pl.loop(0, rows // TILE)
    def _(t):
        place = pl.ds(pl.multiple_of(t * TILE, TILE), TILE)
        matrix = weights[:, :, :, :, pl.ds(3 * wide, wide)].reshape(whole, wide)
        total = tokens[place, :].astype(F32) + dot(mixed[place, :], matrix)
        hidden[place, :] = total
        scaled, _ = norm_parts(total)
        normed_two[place, :] = (scaled * gain_two + shift_two).astype(BF16)

    sort_rows(normed_two, sorted_rows)
    exchanged.append(remote.start(sorted_rows, sorted_other, sibling))
    wait_in(first_far)
    wait_in(first_last)
    wait_in(second_column)
    wait_in(exchanged)
    for one in remote.made:
        one.wait_send()
    for one in writes:
        one.wait()


def forward_pass(moves, tokens, mine, own_in, own_out, seg_row, seg_col, slot_row, grad_out):
    nz, nf = moves.nz, moves.nf
    rows, wide = tokens.shape
    deep, half = own_in.shape[1], own_in.shape[2] // 2
    part = own_out.shape[1]
    capacity = 3 * rows // 4
    anywhere = pl.BlockSpec(memory_space=pl.ANY)
    inside = pl.BlockSpec(memory_space=pltpu.VMEM)
    shape = jax.ShapeDtypeStruct
    remote = 6 * (nz - 1) + 2 * nz + 24
    return pl.pallas_call(
        functools.partial(forward_kernel, moves),
        in_specs=[inside] * 8,
        out_specs=[anywhere] * 9 + [inside] * 7,
        out_shape=[
            shape((nz, 2, nf, deep, 3 * wide), BF16),
            shape((nz, 2, nf, deep, wide), BF16),
            shape((nz, 2, nf, deep, BLOCK), BF16),
            shape((nz, 2, nf, deep, half), BF16),
            shape((nz, nf, part, wide), BF16),
            shape((nz, 2, deep, half), BF16),
            shape((nz, part, wide), BF16),
            shape((EXPERTS * capacity, wide), BF16),
            shape((EXPERTS * capacity, wide), BF16),
            shape((rows, wide), BF16),
            shape((rows, 3 * wide), BF16),
            shape((rows, wide), BF16),
            shape((rows, BLOCK), F32),
            shape((rows, wide), F32),
            shape((EXPERTS * capacity, wide), BF16),
            shape((EXPERTS * capacity, wide), BF16),
        ],
        scratch_shapes=[
            pltpu.VMEM((nz, 2, nf, deep, 4 * wide + BLOCK), BF16),
            pltpu.VMEM((rows, rows), F32),
            pltpu.VMEM((rows, wide), BF16),
            pltpu.SemaphoreType.DMA((remote,)),
            pltpu.SemaphoreType.DMA((remote,)),
            pltpu.SemaphoreType.DMA((2 * nz + 6,)),
        ],
        compiler_params=pltpu.CompilerParams(
            collective_id=0, has_side_effects=True, vmem_limit_bytes=60 * MIB
        ),
        cost_estimate=pl.CostEstimate(
            flops=10 * rows * wide * wide, bytes_accessed=80 * wide * wide, transcendentals=0
        ),
        name="forward_pass",
    )(tokens, mine, own_in, own_out, seg_row, seg_col, slot_row, grad_out)


def sum_low(*values):
    total = values[0].astype(F32)
    for one in values[1:]:
        total = total + one.astype(F32)
    return total


def backward_kernel(
    moves,
    deep,
    projected,
    whole_qkv,
    whole_attn,
    hidden,
    normed_out,
    tokens_in,
    grad_out,
    rows_first,
    rows_second,
    landed_first,
    other_second,
    keep_first_in,
    keep_first_out,
    arrived_in,
    arrived_out,
    first_hop_in,
    first_hop_out,
    first_own,
    first_landed,
    keep_in,
    sent_in,
    keep_out,
    sent_out,
    stats,
    seg_row,
    seg_col,
    slot_col,
    mixed,
    params,
    block_out,
    grad_tokens,
    share_in,
    share_out,
    share_qkv,
    share_attn,
    share_vectors,
    got_in,
    got_out,
    hop_in,
    hop_out,
    landed,
    wide_low,
    wide_f32,
    grad_projected,
    grad_mixed,
    branch,
    normed,
    tokens,
    key_sums,
    value_sums,
    low,
    cross,
    got_q,
    hop_q,
    z_q,
    up_q,
    vec,
    cross_vec,
    got_vec,
    hop_vec,
    z_vec,
    up,
    spare,
    up_first,
    z_first,
    early,
    z_second,
    final,
    send_sems,
    recv_sems,
    local_sems,
):
    nz, nf = moves.nz, moves.nf
    dp, flat = lax.axis_index("dp"), lax.axis_index("fsdp")
    zed, core = dp // 2, lax.rem(dp, 2)
    rows, wide = tokens.shape
    share = wide // PARTS
    sibling = (zed * 2 + 1 - core, flat)
    others = [((zed ^ k) * 2 + core, flat) for k in range(1, nz)]
    hops = {bit: (dp, flat ^ bit) for bit in moves.orders[0]}

    barrier = pltpu.get_barrier_semaphore()
    for device in [sibling] + others + list(hops.values()):
        pl.semaphore_signal(barrier, inc=1, device_id=device, device_id_type=pl.DeviceIdType.MESH)
    pl.semaphore_wait(barrier, 1 + len(others) + len(hops))

    remote = Copies(send_sems, recv_sems)
    local = []

    def local_start(source, target):
        one = pltpu.make_async_copy(source, target, local_sems.at[len(local)])
        one.start()
        local.append(one)
        return one

    def load(*pairs):
        for one in [local_start(source, target) for source, target in pairs]:
            one.wait()

    capacity = rows_first.shape[1]
    crossed_rows = [
        remote.start(other_second.at[1], grad_mixed.at[pl.ds(0, capacity)], sibling)
    ]
    crossed_late = [remote.start(other_second.at[0], landed, sibling)]
    row_loads = [
        local_start(source.at[1], grad_projected.at[pl.ds(0, capacity), pl.ds(e * wide, wide)])
        for e, source in enumerate((rows_first, rows_second, landed_first))
    ]
    loaded = local_start(projected, wide_low)
    phase_loads = [
        local_start(hidden, wide_f32),
        local_start(whole_attn, normed),
        local_start(grad_out, tokens),
    ]
    one_way = [moves.orders[n][0] for n in range(2)]
    other_way = [moves.orders[n][1] for n in range(2)]
    keep_first, arrived = (keep_first_in, keep_first_out), (arrived_in, arrived_out)
    first_hop = (first_hop_in, first_hop_out)

    keep, sent = (keep_in, keep_out), (sent_in, sent_out)
    got, hop = (got_in, got_out), (hop_in, hop_out)
    half_rows = [pl.ds(h * deep, deep) for h in range(2)]
    second_got = {}

    def second_start(h):
        for index in (1, 0):
            for n in range(2):
                second_got[n, index, h] = remote.start(
                    sent[n].at[index, :, half_rows[h]],
                    got[n].at[index, :, half_rows[h]],
                    hops[one_way[n]],
                )

    def sum_blocks(target, sources, h):
        pairs = []
        for n in range(2):
            for source, place in zip(sources[n], [target.at[n], spare.at[n, 0], spare.at[n, 1]]):
                pairs.append((source.at[:, half_rows[h]], place))
        load(*pairs)

        @pl.loop(0, nz)
        def _(k):
            for n in range(2):
                arrived = [spare[n, m, k] for m in range(len(sources[n]) - 1)]
                target[n, k] = sum_low(target[n, k], *arrived).astype(BF16)

    def z_send(source, landing):
        return [
            remote.start(source.at[n, k], landing.at[n, k - 1], others[k - 1])
            for k in range(1, nz)
            for n in range(2)
        ]

    second_start(0)
    sum_blocks(
        up_first,
        [(keep_first[n].at[0], arrived[n].at[0], first_hop[n]) for n in range(2)],
        1,
    )
    first_z = z_send(up_first, z_first)

    for one in row_loads + phase_loads:
        one.wait()
    wait_in(crossed_rows)

    def add_rows(target, source, columns):
        @pl.loop(0, capacity // TILE)
        def _(t):
            place = pl.ds(pl.multiple_of(t * TILE, TILE), TILE)
            total = sum_low(grad_projected[place, target], source[place, columns])
            grad_projected[place, target] = total.astype(BF16)

    first_columns, second_columns = pl.ds(0, wide), pl.ds(wide, wide)
    add_rows(first_columns, grad_projected, pl.ds(2 * wide, wide))
    add_rows(second_columns, grad_mixed, first_columns)

    def tokens_order(place):
        total = jnp.zeros((TILE, wide), F32)
        for e in range(EXPERTS):
            slot = lax.broadcasted_iota(jnp.int32, (TILE, capacity), 1) + e * capacity
            chosen = (slot == slot_col[place, 0:1]).astype(F32).astype(BF16)
            total = total + dot(chosen, grad_projected[pl.ds(0, capacity), pl.ds(e * wide, wide)])
        return total

    turned = params[...].astype(F32).T
    gain_one, gain_two = turned[0:1, :], turned[2:3, :]
    empty = jnp.zeros((1, wide), F32)

    def second_norm_tile(t, sums):
        place = pl.ds(pl.multiple_of(t * TILE, TILE), TILE)
        grad = tokens_order(place)
        scaled, inverse = norm_parts(wide_f32[place, :])
        total = tokens[place, :].astype(F32) + norm_back(grad, scaled, inverse, gain_two)
        wide_f32[place, :] = total
        low_total = total.astype(BF16)
        branch[place, :] = low_total
        grad_mixed[place, :] = dot_nt(low_total, normed[...]).astype(BF16)
        return (
            sums[0] + jnp.sum(grad * scaled, axis=0, keepdims=True),
            sums[1] + jnp.sum(grad, axis=0, keepdims=True),
        )

    sums_two = lax.fori_loop(0, rows // TILE, second_norm_tile, (empty, empty))
    reloads = [local_start(normed_out, normed), local_start(tokens_in, tokens)]
    saved = local_start(wide_f32, grad_tokens)

    def second_next(h):
        wait_in([second_got[n, 1, h] for n in range(2)])
        sum_blocks(up.at[h], [(keep[n].at[1], got[n].at[1]) for n in range(2)], h)
        return [
            remote.start(up.at[h, n], hop[n].at[:, half_rows[h]], hops[other_way[n]])
            for n in range(2)
        ]

    def second_z(h, hopped):
        wait_in([second_got[n, 0, h] for n in range(2)] + hopped)
        for one in hopped:
            one.wait_send()
        sum_blocks(
            up.at[h], [(keep[n].at[0], got[n].at[0], hop[n]) for n in range(2)], h
        )
        return z_send(up.at[h], z_second.at[h])

    second_hop = second_next(0)
    second_start(1)
    saved.wait()

    lane = lax.broadcasted_iota(jnp.int32, (1, BLOCK), 1)
    row = lax.broadcasted_iota(jnp.int32, (BLOCK, 1), 0)
    for i in range(rows // TILE):
        span = (i + 1) * TILE
        place = slice(i * TILE, span)
        query = lax.broadcasted_iota(jnp.int32, (span, TILE), 1) + i * TILE
        key = lax.broadcasted_iota(jnp.int32, (span, TILE), 0)
        same = seg_col[:span, 0:1] == seg_row[0:1, place]
        wide_f32[:span, place] = jnp.where(same & (key <= query), 0.0, MASKED)
    loaded.wait()
    pairs = wide // BLOCK

    def attend_pair(pair):
        columns = [
            pl.ds(pl.multiple_of(n * wide + pair * BLOCK, BLOCK), BLOCK) for n in range(3)
        ]
        key_sums[...] = jnp.zeros_like(key_sums)
        value_sums[...] = jnp.zeros_like(value_sums)
        keys_turned = wide_low[:, columns[1]].T
        for i in range(rows // TILE):
            span = (i + 1) * TILE
            place = slice(i * TILE, span)
            query = wide_low[place, columns[0]] * jnp.asarray(HEAD_DIM**-0.5, BF16)
            grad = grad_mixed[place, columns[0]]
            turned = jnp.zeros((BLOCK, TILE), F32)
            for side in range(2):
                ours = (lane // HEAD_DIM) == side
                part = jnp.where(ours, query, jnp.zeros_like(query))
                grad_part = jnp.where(ours, grad, jnp.zeros_like(grad))
                level = stats[pl.ds(2 * pair + side, 1), place]
                scores = dot_nt(wide_low[:span, columns[1]], part) + wide_f32[:span, place]
                attend = jnp.exp(scores - level)
                grad_attend = dot_nt(wide_low[:span, columns[2]], grad_part)
                inner = jnp.sum(attend * grad_attend, axis=0, keepdims=True)
                grad_scores = (attend * (grad_attend - inner)).astype(BF16)
                key_sums[:span, :] += dot(grad_scores, part)
                value_sums[:span, :] += dot(attend.astype(BF16), grad_part)
                turned = jnp.where(
                    (row // HEAD_DIM) == side, dot(keys_turned[:, :span], grad_scores), turned
                )
            grad_projected[place, columns[0]] = (turned.T * HEAD_DIM**-0.5).astype(BF16)
        grad_projected[:, columns[1]] = key_sums[...].astype(BF16)
        grad_projected[:, columns[2]] = value_sums[...].astype(BF16)

    def attend_pairs(start, stop):
        @pl.loop(start, stop)
        def _(pair):
            attend_pair(pair)

    def weight_grads(n):
        @pl.loop(0, nz)
        def _(z_of):
            span = 2 * nf * deep
            place = pl.ds(pl.multiple_of(z_of * span, span), span)
            turned = normed[:, place].T
            mixed_turned = mixed[:, place].T
            for part in range(4):
                if part < 3:
                    columns = pl.ds(part * wide + n * share, share)
                    made = dot(turned, grad_projected[:, columns])
                else:
                    made = dot(mixed_turned, branch[:, pl.ds(n * share, share)])
                made = made.astype(BF16).reshape(2, nf, deep, share)
                low[n, z_of, :, :, :, pl.ds(part * share, share)] = made

    def cross_start(source, target):
        return remote.start(source.at[:, 1 - core], target, sibling)

    def cross_add(source, target):
        @pl.loop(0, nz)
        def _(k):
            source[k, core] = sum_low(source[k, core], target[k]).astype(source.dtype)

    def hop_start(source, target, n):
        bits = one_way[n], other_way[n]
        return [
            remote.start(
                source.at[:, core, flat ^ bits[0] ^ (bits[1] * index)],
                target.at[index],
                hops[bits[0]],
            )
            for index in (1, 0)
        ]

    def hop_next(source, arrived, target, landing, n):
        @pl.loop(0, nz)
        def _(k):
            mine = source[k, core, flat ^ other_way[n]]
            target[k] = sum_low(mine, arrived[1, k]).astype(target.dtype)

        return remote.start(target, landing, hops[other_way[n]])

    def z_start(source, arrived, landing, z_landing):
        @pl.loop(0, nz)
        def _(k):
            total = sum_low(source[k, core, flat], arrived[0, k], landing[k])
            source[k, core, flat] = total.astype(source.dtype)

        return [
            remote.start(source.at[zed ^ k, core, flat], z_landing.at[k - 1], others[k - 1])
            for k in range(1, nz)
        ]

    def z_total(source, z_landing):
        return sum_low(source[zed, core, flat], *[z_landing[k] for k in range(nz - 1)])

    def finish_half(e, h, own, landing):
        for n in range(2):
            total = sum_low(own[n], *[landing[n, k] for k in range(nz - 1)])
            final[2 * e + n, half_rows[h]] = total

    def finish_expert(e, writes):
        cut = share_in.shape[2] // (2 * nz)
        for z_of in range(nz):
            place = pl.ds(pl.multiple_of((z_of * 2 + core) * cut, cut), cut)
            target = share_in.at[e, :, place]
            source = final.at[2 * e]
            there = source.at[pl.ds(pl.multiple_of((1 - core) * deep, deep), deep)]
            here = source.at[pl.ds(pl.multiple_of(core * deep, deep), deep)]
            writes.append(remote.start(there.at[:, pl.ds(z_of * cut, cut)], target, sibling))
            stored.append(local_start(here.at[:, pl.ds(z_of * cut, cut)], target))
        part = share_out.shape[1] // 2
        for index in range(2):
            stored.append(
                local_start(
                    final.at[2 * e + 1, :, pl.ds(index * wide, wide)],
                    share_out.at[e, pl.ds(index * part, part)],
                )
            )

    def put_share(n, total):
        for part in range(4):
            piece = total[:, part * share : (part + 1) * share]
            if part < 3:
                share_qkv[:, pl.ds(part * wide + n * share, share)] = piece
            else:
                share_attn[:, pl.ds(n * share, share)] = piece

    def norm_tile(t, sums):
        place = pl.ds(pl.multiple_of(t * TILE, TILE), TILE)
        grad = dot_nt(grad_projected[place, :], wide_low[...])
        scaled, inverse = norm_parts(tokens[place, :].astype(F32))
        wide_f32[place, :] += norm_back(grad, scaled, inverse, gain_one)
        return (
            sums[0] + jnp.sum(grad * scaled, axis=0, keepdims=True),
            sums[1] + jnp.sum(grad, axis=0, keepdims=True),
        )

    stored, writes = [], []
    step = pairs // PARTS
    crossed, hopped, went, turned_z = {}, {}, {}, {}

    def part_begin(n):
        attend_pairs(n * step, (n + 1) * step)
        if n == 0:
            for one in reloads:
                one.wait()
        weight_grads(n)
        crossed[n] = cross_start(low.at[n], cross.at[n])

    def part_hop(n):
        wait_in([crossed[n]])
        cross_add(low.at[n], cross.at[n])
        hopped[n] = hop_start(low.at[n], got_q.at[n], n % 2)

    def part_next(n):
        wait_in([hopped[n][0]])
        went[n] = hop_next(low.at[n], got_q.at[n], up_q.at[n], hop_q.at[n], n % 2)

    def part_z(n):
        wait_in([hopped[n][1], went[n]])
        turned_z[n] = z_start(low.at[n], got_q.at[n], hop_q.at[n], z_q.at[n])

    def part_end(n):
        wait_in(turned_z[n])
        put_share(n, z_total(low.at[n], z_q.at[n]))

    part_begin(0)
    second_zs = second_z(0, second_hop)
    part_begin(1)
    part_hop(0)
    second_hop_late = second_next(1)
    part_begin(2)
    part_hop(1)
    part_next(0)
    attend_pairs(3 * step, 4 * step)
    reload = local_start(whole_qkv, wide_low)
    restore = local_start(grad_tokens, wide_f32)
    weight_grads(3)
    crossed[3] = cross_start(low.at[3], cross.at[3])
    part_hop(2)
    part_next(1)
    part_z(0)
    part_hop(3)
    second_zs += second_z(1, second_hop_late)
    reload.wait()
    restore.wait()
    sums = lax.fori_loop(0, rows // TILE // 2, norm_tile, (empty, empty))
    part_next(2)
    part_z(1)
    part_next(3)
    sums = lax.fori_loop(rows // TILE // 2, rows // TILE, norm_tile, sums)
    result = local_start(wide_f32, grad_tokens)
    index = lax.broadcasted_iota(jnp.int32, (BLOCK, 1), 0)
    stacked = jnp.zeros((BLOCK, wide), F32)
    for n, one in enumerate(sums + sums_two):
        stacked = jnp.where(index == n, one, stacked)
    vec[...] = stacked.T.reshape(nz, 2, nf, deep, BLOCK)
    crossed_v = [cross_start(vec, cross_vec)]
    part_z(2)
    part_z(3)
    wait_in(crossed_v)
    cross_add(vec, cross_vec)
    hops_v = hop_start(vec, got_vec, 0)
    wait_in(first_z)
    load((first_own, spare.at[0, 0, pl.ds(0, 2)]), (first_landed, early))
    finish_half(0, 0, [spare[0, 0, n] for n in range(2)], early)
    finish_half(0, 1, [up_first[n, 0] for n in range(2)], z_first)
    finish_expert(0, writes)
    wait_in(hops_v)
    next_v = hop_next(vec, got_vec, hop_vec.at[1], hop_vec.at[0], 0)

    result.wait()
    wait_in(crossed_late)
    load(
        (hidden, wide_f32),
        *[
            (source.at[0], grad_projected.at[pl.ds(0, capacity), pl.ds(e * wide, wide)])
            for e, source in enumerate((rows_first, rows_second, landed_first))
        ],
        (landed, grad_mixed.at[pl.ds(0, capacity)]),
    )
    add_rows(first_columns, grad_projected, pl.ds(2 * wide, wide))
    add_rows(second_columns, grad_mixed, first_columns)

    @pl.loop(0, rows // TILE)
    def _(t):
        place = pl.ds(pl.multiple_of(t * TILE, TILE), TILE)
        branch[place, :] = (wide_f32[place, :] + tokens_order(place)).astype(BF16)

    stored.append(local_start(branch, block_out))
    wait_in([next_v])
    z_v = z_start(vec, got_vec, hop_vec.at[0], z_vec)
    for n in range(PARTS - 1):
        part_end(n)
    wait_in(second_zs)
    for h in range(2):
        finish_half(1, h, [up[h, n, 0] for n in range(2)], z_second.at[h])
    finish_expert(1, writes)
    part_end(PARTS - 1)
    wait_in(z_v)
    share_vectors[...] = z_total(vec, z_vec)
    wait_in(writes)
    for one in remote.made:
        if not any(one is other for other in second_hop + second_hop_late):
            one.wait_send()
    for one in stored:
        one.wait()


def backward_pass(moves, deep, big, row_parts, sums, stats, seg, slot_col, mixed, params):
    nz, nf = moves.nz, moves.nf
    rows, wide = mixed.shape
    share = wide // PARTS
    block = sums[0].shape[2:]
    half_block = (deep, block[1])
    capacity = row_parts[0].shape[1]
    anywhere = pl.BlockSpec(memory_space=pl.ANY)
    inside = pl.BlockSpec(memory_space=pltpu.VMEM)
    shape = jax.ShapeDtypeStruct
    landing = (2, nz) + block
    remote = 24 + 5 * PARTS + (PARTS + 7) * (nz - 1) + 2 * nz
    inputs = list(big) + list(row_parts) + list(sums)
    return pl.pallas_call(
        functools.partial(backward_kernel, moves, deep),
        in_specs=[anywhere] * len(inputs) + [inside] * 6,
        out_specs=[anywhere] * 4 + [inside] * 3 + [anywhere] * 5,
        out_shape=[
            shape((rows, wide), BF16),
            shape((rows, wide), F32),
            shape((EXPERTS, deep, 2 * block[1]), F32),
            shape((EXPERTS, block[0] * block[1] // wide, wide), F32),
            shape((deep, 3 * wide), F32),
            shape((deep, wide), F32),
            shape((deep, BLOCK), F32),
            shape(landing, BF16),
            shape(landing, BF16),
            shape(landing[1:], BF16),
            shape(landing[1:], BF16),
            shape((capacity, wide), BF16),
        ],
        scratch_shapes=[
            pltpu.VMEM((rows, 3 * wide), BF16),
            pltpu.VMEM((rows, rows), F32),
            pltpu.VMEM((rows, 3 * wide), BF16),
            pltpu.VMEM((rows, wide), BF16),
            pltpu.VMEM((rows, wide), BF16),
            pltpu.VMEM((rows, wide), BF16),
            pltpu.VMEM((rows, wide), BF16),
            pltpu.VMEM((rows, BLOCK), F32),
            pltpu.VMEM((rows, BLOCK), F32),
            pltpu.VMEM((PARTS, nz, 2, nf, deep, 4 * share), BF16),
            pltpu.VMEM((PARTS, nz, nf, deep, 4 * share), BF16),
            pltpu.VMEM((PARTS, 2, nz, deep, 4 * share), BF16),
            pltpu.VMEM((PARTS, nz, deep, 4 * share), BF16),
            pltpu.VMEM((PARTS, nz - 1, deep, 4 * share), BF16),
            pltpu.VMEM((PARTS, nz, deep, 4 * share), BF16),
            pltpu.VMEM((nz, 2, nf, deep, BLOCK), F32),
            pltpu.VMEM((nz, nf, deep, BLOCK), F32),
            pltpu.VMEM((2, nz, deep, BLOCK), F32),
            pltpu.VMEM((2, nz, deep, BLOCK), F32),
            pltpu.VMEM((nz - 1, deep, BLOCK), F32),
            pltpu.VMEM((2, 2, nz) + half_block, BF16),
            pltpu.VMEM((2, 2, nz) + half_block, BF16),
            pltpu.VMEM((2, nz) + half_block, BF16),
            pltpu.VMEM((2, nz - 1) + half_block, BF16),
            pltpu.VMEM((2, nz - 1) + half_block, BF16),
            pltpu.VMEM((2, 2, nz - 1) + half_block, BF16),
            pltpu.VMEM((4,) + block, F32),
            pltpu.SemaphoreType.DMA((remote,)),
            pltpu.SemaphoreType.DMA((remote,)),
            pltpu.SemaphoreType.DMA((60 + 2 * nz,)),
        ],
        compiler_params=pltpu.CompilerParams(
            collective_id=1, has_side_effects=True, vmem_limit_bytes=62 * MIB
        ),
        cost_estimate=pl.CostEstimate(
            flops=30 * rows * wide * wide, bytes_accessed=80 * wide * wide, transcendentals=0
        ),
        name="backward_pass",
    )(*inputs, stats, *seg, slot_col, mixed, params)


def gelu_both(value):
    square = value * value
    bent = jnp.tanh(ROOT_2_PI * value * (1.0 + CUBIC * square))
    half = 0.5 + 0.5 * bent
    slope = half + (0.5 * ROOT_2_PI) * value * (1.0 - bent * bent) * (1.0 + 3.0 * CUBIC * square)
    return (value * half, slope)


def expert_kernel(moves, mode, expert, deep, chunk, chunks, x_own, x_other, g_own, g_other, *refs):
    refs = list(refs)

    def take(count):
        taken, refs[:] = refs[:count], refs[count:]
        return taken

    if mode == "first":
        weights, columns_own = take(2), take(2)
    elif mode == "second":
        columns_own, pieces = take(2), take(2)
        first_grads, first_other = take(4), take(1)[0]
    else:
        weights = take(2)
    rows_own, rows_other = take(2)
    grads = take(2 if mode == "plain" else 4)
    if mode == "first":
        landing = take(2)
    elif mode == "second":
        got, hop, landed, own_z, landed_z = take(2), take(2), take(1)[0], *take(2)
    (win, wout, x, x_turned, g, branch, back, sum_in, sum_out, low_in, low_out) = take(11)
    w_sems, row_sems, out_sems = take(3)
    width = x.shape[1]
    rows = x.shape[0]
    capacity = rows // 2
    tiles = rows // TILE

    if mode != "plain":
        dp, flat = lax.axis_index("dp"), lax.axis_index("fsdp")
        zed, core = dp // 2, lax.rem(dp, 2)
        one_way = [moves.orders[n][0] for n in range(2)]
        other_way = [moves.orders[n][1] for n in range(2)]
        hops = {bit: (dp, flat ^ bit) for bit in moves.orders[0]}
        sibling = (zed * 2 + 1 - core, flat)
        devices = list(hops.values())
        if mode == "second":
            others = [((zed ^ k) * 2 + core, flat) for k in range(1, moves.nz)]
            devices += [sibling] + others
            up, spare, load_sems = take(3)
            half_rows = [pl.ds(h * deep, deep) for h in range(2)]
        barrier = pltpu.get_barrier_semaphore()
        for device in devices:
            pl.semaphore_signal(
                barrier, inc=1, device_id=device, device_id_type=pl.DeviceIdType.MESH
            )
        pl.semaphore_wait(barrier, len(devices))
        remote = Copies(*take(2))

    if mode == "first":
        near = [
            remote.start(columns_own[n], landing[n].at[other_way[n] - 1], hops[other_way[n]])
            for n in range(2)
        ]
        far = [
            remote.start(columns_own[n], landing[n].at[one_way[n] - 1], hops[one_way[n]])
            for n in range(2)
        ]
    elif mode == "second":
        hopped = {}

        def first_hop(h):
            for index in (1, 0):
                for n in range(2):
                    hopped[n, index, h] = remote.start(
                        first_grads[2 * n + 1].at[index, :, half_rows[h]],
                        got[n].at[index, :, half_rows[h]],
                        hops[one_way[n]],
                    )

        def half_sum(index, h, target):
            count = 2 if index else 3
            pairs = []
            for n in range(2):
                sources = [first_grads[2 * n].at[index], got[n].at[index], hop[n]][:count]
                places = [target.at[n], spare.at[n, 0], spare.at[n, 1]]
                for source, there in zip(sources, places):
                    pairs.append((source.at[:, half_rows[h]], there))
            begun = [
                pltpu.make_async_copy(source, there, load_sems.at[m])
                for m, (source, there) in enumerate(pairs)
            ]
            for one in begun:
                one.start()
            for one in begun:
                one.wait()

            @pl.loop(0, moves.nz)
            def _(k):
                for n in range(2):
                    arrived = [spare[n, m, k] for m in range(count - 1)]
                    target[n, k] = sum_low(target[n, k], *arrived).astype(BF16)

        def second_hop(h):
            wait_in([hopped[n, 1, h] for n in range(2)])
            half_sum(1, h, up.at[h])
            return [
                remote.start(up.at[h, n], hop[n].at[:, half_rows[h]], hops[other_way[n]])
                for n in range(2)
            ]

        first_hop(0)
        crossed = remote.start(first_other, landed, sibling)

    loads = []
    for n, (source, target) in enumerate(((x_own, x), (g_own, g), (x_other, x), (g_other, g))):
        place = pl.ds((n // 2) * capacity, capacity)
        loads.append(pltpu.make_async_copy(source.at[expert], target.at[place], row_sems.at[n]))
    copies = []
    if mode == "second":
        part_rows = chunk // moves.nf
        for offset in range(moves.nf):
            owner = flat ^ offset
            for k in range(moves.nz):
                sources = [
                    own.at[k] if offset == 0 else piece.at[offset - 1, k]
                    for own, piece in zip(columns_own, pieces)
                ]
                for part in range(2):
                    start = ((k * 2 + part) * moves.nf + owner) * deep
                    place = pl.ds(pl.multiple_of(start, deep), deep)
                    copies.append((sources[0].at[part], win.at[place]))
                start = (k * moves.nf + owner) * part_rows
                place = pl.ds(pl.multiple_of(start, part_rows), part_rows)
                copies.append((sources[1], wout.at[place]))
    else:
        copies = [(weights[0], win), (weights[1], wout)]
    loads += [
        pltpu.make_async_copy(source, target, w_sems.at[n])
        for n, (source, target) in enumerate(copies)
    ]
    for one in loads:
        one.start()
    branch[...] = jnp.zeros_like(branch)
    back[...] = jnp.zeros_like(back)
    for one in loads[:4]:
        one.wait()

    @pl.loop(0, tiles)
    def _(t):
        place = pl.ds(pl.multiple_of(t * TILE, TILE), TILE)
        x_turned[:, place] = x[place, :].T

    for one in loads[4:]:
        one.wait()

    def grad_copies(j):
        columns = pl.ds(pl.multiple_of(j * chunk, chunk), chunk)
        if mode == "plain":
            made = [(low_in, grads[0].at[:, columns]), (low_out, grads[1].at[columns])]
        else:
            made = []
            k_of = zed ^ j
            half_deep = chunk // moves.nf // 2
            for stream in range(2):
                offsets = moves.relative(stream)
                half = len(offsets) // 2
                for number, offset in enumerate(offsets):
                    target = grads[stream * 2 + number // half].at[number % half]
                    owner = flat ^ offset
                    for part in range(2):
                        if stream == 0:
                            for k in range(moves.nz):
                                start = (((zed ^ k) * 2 + part) * moves.nf + owner) * deep
                                place = pl.ds(pl.multiple_of(start, deep), deep)
                                there = target.at[k, pl.ds(part * deep, deep), columns]
                                made.append((low_in.at[place], there))
                        else:
                            start = (owner * 2 + part) * half_deep
                            place = pl.ds(pl.multiple_of(start, half_deep), half_deep)
                            there = target.at[k_of, :, pl.ds(part * width, width)]
                            made.append((low_out.at[place], there))
        return [
            pltpu.make_async_copy(source, target, out_sems.at[n])
            for n, (source, target) in enumerate(made)
        ]

    def chunk_step(j):
        columns = pl.ds(pl.multiple_of(j * chunk, chunk), chunk)
        sum_in[...] = jnp.zeros_like(sum_in)
        sum_out[...] = jnp.zeros_like(sum_out)

        @pl.loop(0, tiles)
        def _(t):
            place = pl.ds(pl.multiple_of(t * TILE, TILE), TILE)
            g_tile = g[place, :]
            inner = dot(x[place, :], win[:, columns])
            grad_active = dot_nt(g_tile, wout[columns, :])
            active, slope = gelu_both(inner)
            active_low = active.astype(BF16)
            grad_inner = (grad_active * slope).astype(BF16)
            branch[place, :] += dot(active_low, wout[columns, :])
            back[place, :] += dot_nt(grad_inner, win[:, columns])
            sum_in[...] += dot(x_turned[:, place], grad_inner)
            sum_out[...] += dot_tn(active_low, g_tile)

        @pl.when(j > 0)
        def _():
            for one in grad_copies(j - 1):
                one.wait()

        low_in[...] = sum_in[...].astype(BF16)
        low_out[...] = sum_out[...].astype(BF16)
        for one in grad_copies(j):
            one.start()

    def run_chunks(start, stop):
        @pl.loop(start, stop)
        def _(j):
            chunk_step(j)

    if mode == "plain":
        run_chunks(0, chunks)
    elif mode == "first":
        run_chunks(0, chunks // 2)
        wait_in(near)
        far += [
            remote.start(
                landing[n].at[other_way[n] - 1],
                landing[n].at[(one_way[n] ^ other_way[n]) - 1],
                hops[one_way[n]],
            )
            for n in range(2)
        ]
        run_chunks(chunks // 2, chunks)
    else:
        run_chunks(0, chunks // 4)
        last = second_hop(0)
        first_hop(1)
        run_chunks(chunks // 4, chunks // 2)
        wait_in([hopped[n, 0, 0] for n in range(2)] + last)
        half_sum(0, 0, up.at[2])
        z_sent = [
            remote.start(up.at[2, n, k], landed_z.at[n, k - 1], others[k - 1])
            for k in range(1, moves.nz)
            for n in range(2)
        ]
        own = pltpu.make_async_copy(up.at[2, :, 0], own_z, load_sems.at[0])
        own.start()
        own.wait()
        run_chunks(chunks // 2, chunks - 1)
        last = second_hop(1)
        run_chunks(chunks - 1, chunks)

    @pl.loop(0, tiles)
    def _(t):
        place = pl.ds(pl.multiple_of(t * TILE, TILE), TILE)
        x[place, :] = branch[place, :].astype(BF16)
        g[place, :] = back[place, :].astype(BF16)

    stored = []
    for n, (source, target) in enumerate(
        ((x, rows_own.at[0]), (g, rows_own.at[1]), (x, rows_other.at[0]), (g, rows_other.at[1]))
    ):
        place = pl.ds((n // 2) * capacity, capacity)
        stored.append(pltpu.make_async_copy(source.at[place], target, row_sems.at[n]))
    for one in stored:
        one.start()
    for one in grad_copies(chunks - 1) + stored:
        one.wait()
    if mode == "first":
        wait_in(far)
    elif mode == "second":
        wait_in([hopped[n, 0, 1] for n in range(2)] + last + z_sent + [crossed])
    if mode != "plain":
        for one in remote.made:
            one.wait_send()


def expert_block(moves, mode, expert, sorted_rows, extra, deep, half_hidden, grad_shapes, landing):
    capacity, width = sorted_rows[0].shape[1:]
    rows = 2 * capacity
    chunks = 4 if mode == "plain" else moves.nz
    chunk = half_hidden // chunks
    anywhere = pl.BlockSpec(memory_space=pl.ANY)
    row_shape = jax.ShapeDtypeStruct((2, capacity, width), BF16)
    outs = [row_shape] * 2 + grad_shapes + landing
    scratch = [
        pltpu.VMEM((width, half_hidden), BF16),
        pltpu.VMEM((half_hidden, width), BF16),
        pltpu.VMEM((rows, width), BF16),
        pltpu.VMEM((width, rows), BF16),
        pltpu.VMEM((rows, width), BF16),
        pltpu.VMEM((rows, width), F32),
        pltpu.VMEM((rows, width), F32),
        pltpu.VMEM((width, chunk), F32),
        pltpu.VMEM((chunk, width), F32),
        pltpu.VMEM((width, chunk), BF16),
        pltpu.VMEM((chunk, width), BF16),
    ]
    copies = 2 if mode == "plain" else 4 * moves.nz * moves.nf
    scratch += [
        pltpu.SemaphoreType.DMA((copies,)),
        pltpu.SemaphoreType.DMA((4,)),
        pltpu.SemaphoreType.DMA((copies,)),
    ]
    options = {}
    if mode == "second":
        block = (moves.nz, deep, half_hidden)
        scratch += [
            pltpu.VMEM((3, 2) + block, BF16),
            pltpu.VMEM((2, 2) + block, BF16),
            pltpu.SemaphoreType.DMA((6,)),
        ]
    if mode != "plain":
        count = 13 + 2 * (moves.nz - 1) if mode == "second" else 6
        scratch += [pltpu.SemaphoreType.DMA((count,))] * 2
        options = {"collective_id": 2 + expert, "has_side_effects": True}
    return pl.pallas_call(
        functools.partial(expert_kernel, moves, mode, expert, deep, chunk, chunks),
        in_specs=[anywhere] * (4 + len(extra)),
        out_specs=[anywhere] * len(outs),
        out_shape=outs,
        scratch_shapes=scratch,
        compiler_params=pltpu.CompilerParams(vmem_limit_bytes=58 * MIB, **options),
        cost_estimate=pl.CostEstimate(
            flops=12 * rows * width * half_hidden,
            bytes_accessed=8 * width * half_hidden + 16 * rows * width,
            transcendentals=rows * half_hidden,
        ),
        name="expert_" + mode,
    )(*sorted_rows, *extra)


def gather_experts_whole(w_expert_in, w_expert_out, core, nz):
    width, hidden = w_expert_out.shape[2], w_expert_in.shape[2]
    all_in = lax.all_gather(w_expert_in, AXES, axis=1, tiled=True)
    all_out = lax.all_gather(w_expert_out, AXES, axis=1, tiled=True)
    all_in = all_in.reshape(EXPERTS, width, nz, 2, hidden // (2 * nz))
    all_in = lax.dynamic_index_in_dim(all_in, core, 3, False)
    all_in = all_in.reshape(EXPERTS, width, hidden // 2)
    all_out = all_out.reshape(EXPERTS, nz, 2, hidden // (2 * nz), width)
    all_out = lax.dynamic_index_in_dim(all_out, core, 2, False)
    all_out = all_out.reshape(EXPERTS, hidden // 2, width)
    return [[all_in[e], all_out[e]] for e in range(EXPERTS)]


def local(
    nd,
    nf,
    tokens,
    seq_lengths,
    expert_ids,
    grad_out,
    ln1_gain,
    ln1_bias,
    w_qkv,
    w_attn_out,
    ln2_gain,
    ln2_bias,
    w_expert_in,
    w_expert_out,
):
    rows, width = tokens.shape
    deep = w_qkv.shape[0]
    moves = Moves(nd, nf)
    staged = deep % 32 == 0 and nf == 4 and moves.nz in (2, 4)
    core = lax.rem(lax.axis_index("dp"), 2)
    zed = lax.axis_index("dp") // 2
    flat = lax.axis_index("fsdp")

    positions = jnp.arange(rows, dtype=jnp.int32)
    bounds = jnp.cumsum(seq_lengths[0])
    segment = jnp.sum((positions[:, None] >= bounds[None, :]).astype(jnp.int32), axis=1)
    seg_row = jnp.broadcast_to(segment[None, :], (8, rows))
    seg_col = jnp.broadcast_to(segment[:, None], (rows, BLOCK))
    routed = expert_ids[:, 0]
    rank_second = jnp.cumsum(routed) - routed
    capacity = 3 * rows // 4
    slot = jnp.where(routed == 1, capacity + rank_second, positions - rank_second)

    params = jnp.stack([ln1_gain, ln1_bias, ln2_gain, ln2_bias], axis=1)
    params = jnp.pad(params, ((0, 0), (0, BLOCK - 4)))
    mine = jnp.concatenate([w_qkv, w_attn_out, params], axis=1)
    arguments = (tokens, grad_out, mine, w_expert_in, w_expert_out)
    if staged:
        return staged_block(moves, arguments, seg_row, seg_col, slot, (zed, core, flat))
    return plain_block(moves, arguments, seg_row, seg_col, slot, (zed, core, flat))


def staged_block(moves, arguments, seg_row, seg_col, slot, place):
    tokens, grad_out, mine, w_expert_in, w_expert_out = arguments
    rows, width = tokens.shape
    deep, hidden = w_expert_in.shape[1:]
    half_hidden = hidden // 2
    capacity = 3 * rows // 4
    zed, core, flat = place
    slot_row = jnp.broadcast_to(slot[None, :], (8, rows))
    slot_col = jnp.broadcast_to(slot[:, None], (rows, BLOCK))
    outs = forward_pass(
        moves, tokens, mine, w_expert_in, w_expert_out, seg_row, seg_col, slot_row, grad_out
    )
    whole_qkv, whole_attn, params, first_in = [one.reshape(-1, one.shape[-1]) for one in outs[:4]]
    first_out = outs[4].reshape(half_hidden, width)
    columns = list(outs[5:7])
    sorted_other, grad_other = outs[7:9]
    normed_one, projected, mixed, stats, hidden_one, sorted_rows, grad_sorted = outs[9:]
    by_expert = lambda value: value.reshape(EXPERTS, capacity, width)
    row_inputs = [by_expert(one) for one in (sorted_rows, sorted_other, grad_sorted, grad_other)]
    shape = lambda *dims: jax.ShapeDtypeStruct(dims, BF16)
    nz, nf = moves.nz, moves.nf
    block = (nz, 2 * deep, half_hidden)
    grad_shapes = [shape(nf // 2, *block)] * 4
    first = expert_block(
        moves,
        "first",
        0,
        row_inputs,
        [first_in, first_out] + columns,
        deep,
        half_hidden,
        grad_shapes,
        [shape(nf - 1, *one.shape) for one in columns],
    )
    second = expert_block(
        moves,
        "second",
        1,
        row_inputs,
        columns + list(first[6:8]) + list(first[2:6]) + [first[1]],
        deep,
        half_hidden,
        grad_shapes,
        [shape(2, *block)] * 2
        + [shape(*block)] * 2
        + [shape(2, capacity, width)]
        + [shape(2, deep, half_hidden), shape(2, nz - 1, deep, half_hidden)],
    )
    landed = second[10]
    results = backward_pass(
        moves,
        deep,
        [projected, whole_qkv, whole_attn, hidden_one, normed_one, tokens, grad_out],
        [first[0], second[0], landed, second[1]],
        [first[2], first[4]] + list(second[6:10]) + list(second[11:13]) + list(second[2:6]),
        stats.T,
        [seg_row, seg_col],
        slot_col,
        mixed,
        params,
    )
    block_result, grad_input, share_in, share_out, share_qkv, share_attn, vectors = results[:7]
    vectors = vectors[:, :4].T
    return (
        block_result,
        grad_input,
        vectors[0],
        vectors[1],
        share_qkv,
        share_attn,
        vectors[2],
        vectors[3],
        share_in,
        share_out,
    )


def plain_block(moves, arguments, seg_row, seg_col, slot, place):
    tokens, grad_out, mine, w_expert_in, w_expert_out = arguments
    rows, width = tokens.shape
    hidden = w_expert_in.shape[2]
    deep = mine.shape[0]
    nz = moves.nz
    zed, core, flat = place
    capacity = 3 * rows // 4
    whole = lax.all_gather(mine, AXES, axis=0, tiled=True)
    whole_qkv, whole_attn = whole[:, : 3 * width], whole[:, 3 * width : 4 * width]
    params = whole[:, 4 * width :]
    expert_weights = gather_experts_whole(w_expert_in, w_expert_out, core, nz)
    gain_one, bias_one, gain_two, bias_two = [
        params[:, n].astype(F32)[None, :] for n in range(4)
    ]
    tokens_wide = tokens.astype(F32)
    scaled_one, inverse_one = norm_parts(tokens_wide)
    normed_one = (scaled_one * gain_one + bias_one).astype(BF16)
    projected = dot(normed_one, whole_qkv).astype(BF16)
    mixed, stats = attention_forward(projected, seg_row, seg_col, 0, width // BLOCK)
    hidden_one = tokens_wide + dot(mixed, whole_attn)
    scaled_two, inverse_two = norm_parts(hidden_one)
    normed_two = (scaled_two * gain_two + bias_two).astype(BF16)
    slots = jnp.arange(EXPERTS * capacity, dtype=jnp.int32)[:, None]
    spread = (slots == slot[None, :]).astype(BF16)
    by_expert = lambda value: value.reshape(EXPERTS, capacity, width)
    row_inputs = []
    for value in (normed_two, grad_out):
        ordered = dot(spread, value).astype(BF16)
        row_inputs += [by_expert(ordered), by_expert(moves.core(ordered))]
    results, grad_pieces = [], []
    for e in range(EXPERTS):
        weights = expert_weights[e]
        shapes = [jax.ShapeDtypeStruct(one.shape, BF16) for one in weights]
        outs = expert_block(
            moves, "plain", e, row_inputs, weights, deep, hidden // 2, shapes, []
        )
        results.append(add_low(outs[0], moves.core(outs[1])))
        grad_pieces.append(outs[2:])
    both = jnp.concatenate(results, axis=1)
    grad_normed_two = dot_tn(spread, both[1])
    block_result = (hidden_one + dot_tn(spread, both[0])).astype(BF16)
    grad_hidden = grad_out.astype(F32) + norm_back(
        grad_normed_two, scaled_two, inverse_two, gain_two
    )
    grad_branch = grad_hidden.astype(BF16)
    grad_mixed = dot_nt(grad_branch, whole_attn).astype(BF16)
    trio = attention_backward(
        projected, grad_mixed, stats.T, seg_row, seg_col, 0, width // BLOCK
    )
    grad_projected = jnp.concatenate(trio, axis=1)
    grad_normed_one = dot_nt(grad_projected, whole_qkv)
    grad_input = grad_hidden + norm_back(grad_normed_one, scaled_one, inverse_one, gain_one)
    vectors = jnp.stack(
        [
            jnp.sum(grad_normed_one * scaled_one, axis=0),
            jnp.sum(grad_normed_one, axis=0),
            jnp.sum(grad_normed_two * scaled_two, axis=0),
            jnp.sum(grad_normed_two, axis=0),
        ]
    )
    own = lambda value, dim: lax.psum_scatter(value, AXES, scatter_dimension=dim, tiled=True)
    vectors = own(vectors, 1)
    full_in = jnp.stack([pieces[0] for pieces in grad_pieces])
    full_out = jnp.stack([pieces[1] for pieces in grad_pieces])
    full_in = full_in.reshape(EXPERTS, width, nz, 1, -1).astype(F32)
    full_out = full_out.reshape(EXPERTS, nz, 1, -1, width).astype(F32)
    chosen = jnp.arange(2) == core
    full_in = jnp.where(chosen[None, None, None, :, None], full_in, 0.0)
    full_out = jnp.where(chosen[None, None, :, None, None], full_out, 0.0)
    return (
        block_result,
        grad_input,
        vectors[0],
        vectors[1],
        own(dot_tn(normed_one, grad_projected), 0),
        own(dot_tn(mixed, grad_branch), 0),
        vectors[2],
        vectors[3],
        own(full_in.reshape(EXPERTS, width, hidden), 1),
        own(full_out.reshape(EXPERTS, hidden, width), 1),
    )


def solution(mesh):
    rows = P(AXES, None)
    vector = P(AXES)
    expert = P(None, AXES, None)
    return jax.shard_map(
        functools.partial(local, mesh.shape["dp"], mesh.shape["fsdp"]),
        mesh=mesh,
        in_specs=(
            rows, rows, rows, rows, vector, vector, rows, rows, vector, vector, expert, expert
        ),
        out_specs=(
            rows, rows, vector, vector, rows, rows, vector, vector, expert, expert
        ),
        check_vma=False,
    )
```

```python
import functools

import jax
import jax.numpy as jnp
from jax import lax
from jax.experimental import pallas as pl
from jax.experimental.pallas import tpu as pltpu
from jax.sharding import PartitionSpec as P

HEADS = 16
HEAD_DIM = 64
EXPERTS = 2
EPSILON = 1e-05
MASKED = -1000000000.0
AXES = ("dp", "fsdp")
BLOCK = 128
TILE = 256
MIB = 1024 * 1024
PARTS = 4
F32 = jnp.float32
BF16 = jnp.bfloat16
NT = (((1,), (1,)), ((), ()))
TN = (((0,), (0,)), ((), ()))
ROOT_2_PI = 0.7978845608028654
CUBIC = 0.044715


def dot(a, b):
    return jnp.dot(a, b, preferred_element_type=F32)


def dot_nt(a, b):
    return lax.dot_general(a, b, NT, preferred_element_type=F32)


def dot_tn(a, b):
    return lax.dot_general(a, b, TN, preferred_element_type=F32)


def norm_parts(values):
    average = jnp.mean(values, axis=-1, keepdims=True)
    centred = values - average
    variance = jnp.mean(centred * centred, axis=-1, keepdims=True)
    inverse = lax.rsqrt(variance + EPSILON)
    return (centred * inverse, inverse)


def norm_back(grad_normed, scaled, inverse, gain):
    grad_scaled = grad_normed * gain
    middle = jnp.mean(grad_scaled, axis=-1, keepdims=True)
    along = jnp.mean(grad_scaled * scaled, axis=-1, keepdims=True)
    return inverse * (grad_scaled - middle - scaled * along)


class Moves:
    def __init__(self, nd, nf):
        self.nz, self.nf = nd // 2, nf
        bits = []
        bit = 1
        while bit < nf:
            bits.append(bit)
            bit *= 2
        self.orders = (tuple(bits), tuple(reversed(bits)))

    def send(self, value, where):
        pairs = []
        for zed in range(self.nz):
            for core in range(2):
                for flat in range(self.nf):
                    z_to, core_to, f_to = where(zed, core, flat)
                    pairs.append(
                        (
                            (zed * 2 + core) * self.nf + flat,
                            (z_to * 2 + core_to) * self.nf + f_to,
                        )
                    )
        return lax.ppermute(value, AXES, pairs)

    def core(self, value):
        return self.send(value, lambda z, c, f: (z, 1 - c, f))

    def flat(self, value, bit):
        return self.send(value, lambda z, c, f: (z, c, f ^ bit))

    def along(self, value, steps):
        return self.send(value, lambda z, c, f: ((z + steps) % self.nz, c, f))

    def near(self, value, bit):
        return self.send(value, lambda z, c, f: (z ^ bit, c, f))

    def relative(self, stream):
        offsets = [0]
        for bit in reversed(self.orders[stream]):
            offsets = offsets + [one ^ bit for one in offsets]
        return tuple(offsets)

    def gather_z(self, value):
        return [value] + [self.along(value, k) for k in range(1, self.nz)]

    def gather_z_pair(self, value):
        held, bit = value[:, None], 1
        while 2 * bit < self.nz:
            held = jnp.concatenate([held, self.near(held, bit)], axis=1)
            bit *= 2
        got = self.near(held, bit)
        return [jnp.concatenate([held[n], got[n]], axis=0) for n in range(2)], got

    def gather_first(self, value, stream):
        held = value[None]
        for bit in tuple(reversed(self.orders[stream]))[:-1]:
            held = jnp.concatenate([held, self.flat(held, bit)], axis=0)
        return held

    def gather_last(self, held, stream):
        return self.flat(held, self.orders[stream][0])

    def reduce_flat(self, keep, sent, stream):
        order = self.orders[stream]
        now = add_low(keep, self.flat(sent, order[0]))
        for bit in order[1:]:
            half = now.shape[0] // 2
            now = add_low(now[:half], self.flat(now[half:], bit))
        return now[0]

    def reduce_z(self, value):
        total = value[0].astype(F32)
        for k in range(1, self.nz):
            total = total + self.along(value[k], k).astype(F32)
        return total

    def reduce_z_pair(self, value):
        bit = self.nz // 2
        while bit > 1:
            value = add_low(value[:bit], self.near(value[bit:], bit))
            bit //= 2
        return value[0].astype(F32) + self.near(value[1], 1).astype(F32)


def after(value, *others):
    return lax.optimization_barrier((value,) + others)[0]


def add_low(a, b):
    return (a.astype(F32) + b.astype(F32)).astype(BF16)


def attention_forward_kernel(seg_row, seg_col, q, k, v, out, stats, bias):
    rows = q.shape[0]
    pair = pl.program_id(0)
    lane = lax.broadcasted_iota(jnp.int32, (1, BLOCK), 1)

    @pl.when(pair == 0)
    def _():
        stats[...] = jnp.zeros_like(stats)
        for i in range(rows // TILE):
            span = (i + 1) * TILE
            place = slice(i * TILE, span)
            query = lax.broadcasted_iota(jnp.int32, (TILE, span), 0) + i * TILE
            key = lax.broadcasted_iota(jnp.int32, (TILE, span), 1)
            same = seg_col[place, 0:1] == seg_row[0:1, :span]
            bias[place, :span] = jnp.where(same & (key <= query), 0.0, MASKED)

    for i in range(rows // TILE):
        span = (i + 1) * TILE
        place = slice(i * TILE, span)
        query = q[place, :] * jnp.asarray(HEAD_DIM**-0.5, BF16)
        mixed = jnp.zeros((TILE, BLOCK), F32)
        held = stats[place, :]
        for side in range(2):
            mine = (lane // HEAD_DIM) == side
            part = jnp.where(mine, query, jnp.zeros_like(query))
            scores = dot_nt(part, k[:span, :]) + bias[place, :span]
            highest = jnp.max(scores, axis=1, keepdims=True)
            terms = jnp.exp(scores - highest)
            total = jnp.sum(terms, axis=1, keepdims=True)
            attend = (terms * (1.0 / total)).astype(BF16)
            mixed = jnp.where(mine, dot(attend, v[:span, :]), mixed)
            held = jnp.where(lane == 2 * pair + side, highest + jnp.log(total), held)
        stats[place, :] = held
        out[place, :] = mixed.astype(BF16)


def attention_forward(projected, seg_row, seg_col, first, count):
    rows, width = projected.shape[0], projected.shape[1] // 3
    pairs = width // BLOCK
    column = lambda start: pl.BlockSpec((rows, BLOCK), lambda h: (0, start + h))
    whole = lambda shape: pl.BlockSpec(shape, lambda h: (0, 0))
    return pl.pallas_call(
        attention_forward_kernel,
        grid=(count,),
        in_specs=[
            whole((8, rows)),
            whole((rows, BLOCK)),
            column(first),
            column(first + pairs),
            column(first + 2 * pairs),
        ],
        out_specs=[column(0), whole((rows, BLOCK))],
        out_shape=[
            jax.ShapeDtypeStruct((rows, count * BLOCK), BF16),
            jax.ShapeDtypeStruct((rows, BLOCK), F32),
        ],
        scratch_shapes=[pltpu.VMEM((rows, rows), F32)],
        compiler_params=pltpu.CompilerParams(vmem_limit_bytes=40 * MIB),
        cost_estimate=pl.CostEstimate(
            flops=4 * rows * rows * count * BLOCK,
            bytes_accessed=8 * rows * count * BLOCK,
            transcendentals=2 * count * rows * rows,
        ),
        name="attention_forward",
    )(seg_row, seg_col, projected, projected, projected)


def attention_backward_kernel(first, seg_row, seg_col, stats, q, k, v, g, dq, dk, dv, bias, dks, dvs):
    rows = q.shape[0]
    pair = pl.program_id(0)
    lane = lax.broadcasted_iota(jnp.int32, (1, BLOCK), 1)
    row = lax.broadcasted_iota(jnp.int32, (BLOCK, 1), 0)

    @pl.when(pair == 0)
    def _():
        for i in range(rows // TILE):
            span = (i + 1) * TILE
            place = slice(i * TILE, span)
            query = lax.broadcasted_iota(jnp.int32, (span, TILE), 1) + i * TILE
            key = lax.broadcasted_iota(jnp.int32, (span, TILE), 0)
            same = seg_col[:span, 0:1] == seg_row[0:1, place]
            bias[:span, place] = jnp.where(same & (key <= query), 0.0, MASKED)

    dks[...] = jnp.zeros_like(dks)
    dvs[...] = jnp.zeros_like(dvs)
    k_turned = k[...].T
    for i in range(rows // TILE):
        span = (i + 1) * TILE
        place = slice(i * TILE, span)
        query = q[place, :] * jnp.asarray(HEAD_DIM**-0.5, BF16)
        grad = g[place, :]
        turned = jnp.zeros((BLOCK, TILE), F32)
        for side in range(2):
            mine = (lane // HEAD_DIM) == side
            part = jnp.where(mine, query, jnp.zeros_like(query))
            grad_part = jnp.where(mine, grad, jnp.zeros_like(grad))
            level = stats[pl.ds(2 * (first + pair) + side, 1), place]
            scores = dot_nt(k[:span, :], part) + bias[:span, place]
            attend = jnp.exp(scores - level)
            grad_attend = dot_nt(v[:span, :], grad_part)
            inner = jnp.sum(attend * grad_attend, axis=0, keepdims=True)
            grad_scores = (attend * (grad_attend - inner)).astype(BF16)
            dks[:span, :] += dot(grad_scores, part)
            dvs[:span, :] += dot(attend.astype(BF16), grad_part)
            turned = jnp.where(
                (row // HEAD_DIM) == side, dot(k_turned[:, :span], grad_scores), turned
            )
        dq[place, :] = (turned.T * HEAD_DIM**-0.5).astype(BF16)
    dk[...] = dks[...].astype(BF16)
    dv[...] = dvs[...].astype(BF16)


def attention_backward(projected, grad_mixed, stats, seg_row, seg_col, first, count):
    rows, width = projected.shape[0], projected.shape[1] // 3
    pairs = width // BLOCK
    column = lambda start: pl.BlockSpec((rows, BLOCK), lambda h: (0, start + h))
    whole = lambda shape: pl.BlockSpec(shape, lambda h: (0, 0))
    share = jax.ShapeDtypeStruct((rows, count * BLOCK), BF16)
    return pl.pallas_call(
        functools.partial(attention_backward_kernel, first),
        grid=(count,),
        in_specs=[
            whole((8, rows)),
            whole((rows, BLOCK)),
            whole((BLOCK, rows)),
            column(first),
            column(first + pairs),
            column(first + 2 * pairs),
            column(first),
        ],
        out_specs=[column(0), column(0), column(0)],
        out_shape=[share, share, share],
        scratch_shapes=[
            pltpu.VMEM((rows, rows), F32),
            pltpu.VMEM((rows, BLOCK), F32),
            pltpu.VMEM((rows, BLOCK), F32),
        ],
        compiler_params=pltpu.CompilerParams(vmem_limit_bytes=40 * MIB),
        cost_estimate=pl.CostEstimate(
            flops=10 * rows * rows * count * BLOCK,
            bytes_accessed=14 * rows * count * BLOCK,
            transcendentals=2 * count * rows * rows,
        ),
        name="attention_backward",
    )(seg_row, seg_col, stats, projected, projected, projected, grad_mixed)


class Copies:
    def __init__(self, send_sems, recv_sems):
        self.send_sems, self.recv_sems, self.made = send_sems, recv_sems, []

    def start(self, source, target, device):
        n = len(self.made)
        one = pltpu.make_async_remote_copy(
            src_ref=source,
            dst_ref=target,
            send_sem=self.send_sems.at[n],
            recv_sem=self.recv_sems.at[n],
            device_id=device,
            device_id_type=pl.DeviceIdType.MESH,
        )
        one.start()
        self.made.append(one)
        return one


def wait_in(copies):
    for one in copies:
        one.wait_recv()


def forward_kernel(
    moves,
    tokens,
    mine,
    own_in,
    own_out,
    seg_row,
    seg_col,
    slot_row,
    grad_out,
    out_qkv,
    out_attn,
    out_params,
    first_in,
    first_out,
    column_in,
    column_out,
    sorted_other,
    grad_other,
    turned_normed,
    projected,
    turned_mixed,
    stats,
    hidden,
    sorted_rows,
    grad_sorted,
    weights,
    bias,
    normed,
    mixed,
    normed_two,
    send_sems,
    recv_sems,
    local_sems,
):
    nz, nf = moves.nz, moves.nf
    dp, flat = lax.axis_index("dp"), lax.axis_index("fsdp")
    zed, core = dp // 2, lax.rem(dp, 2)
    rows, wide = tokens.shape
    sibling = (zed * 2 + 1 - core, flat)
    next_z, across_z = [((zed ^ k) * 2 + core, flat) for k in (1, 2)]
    others = [next_z, across_z]
    hops = {bit: (dp, flat ^ bit) for bit in moves.orders[0]}

    barrier = pltpu.get_barrier_semaphore()
    for device in [sibling] + others + list(hops.values()):
        pl.semaphore_signal(barrier, inc=1, device_id=device, device_id_type=pl.DeviceIdType.MESH)
    pl.semaphore_wait(barrier, 1 + len(others) + len(hops))

    remote = Copies(send_sems, recv_sems)
    local = []

    def local_start(source, target):
        one = pltpu.make_async_copy(source, target, local_sems.at[len(local)])
        one.start()
        local.append(one)
        return one

    own = local_start(mine, weights.at[zed, core, flat])
    stream_columns = (slice(0, 2 * wide), slice(2 * wide, 4 * wide + BLOCK))

    def column_start(source, place):
        return [remote.start(source, place(zed), device) for device in (across_z, next_z)]

    def column_next(column, place):
        wait_in(column[:1])
        column.append(remote.start(place(zed ^ 2), place(zed ^ 2), next_z))

    def column_wait(column):
        wait_in(column[1:])

    def weight_place(stream):
        return lambda z_of: weights.at[z_of, core, flat, :, stream_columns[stream]]

    def weight_column(stream):
        return column_start(mine.at[:, stream_columns[stream]], weight_place(stream))

    columns_a = weight_column(0)
    targets = (first_in.at[zed, core, flat], column_in.at[zed, core])
    cut = own_in.shape[2] // (2 * nz)
    crossed, blocks = [], []
    for e in range(EXPERTS):
        for z_of in range(nz):
            target = targets[e].at[:, pl.ds(z_of * cut, cut)]
            theirs, ours = [
                own_in.at[e, :, pl.ds(pl.multiple_of((2 * z_of + which) * cut, cut), cut)]
                for which in (1 - core, core)
            ]
            crossed.append(remote.start(theirs, target, sibling))
            blocks.append(local_start(ours, target))
    blocks.append(local_start(own_out.at[0], first_out.at[zed, flat]))
    blocks.append(local_start(own_out.at[1], column_out.at[zed]))

    capacity = sorted_rows.shape[0] // EXPERTS

    def sort_rows(source, target, first):
        @pl.loop(0, target.shape[0] // TILE)
        def _(t):
            place = pl.ds(pl.multiple_of(t * TILE, TILE), TILE)
            slot = lax.broadcasted_iota(jnp.int32, (TILE, rows), 0) + t * TILE + first
            chosen = (slot == slot_row[0:1, :]).astype(F32).astype(BF16)
            target[place, :] = dot(chosen, source[...]).astype(BF16)

    sort_rows(grad_out, grad_sorted, 0)
    for i in range(rows // TILE):
        span = (i + 1) * TILE
        place = slice(i * TILE, span)
        query = lax.broadcasted_iota(jnp.int32, (TILE, span), 0) + i * TILE
        key = lax.broadcasted_iota(jnp.int32, (TILE, span), 1)
        same = seg_col[place, 0:1] == seg_row[0:1, :span]
        bias[place, :span] = jnp.where(same & (key <= query), 0.0, MASKED)
    stats[...] = jnp.zeros_like(stats)

    def send_weights(stream, owner, device):
        place = weights.at[:, core, owner, :, stream_columns[stream]]
        return remote.start(place, place, device)

    near = [tuple(reversed(moves.orders[n]))[0] for n in range(2)]
    far = [moves.orders[n][0] for n in range(2)]
    hop_near, hop_far, across = [], [], []
    own.wait()
    column_next(columns_a, weight_place(0))
    columns_b = weight_column(1)
    column_wait(columns_a)
    hop_near.append(send_weights(0, flat, hops[near[0]]))
    hop_far.append(send_weights(0, flat, hops[far[0]]))
    across.append(send_weights(0, flat, sibling))

    first_places = (
        lambda z_of: first_in.at[z_of, :, flat],
        lambda z_of: first_out.at[z_of, flat],
    )
    wait_in(crossed)
    for one in blocks:
        one.wait()
    column_next(columns_b, weight_place(1))
    first_a = column_start(first_in.at[zed, :, flat], first_places[0])
    column_wait(columns_b)
    hop_near.append(send_weights(1, flat, hops[near[1]]))
    hop_far.append(send_weights(1, flat, hops[far[1]]))
    across.append(send_weights(1, flat, sibling))
    column_next(first_a, first_places[0])
    first_b = column_start(own_out.at[0], first_places[1])
    wait_in(hop_near)
    hop_last = [send_weights(n, flat ^ near[n], hops[far[n]]) for n in range(2)]
    across += [send_weights(n, flat ^ near[n], sibling) for n in range(2)]
    exchanged = [remote.start(grad_sorted, grad_other, sibling)]

    def send_first(stream, owner, device):
        place = first_in.at[:, :, owner] if stream == 0 else first_out.at[:, owner]
        return remote.start(place, place, device)

    column_wait(first_a)
    first_near = [send_first(0, flat, hops[near[0]])]
    first_far = [send_first(0, flat, hops[far[0]])]
    column_next(first_b, first_places[1])
    wait_in(hop_far)
    across += [send_weights(n, flat ^ far[n], sibling) for n in range(2)]
    wait_in(hop_last)
    across += [send_weights(n, flat ^ near[n] ^ far[n], sibling) for n in range(2)]

    wait_in(across)
    whole = 2 * nz * nf * mine.shape[0]
    writes = [
        local_start(weights.at[:, :, :, :, pl.ds(0, 3 * wide)], out_qkv),
        local_start(weights.at[:, :, :, :, pl.ds(3 * wide, wide)], out_attn),
        local_start(weights.at[:, :, :, :, pl.ds(4 * wide, BLOCK)], out_params),
    ]
    turned = weights[:, :, :, :, pl.ds(4 * wide, BLOCK)].reshape(whole, BLOCK).astype(F32).T
    gain, shift = turned[0:1, :], turned[1:2, :]

    @pl.loop(0, rows // TILE)
    def _(t):
        place = pl.ds(pl.multiple_of(t * TILE, TILE), TILE)
        scaled, _ = norm_parts(tokens[place, :].astype(F32))
        normed[place, :] = (scaled * gain + shift).astype(BF16)
        for part in range(3):
            columns = pl.ds(part * wide, wide)
            matrix = weights[:, :, :, :, columns].reshape(whole, wide)
            projected[place, columns] = dot(normed[place, :], matrix).astype(BF16)

    lane = lax.broadcasted_iota(jnp.int32, (1, BLOCK), 1)
    pairs = wide // BLOCK

    def attend_pair(pair):
        columns = [
            pl.ds(pl.multiple_of(n * wide + pair * BLOCK, BLOCK), BLOCK) for n in range(3)
        ]
        for i in range(rows // TILE):
            span = (i + 1) * TILE
            place = slice(i * TILE, span)
            query = projected[place, columns[0]] * jnp.asarray(HEAD_DIM**-0.5, BF16)
            result = jnp.zeros((TILE, BLOCK), F32)
            held = stats[place, :]
            for side in range(2):
                ours = (lane // HEAD_DIM) == side
                part = jnp.where(ours, query, jnp.zeros_like(query))
                scores = dot_nt(part, projected[:span, columns[1]]) + bias[place, :span]
                highest = jnp.max(scores, axis=1, keepdims=True)
                terms = jnp.exp(scores - highest)
                total = jnp.sum(terms, axis=1, keepdims=True)
                attend = (terms * (1.0 / total)).astype(BF16)
                result = jnp.where(ours, dot(attend, projected[:span, columns[2]]), result)
                held = jnp.where(lane == 2 * pair + side, highest + jnp.log(total), held)
            stats[place, :] = held
            mixed[place, columns[0]] = result.astype(BF16)

    def attend_pairs(start, stop):
        @pl.loop(start, stop)
        def _(pair):
            attend_pair(pair)

    attend_pairs(0, pairs // 4)
    column_wait(first_b)
    first_near.append(send_first(1, flat, hops[near[1]]))
    first_far.append(send_first(1, flat, hops[far[1]]))

    second_places = (lambda z_of: column_in.at[z_of], lambda z_of: column_out.at[z_of])
    second_a = column_start(column_in.at[zed], second_places[0])

    attend_pairs(pairs // 4, pairs // 2)
    wait_in([first_near[0]])
    first_last = [send_first(0, flat ^ near[0], hops[far[0]])]
    column_next(second_a, second_places[0])
    second_b = column_start(own_out.at[1], second_places[1])
    attend_pairs(pairs // 2, 3 * pairs // 4)
    wait_in([first_near[1]])
    first_last.append(send_first(1, flat ^ near[1], hops[far[1]]))
    column_next(second_b, second_places[1])
    attend_pairs(3 * pairs // 4, pairs)

    gain_two, shift_two = turned[2:3, :], turned[3:4, :]

    @pl.loop(0, rows // TILE)
    def _(t):
        place = pl.ds(pl.multiple_of(t * TILE, TILE), TILE)
        matrix = weights[:, :, :, :, pl.ds(3 * wide, wide)].reshape(whole, wide)
        total = tokens[place, :].astype(F32) + dot(mixed[place, :], matrix)
        hidden[place, :] = total
        scaled, _ = norm_parts(total)
        normed_two[place, :] = (scaled * gain_two + shift_two).astype(BF16)

    sort_rows(normed_two, sorted_rows.at[pl.ds(0, capacity)], 0)
    place = pl.ds(0, capacity)
    exchanged.append(remote.start(sorted_rows.at[place], sorted_other.at[place], sibling))
    sort_rows(normed_two, sorted_rows.at[pl.ds(capacity, capacity)], capacity)
    place = pl.ds(capacity, capacity)
    exchanged.append(remote.start(sorted_rows.at[place], sorted_other.at[place], sibling))
    turned_normed[...] = normed[...].T
    turned_mixed[...] = mixed[...].T
    wait_in(first_far)
    wait_in(first_last)
    column_wait(second_a)
    column_wait(second_b)
    wait_in(exchanged)
    for one in remote.made:
        one.wait_send()
    for one in writes:
        one.wait()


def forward_pass(moves, tokens, mine, own_in, own_out, seg_row, seg_col, slot_row, grad_out):
    nz, nf = moves.nz, moves.nf
    rows, wide = tokens.shape
    deep, half = own_in.shape[1], own_in.shape[2] // 2
    part = own_out.shape[1]
    capacity = 3 * rows // 4
    anywhere = pl.BlockSpec(memory_space=pl.ANY)
    inside = pl.BlockSpec(memory_space=pltpu.VMEM)
    shape = jax.ShapeDtypeStruct
    remote = 6 * (nz - 1) + 2 * nz + 26
    return pl.pallas_call(
        functools.partial(forward_kernel, moves),
        in_specs=[inside] * 8,
        out_specs=[anywhere] * 9 + [inside] * 7,
        out_shape=[
            shape((nz, 2, nf, deep, 3 * wide), BF16),
            shape((nz, 2, nf, deep, wide), BF16),
            shape((nz, 2, nf, deep, BLOCK), BF16),
            shape((nz, 2, nf, deep, half), BF16),
            shape((nz, nf, part, wide), BF16),
            shape((nz, 2, deep, half), BF16),
            shape((nz, part, wide), BF16),
            shape((EXPERTS * capacity, wide), BF16),
            shape((EXPERTS * capacity, wide), BF16),
            shape((wide, rows), BF16),
            shape((rows, 3 * wide), BF16),
            shape((wide, rows), BF16),
            shape((rows, BLOCK), F32),
            shape((rows, wide), F32),
            shape((EXPERTS * capacity, wide), BF16),
            shape((EXPERTS * capacity, wide), BF16),
        ],
        scratch_shapes=[
            pltpu.VMEM((nz, 2, nf, deep, 4 * wide + BLOCK), BF16),
            pltpu.VMEM((rows, rows), F32),
            pltpu.VMEM((rows, wide), BF16),
            pltpu.VMEM((rows, wide), BF16),
            pltpu.VMEM((rows, wide), BF16),
            pltpu.SemaphoreType.DMA((remote,)),
            pltpu.SemaphoreType.DMA((remote,)),
            pltpu.SemaphoreType.DMA((2 * nz + 6,)),
        ],
        compiler_params=pltpu.CompilerParams(
            collective_id=0, has_side_effects=True, vmem_limit_bytes=60 * MIB
        ),
        cost_estimate=pl.CostEstimate(
            flops=10 * rows * wide * wide, bytes_accessed=80 * wide * wide, transcendentals=0
        ),
        name="forward_pass",
    )(tokens, mine, own_in, own_out, seg_row, seg_col, slot_row, grad_out)


def sum_low(*values):
    total = values[0].astype(F32)
    for one in values[1:]:
        total = total + one.astype(F32)
    return total


def backward_kernel(
    moves,
    deep,
    projected,
    whole_qkv,
    whole_attn,
    hidden,
    normed_out,
    tokens_in,
    grad_out,
    rows_first,
    rows_second,
    landed_first,
    other_second,
    keep_first_in,
    keep_first_out,
    arrived_in,
    arrived_out,
    first_hop_in,
    first_hop_out,
    first_own,
    first_landed,
    keep_in,
    sent_in,
    keep_out,
    sent_out,
    stats,
    seg_row,
    marks,
    mixed,
    params,
    block_out,
    grad_tokens,
    share_in,
    share_out,
    share_qkv,
    share_attn,
    share_vectors,
    got_in,
    got_out,
    hop_in,
    hop_out,
    landed,
    wide_low,
    wide_f32,
    grad_projected,
    grad_mixed,
    branch,
    normed,
    tokens,
    key_sums,
    value_sums,
    low,
    cross,
    got_q,
    hop_q,
    z_q,
    up_q,
    vec,
    cross_vec,
    got_vec,
    hop_vec,
    z_vec,
    up,
    spare,
    up_first,
    z_first,
    z_second,
    final,
    send_sems,
    recv_sems,
    local_sems,
):
    nz, nf = moves.nz, moves.nf
    dp, flat = lax.axis_index("dp"), lax.axis_index("fsdp")
    zed, core = dp // 2, lax.rem(dp, 2)
    rows, wide = tokens.shape
    share = wide // PARTS
    sibling = (zed * 2 + 1 - core, flat)
    next_z, across_z = [((zed ^ k) * 2 + core, flat) for k in (1, 2)]
    others = [next_z, across_z]
    hops = {bit: (dp, flat ^ bit) for bit in moves.orders[0]}

    barrier = pltpu.get_barrier_semaphore()
    for device in [sibling] + others + list(hops.values()):
        pl.semaphore_signal(barrier, inc=1, device_id=device, device_id_type=pl.DeviceIdType.MESH)
    pl.semaphore_wait(barrier, 1 + len(others) + len(hops))

    remote = Copies(send_sems, recv_sems)
    local = []

    def local_start(source, target):
        one = pltpu.make_async_copy(source, target, local_sems.at[len(local)])
        one.start()
        local.append(one)
        return one

    def load(*pairs):
        for one in [local_start(source, target) for source, target in pairs]:
            one.wait()

    capacity = rows_first.shape[1]
    crossed_rows = [
        remote.start(other_second.at[1], grad_mixed.at[pl.ds(0, capacity)], sibling)
    ]
    crossed_late = [remote.start(other_second.at[0], landed, sibling)]
    row_loads = [
        local_start(source.at[1], grad_projected.at[pl.ds(0, capacity), pl.ds(e * wide, wide)])
        for e, source in enumerate((rows_first, rows_second, landed_first))
    ]
    loaded = local_start(projected, wide_low)
    phase_loads = [
        local_start(hidden, wide_f32),
        local_start(whole_attn, normed),
        local_start(grad_out, tokens),
    ]
    one_way = [moves.orders[n][0] for n in range(2)]
    other_way = [moves.orders[n][1] for n in range(2)]
    keep_first, arrived = (keep_first_in, keep_first_out), (arrived_in, arrived_out)
    first_hop = (first_hop_in, first_hop_out)

    keep, sent = (keep_in, keep_out), (sent_in, sent_out)
    got, hop = (got_in, got_out), (hop_in, hop_out)
    half_rows = [pl.ds(h * deep, deep) for h in range(2)]
    second_got = {}

    def second_start(h):
        for index in (1, 0):
            for n in range(2):
                second_got[n, index, h] = remote.start(
                    sent[n].at[index, :, half_rows[h]],
                    got[n].at[index, :, half_rows[h]],
                    hops[one_way[n]],
                )

    def sum_blocks(target, sources, h):
        pairs = []
        for n in range(2):
            for source, place in zip(sources[n], [target.at[n], spare.at[n, 0], spare.at[n, 1]]):
                pairs.append((source.at[:, half_rows[h]], place))
        load(*pairs)

        @pl.loop(0, nz)
        def _(k):
            for n in range(2):
                arrived = [spare[n, m, k] for m in range(len(sources[n]) - 1)]
                target[n, k] = sum_low(target[n, k], *arrived).astype(BF16)

    def z_first_step(source, landing):
        return [
            remote.start(source.at[n, k], landing.at[n, k // 2], next_z)
            for k in (3, 1)
            for n in range(2)
        ]

    def z_second_step(source, landing, begun):
        wait_in(begun[:2])
        for n in range(2):
            source[n, 2] = sum_low(source[n, 2], landing[n, 1]).astype(BF16)
            begun.append(remote.start(source.at[n, 2], landing.at[n, 2], across_z))
        return begun

    second_start(0)
    sum_blocks(
        up_first,
        [(keep_first[n].at[0], arrived[n].at[0], first_hop[n]) for n in range(2)],
        1,
    )
    first_z = z_first_step(up_first, z_first)

    for one in row_loads + phase_loads:
        one.wait()
    wait_in(crossed_rows)

    def add_rows(target, source, columns):
        @pl.loop(0, capacity // TILE)
        def _(t):
            place = pl.ds(pl.multiple_of(t * TILE, TILE), TILE)
            total = sum_low(grad_projected[place, target], source[place, columns])
            grad_projected[place, target] = total.astype(BF16)

    first_columns, second_columns = pl.ds(0, wide), pl.ds(wide, wide)
    add_rows(first_columns, grad_projected, pl.ds(2 * wide, wide))
    add_rows(second_columns, grad_mixed, first_columns)

    def tokens_order(place):
        total = jnp.zeros((TILE, wide), F32)
        for e in range(EXPERTS):
            slot = lax.broadcasted_iota(jnp.int32, (TILE, capacity), 1) + e * capacity
            chosen = (slot == marks[place, 1:2]).astype(F32).astype(BF16)
            total = total + dot(chosen, grad_projected[pl.ds(0, capacity), pl.ds(e * wide, wide)])
        return total

    turned = params[...].astype(F32).T
    gain_one, gain_two = turned[0:1, :], turned[2:3, :]
    empty = jnp.zeros((1, wide), F32)

    def second_norm_tile(t, sums):
        place = pl.ds(pl.multiple_of(t * TILE, TILE), TILE)
        grad = tokens_order(place)
        scaled, inverse = norm_parts(wide_f32[place, :])
        total = tokens[place, :].astype(F32) + norm_back(grad, scaled, inverse, gain_two)
        wide_f32[place, :] = total
        low_total = total.astype(BF16)
        branch[place, :] = low_total
        grad_mixed[place, :] = dot_nt(low_total, normed[...]).astype(BF16)
        return (
            sums[0] + jnp.sum(grad * scaled, axis=0, keepdims=True),
            sums[1] + jnp.sum(grad, axis=0, keepdims=True),
        )

    sums_two = lax.fori_loop(0, rows // TILE, second_norm_tile, (empty, empty))
    reloads = [local_start(normed_out, normed), local_start(tokens_in, tokens)]
    saved = local_start(wide_f32, grad_tokens)

    def second_next(h):
        wait_in([second_got[n, 1, h] for n in range(2)])
        sum_blocks(up.at[h], [(keep[n].at[1], got[n].at[1]) for n in range(2)], h)
        return [
            remote.start(up.at[h, n], hop[n].at[:, half_rows[h]], hops[other_way[n]])
            for n in range(2)
        ]

    def second_z(h, hopped):
        wait_in([second_got[n, 0, h] for n in range(2)] + hopped)
        for one in hopped:
            one.wait_send()
        sum_blocks(
            up.at[h], [(keep[n].at[0], got[n].at[0], hop[n]) for n in range(2)], h
        )
        return z_first_step(up.at[h], z_second.at[h])

    second_hop = second_next(0)
    second_start(1)
    first_z = z_second_step(up_first, z_first, first_z)
    saved.wait()

    lane = lax.broadcasted_iota(jnp.int32, (1, BLOCK), 1)
    row = lax.broadcasted_iota(jnp.int32, (BLOCK, 1), 0)
    for i in range(rows // TILE):
        span = (i + 1) * TILE
        place = slice(i * TILE, span)
        query = lax.broadcasted_iota(jnp.int32, (span, TILE), 1) + i * TILE
        key = lax.broadcasted_iota(jnp.int32, (span, TILE), 0)
        same = marks[:span, 0:1] == seg_row[0:1, place]
        wide_f32[:span, place] = jnp.where(same & (key <= query), 0.0, MASKED)
    loaded.wait()
    pairs = wide // BLOCK

    def attend_pair(pair):
        columns = [
            pl.ds(pl.multiple_of(n * wide + pair * BLOCK, BLOCK), BLOCK) for n in range(3)
        ]
        key_sums[...] = jnp.zeros_like(key_sums)
        value_sums[...] = jnp.zeros_like(value_sums)
        keys_turned = wide_low[:, columns[1]].T
        for i in range(rows // TILE):
            span = (i + 1) * TILE
            place = slice(i * TILE, span)
            query = wide_low[place, columns[0]] * jnp.asarray(HEAD_DIM**-0.5, BF16)
            grad = grad_mixed[place, columns[0]]
            turned = jnp.zeros((BLOCK, TILE), F32)
            for side in range(2):
                ours = (lane // HEAD_DIM) == side
                part = jnp.where(ours, query, jnp.zeros_like(query))
                grad_part = jnp.where(ours, grad, jnp.zeros_like(grad))
                level = stats[pl.ds(2 * pair + side, 1), place]
                scores = dot_nt(wide_low[:span, columns[1]], part) + wide_f32[:span, place]
                attend = jnp.exp(scores - level)
                grad_attend = dot_nt(wide_low[:span, columns[2]], grad_part)
                inner = jnp.sum(attend * grad_attend, axis=0, keepdims=True)
                grad_scores = (attend * (grad_attend - inner)).astype(BF16)
                key_sums[:span, :] += dot(grad_scores, part)
                value_sums[:span, :] += dot(attend.astype(BF16), grad_part)
                turned = jnp.where(
                    (row // HEAD_DIM) == side, dot(keys_turned[:, :span], grad_scores), turned
                )
            grad_projected[place, columns[0]] = (turned.T * HEAD_DIM**-0.5).astype(BF16)
        grad_projected[:, columns[1]] = key_sums[...].astype(BF16)
        grad_projected[:, columns[2]] = value_sums[...].astype(BF16)

    def attend_pairs(start, stop):
        @pl.loop(start, stop)
        def _(pair):
            attend_pair(pair)

    def weight_grads(n):
        @pl.loop(0, nz)
        def _(z_of):
            span = 2 * nf * deep
            place = pl.ds(pl.multiple_of(z_of * span, span), span)
            turned = normed[place, :]
            mixed_turned = mixed[place, :]
            for part in range(4):
                if part < 3:
                    columns = pl.ds(part * wide + n * share, share)
                    made = dot(turned, grad_projected[:, columns])
                else:
                    made = dot(mixed_turned, branch[:, pl.ds(n * share, share)])
                made = made.astype(BF16).reshape(2, nf, deep, share)
                low[n, z_of, :, :, :, pl.ds(part * share, share)] = made

    def cross_start(source, target):
        return remote.start(source.at[:, 1 - core], target, sibling)

    def cross_add(source, target):
        @pl.loop(0, nz)
        def _(k):
            source[k, core] = sum_low(source[k, core], target[k]).astype(source.dtype)

    def hop_start(source, target, n):
        bits = one_way[n], other_way[n]
        return [
            remote.start(
                source.at[:, core, flat ^ bits[0] ^ (bits[1] * index)],
                target.at[index],
                hops[bits[0]],
            )
            for index in (1, 0)
        ]

    def hop_next(source, arrived, target, landing, n):
        @pl.loop(0, nz)
        def _(k):
            mine = source[k, core, flat ^ other_way[n]]
            target[k] = sum_low(mine, arrived[1, k]).astype(target.dtype)

        return remote.start(target, landing, hops[other_way[n]])

    def z_start(source, arrived, landing, z_landing):
        @pl.loop(0, nz)
        def _(k):
            total = sum_low(source[k, core, flat], arrived[0, k], landing[k])
            source[k, core, flat] = total.astype(source.dtype)

        return [
            remote.start(source.at[zed ^ k, core, flat], z_landing.at[k // 2], next_z)
            for k in (3, 1)
        ]

    def z_next(source, z_landing, begun):
        wait_in(begun[:1])
        total = sum_low(source[zed ^ 2, core, flat], z_landing[1])
        source[zed ^ 2, core, flat] = total.astype(source.dtype)
        begun.append(remote.start(source.at[zed ^ 2, core, flat], z_landing.at[2], across_z))

    def z_total(source, z_landing):
        return sum_low(source[zed, core, flat], z_landing[0], z_landing[2])

    def finish_half(e, h, own, landing):
        for n in range(2):
            total = sum_low(own[n], landing[n, 0], landing[n, 2])
            final[2 * e + n, half_rows[h]] = total

    def finish_expert(e, writes):
        cut = share_in.shape[2] // (2 * nz)
        for z_of in range(nz):
            place = pl.ds(pl.multiple_of((z_of * 2 + core) * cut, cut), cut)
            target = share_in.at[e, :, place]
            source = final.at[2 * e]
            there = source.at[pl.ds(pl.multiple_of((1 - core) * deep, deep), deep)]
            here = source.at[pl.ds(pl.multiple_of(core * deep, deep), deep)]
            writes.append(remote.start(there.at[:, pl.ds(z_of * cut, cut)], target, sibling))
            stored.append(local_start(here.at[:, pl.ds(z_of * cut, cut)], target))
        part = share_out.shape[1] // 2
        for index in range(2):
            stored.append(
                local_start(
                    final.at[2 * e + 1, :, pl.ds(index * wide, wide)],
                    share_out.at[e, pl.ds(index * part, part)],
                )
            )

    def put_share(n, total):
        for part in range(4):
            piece = total[:, part * share : (part + 1) * share]
            if part < 3:
                share_qkv[:, pl.ds(part * wide + n * share, share)] = piece
            else:
                share_attn[:, pl.ds(n * share, share)] = piece

    def norm_tile(t, sums):
        place = pl.ds(pl.multiple_of(t * TILE, TILE), TILE)
        grad = dot_nt(grad_projected[place, :], wide_low[...])
        scaled, inverse = norm_parts(tokens[place, :].astype(F32))
        wide_f32[place, :] += norm_back(grad, scaled, inverse, gain_one)
        return (
            sums[0] + jnp.sum(grad * scaled, axis=0, keepdims=True),
            sums[1] + jnp.sum(grad, axis=0, keepdims=True),
        )

    stored, writes = [], []
    step = pairs // PARTS
    crossed, hopped, went, turned_z = {}, {}, {}, {}

    def part_attend(n):
        attend_pairs(n * step, (n + 1) * step)

    def part_begin(n):
        weight_grads(n)
        crossed[n] = cross_start(low.at[n], cross.at[n])

    def part_hop(n):
        wait_in([crossed[n]])
        cross_add(low.at[n], cross.at[n])
        hopped[n] = hop_start(low.at[n], got_q.at[n], n % 2)

    def part_next(n):
        wait_in([hopped[n][0]])
        went[n] = hop_next(low.at[n], got_q.at[n], up_q.at[n], hop_q.at[n], n % 2)

    def part_z(n):
        wait_in([hopped[n][1], went[n]])
        turned_z[n] = z_start(low.at[n], got_q.at[n], hop_q.at[n], z_q.at[n])

    def part_z_next(n):
        z_next(low.at[n], z_q.at[n], turned_z[n])

    def part_end(n):
        wait_in(turned_z[n][1:])
        put_share(n, z_total(low.at[n], z_q.at[n]))

    part_attend(0)
    for one in reloads:
        one.wait()
    part_begin(0)
    second_z_0 = second_z(0, second_hop)
    part_attend(1)
    part_hop(0)
    part_begin(1)
    z_second_step(up.at[0], z_second.at[0], second_z_0)
    second_hop_late = second_next(1)
    part_attend(2)
    part_hop(1)
    part_next(0)
    part_begin(2)
    second_z_1 = second_z(1, second_hop_late)
    part_attend(3)
    reload = local_start(whole_qkv, wide_low)
    restore = local_start(grad_tokens, wide_f32)
    part_hop(2)
    part_next(1)
    part_z(0)
    part_begin(3)
    z_second_step(up.at[1], z_second.at[1], second_z_1)
    reload.wait()
    restore.wait()
    sums = lax.fori_loop(0, 1, norm_tile, (empty, empty))
    part_hop(3)
    part_next(2)
    sums = lax.fori_loop(1, 3, norm_tile, sums)
    part_z(1)
    part_z_next(0)
    part_next(3)
    sums = lax.fori_loop(3, rows // TILE, norm_tile, sums)
    result = local_start(wide_f32, grad_tokens)
    index = lax.broadcasted_iota(jnp.int32, (BLOCK, 1), 0)
    stacked = jnp.zeros((BLOCK, wide), F32)
    for n, one in enumerate(sums + sums_two):
        stacked = jnp.where(index == n, one, stacked)
    vec[...] = stacked.T.reshape(nz, 2, nf, deep, BLOCK)
    crossed_v = [cross_start(vec, cross_vec)]
    wait_in(first_z[2:])
    load(
        (first_own, spare.at[0, 0, pl.ds(0, 2)]),
        *[(first_landed.at[n], spare.at[n, 1, pl.ds(0, nz - 1)]) for n in range(2)],
    )
    finish_half(0, 0, [spare[0, 0, n] for n in range(2)], spare.at[:, 1])
    finish_half(0, 1, [up_first[n, 0] for n in range(2)], z_first)
    finish_expert(0, writes)
    wait_in(crossed_v)
    cross_add(vec, cross_vec)
    hops_v = hop_start(vec, got_vec, 0)
    part_z(2)
    part_z_next(1)

    result.wait()
    wait_in(crossed_late)
    late = [
        local_start(source, target)
        for source, target in [(hidden, wide_f32), (landed, grad_mixed.at[pl.ds(0, capacity)])]
        + [
            (source.at[0], grad_projected.at[pl.ds(0, capacity), pl.ds(e * wide, wide)])
            for e, source in enumerate((rows_first, rows_second, landed_first))
        ]
    ]
    part_z(3)
    part_z_next(2)
    wait_in(hops_v)
    next_v = hop_next(vec, got_vec, hop_vec.at[1], hop_vec.at[0], 0)
    for one in late:
        one.wait()
    add_rows(first_columns, grad_projected, pl.ds(2 * wide, wide))
    add_rows(second_columns, grad_mixed, first_columns)
    wait_in([next_v])
    z_v = z_start(vec, got_vec, hop_vec.at[0], z_vec)
    part_z_next(3)

    def output_tiles(start, stop):
        @pl.loop(start, stop)
        def _(t):
            place = pl.ds(pl.multiple_of(t * TILE, TILE), TILE)
            branch[place, :] = (wide_f32[place, :] + tokens_order(place)).astype(BF16)

    output_tiles(0, rows // TILE // 2)
    z_next(vec, z_vec, z_v)
    for n in range(PARTS - 1):
        part_end(n)
    output_tiles(rows // TILE // 2, rows // TILE)
    stored.append(local_start(branch, block_out))
    wait_in(second_z_0[2:] + second_z_1[2:])
    for h in range(2):
        finish_half(1, h, [up[h, n, 0] for n in range(2)], z_second.at[h])
    finish_expert(1, writes)
    part_end(PARTS - 1)
    wait_in(z_v[1:])
    share_vectors[...] = z_total(vec, z_vec)
    wait_in(writes)
    for one in remote.made:
        if not any(one is other for other in second_hop + second_hop_late):
            one.wait_send()
    for one in stored:
        one.wait()


def backward_pass(moves, deep, big, row_parts, sums, stats, seg_row, marks, mixed, params):
    nz, nf = moves.nz, moves.nf
    rows, wide = mixed.shape
    share = wide // PARTS
    block = sums[0].shape[2:]
    half_block = (deep, block[1])
    capacity = row_parts[0].shape[1]
    anywhere = pl.BlockSpec(memory_space=pl.ANY)
    inside = pl.BlockSpec(memory_space=pltpu.VMEM)
    shape = jax.ShapeDtypeStruct
    landing = (2, nz) + block
    remote = 24 + 5 * PARTS + (PARTS + 7) * (nz - 1) + 2 * nz
    inputs = list(big) + list(row_parts) + list(sums)
    return pl.pallas_call(
        functools.partial(backward_kernel, moves, deep),
        in_specs=[anywhere] * len(inputs) + [inside] * 5,
        out_specs=[anywhere] * 4 + [inside] * 3 + [anywhere] * 5,
        out_shape=[
            shape((rows, wide), BF16),
            shape((rows, wide), F32),
            shape((EXPERTS, deep, 2 * block[1]), F32),
            shape((EXPERTS, block[0] * block[1] // wide, wide), F32),
            shape((deep, 3 * wide), F32),
            shape((deep, wide), F32),
            shape((deep, BLOCK), F32),
            shape(landing, BF16),
            shape(landing, BF16),
            shape(landing[1:], BF16),
            shape(landing[1:], BF16),
            shape((capacity, wide), BF16),
        ],
        scratch_shapes=[
            pltpu.VMEM((rows, 3 * wide), BF16),
            pltpu.VMEM((rows, rows), F32),
            pltpu.VMEM((rows, 3 * wide), BF16),
            pltpu.VMEM((rows, wide), BF16),
            pltpu.VMEM((rows, wide), BF16),
            pltpu.VMEM((rows, wide), BF16),
            pltpu.VMEM((rows, wide), BF16),
            pltpu.VMEM((rows, BLOCK), F32),
            pltpu.VMEM((rows, BLOCK), F32),
            pltpu.VMEM((PARTS, nz, 2, nf, deep, 4 * share), BF16),
            pltpu.VMEM((PARTS, nz, nf, deep, 4 * share), BF16),
            pltpu.VMEM((PARTS, 2, nz, deep, 4 * share), BF16),
            pltpu.VMEM((PARTS, nz, deep, 4 * share), BF16),
            pltpu.VMEM((PARTS, nz - 1, deep, 4 * share), BF16),
            pltpu.VMEM((PARTS, nz, deep, 4 * share), BF16),
            pltpu.VMEM((nz, 2, nf, deep, BLOCK), F32),
            pltpu.VMEM((nz, nf, deep, BLOCK), F32),
            pltpu.VMEM((2, nz, deep, BLOCK), F32),
            pltpu.VMEM((2, nz, deep, BLOCK), F32),
            pltpu.VMEM((nz - 1, deep, BLOCK), F32),
            pltpu.VMEM((2, 2, nz) + half_block, BF16),
            pltpu.VMEM((2, 2, nz) + half_block, BF16),
            pltpu.VMEM((2, nz) + half_block, BF16),
            pltpu.VMEM((2, nz - 1) + half_block, BF16),
            pltpu.VMEM((2, 2, nz - 1) + half_block, BF16),
            pltpu.VMEM((4,) + block, F32),
            pltpu.SemaphoreType.DMA((remote,)),
            pltpu.SemaphoreType.DMA((remote,)),
            pltpu.SemaphoreType.DMA((60 + 2 * nz,)),
        ],
        compiler_params=pltpu.CompilerParams(
            collective_id=1, has_side_effects=True, vmem_limit_bytes=63 * MIB
        ),
        cost_estimate=pl.CostEstimate(
            flops=30 * rows * wide * wide, bytes_accessed=80 * wide * wide, transcendentals=0
        ),
        name="backward_pass",
    )(*inputs, stats, seg_row, marks, mixed, params)


def gelu_both(value):
    square = value * value
    bent = jnp.tanh(ROOT_2_PI * value * (1.0 + CUBIC * square))
    half = 0.5 + 0.5 * bent
    slope = half + (0.5 * ROOT_2_PI) * value * (1.0 - bent * bent) * (1.0 + 3.0 * CUBIC * square)
    return (value * half, slope)


def expert_kernel(moves, mode, expert, deep, chunk, chunks, x_own, x_other, g_own, g_other, *refs):
    refs = list(refs)

    def take(count):
        taken, refs[:] = refs[:count], refs[count:]
        return taken

    if mode == "first":
        weights, columns_own = take(2), take(2)
    elif mode == "second":
        columns_own, pieces = take(2), take(2)
        first_grads, first_other = take(4), take(1)[0]
    else:
        weights = take(2)
    rows_own, rows_other = take(2)
    grads = take(2 if mode == "plain" else 4)
    if mode == "first":
        landing = take(2)
    elif mode == "second":
        got, hop, landed, own_z, landed_z = take(2), take(2), take(1)[0], *take(2)
    (win, wout, x, x_turned, g, branch, back, sum_in, sum_out, low_in, low_out) = take(11)
    w_sems, row_sems, out_sems = take(3)
    width = x.shape[1]
    rows = x.shape[0]
    capacity = rows // 2
    tiles = rows // TILE

    if mode != "plain":
        dp, flat = lax.axis_index("dp"), lax.axis_index("fsdp")
        zed, core = dp // 2, lax.rem(dp, 2)
        one_way = [moves.orders[n][0] for n in range(2)]
        other_way = [moves.orders[n][1] for n in range(2)]
        hops = {bit: (dp, flat ^ bit) for bit in moves.orders[0]}
        sibling = (zed * 2 + 1 - core, flat)
        devices = list(hops.values())
        if mode == "second":
            others = [((zed ^ k) * 2 + core, flat) for k in (1, 2)]
            devices += [sibling] + others
            up, spare, load_sems = take(3)
            half_rows = [pl.ds(h * deep, deep) for h in range(2)]
        barrier = pltpu.get_barrier_semaphore()
        for device in devices:
            pl.semaphore_signal(
                barrier, inc=1, device_id=device, device_id_type=pl.DeviceIdType.MESH
            )
        pl.semaphore_wait(barrier, len(devices))
        remote = Copies(*take(2))

    if mode == "first":
        near = [
            remote.start(columns_own[n], landing[n].at[other_way[n] - 1], hops[other_way[n]])
            for n in range(2)
        ]
        far = [
            remote.start(columns_own[n], landing[n].at[one_way[n] - 1], hops[one_way[n]])
            for n in range(2)
        ]
    elif mode == "second":
        hopped = {}

        def first_hop(h):
            for index in (1, 0):
                for n in range(2):
                    hopped[n, index, h] = remote.start(
                        first_grads[2 * n + 1].at[index, :, half_rows[h]],
                        got[n].at[index, :, half_rows[h]],
                        hops[one_way[n]],
                    )

        def half_sum(index, h, target):
            count = 2 if index else 3
            pairs = []
            for n in range(2):
                sources = [first_grads[2 * n].at[index], got[n].at[index], hop[n]][:count]
                places = [target.at[n], spare.at[n, 0], spare.at[n, 1]]
                for source, there in zip(sources, places):
                    pairs.append((source.at[:, half_rows[h]], there))
            begun = [
                pltpu.make_async_copy(source, there, load_sems.at[m])
                for m, (source, there) in enumerate(pairs)
            ]
            for one in begun:
                one.start()
            for one in begun:
                one.wait()

            @pl.loop(0, moves.nz)
            def _(k):
                for n in range(2):
                    arrived = [spare[n, m, k] for m in range(count - 1)]
                    target[n, k] = sum_low(target[n, k], *arrived).astype(BF16)

        def second_hop(h):
            wait_in([hopped[n, 1, h] for n in range(2)])
            half_sum(1, h, up.at[h])
            return [
                remote.start(up.at[h, n], hop[n].at[:, half_rows[h]], hops[other_way[n]])
                for n in range(2)
            ]

        first_hop(0)
        crossed = remote.start(first_other, landed, sibling)

    loads = []
    for n, (source, target) in enumerate(((x_own, x), (g_own, g), (x_other, x), (g_other, g))):
        place = pl.ds((n // 2) * capacity, capacity)
        loads.append(pltpu.make_async_copy(source.at[expert], target.at[place], row_sems.at[n]))
    copies = []
    if mode == "second":
        part_rows = chunk // moves.nf
        for offset in range(moves.nf):
            owner = flat ^ offset
            for k in range(moves.nz):
                sources = [
                    own.at[k] if offset == 0 else piece.at[offset - 1, k]
                    for own, piece in zip(columns_own, pieces)
                ]
                for part in range(2):
                    start = ((k * 2 + part) * moves.nf + owner) * deep
                    place = pl.ds(pl.multiple_of(start, deep), deep)
                    copies.append((sources[0].at[part], win.at[place]))
                start = (k * moves.nf + owner) * part_rows
                place = pl.ds(pl.multiple_of(start, part_rows), part_rows)
                copies.append((sources[1], wout.at[place]))
    else:
        copies = [(weights[0], win), (weights[1], wout)]
    loads += [
        pltpu.make_async_copy(source, target, w_sems.at[n])
        for n, (source, target) in enumerate(copies)
    ]
    for one in loads:
        one.start()
    branch[...] = jnp.zeros_like(branch)
    back[...] = jnp.zeros_like(back)
    for one in loads[:4]:
        one.wait()

    @pl.loop(0, tiles)
    def _(t):
        place = pl.ds(pl.multiple_of(t * TILE, TILE), TILE)
        x_turned[:, place] = x[place, :].T

    for one in loads[4:]:
        one.wait()

    def grad_copies(j):
        columns = pl.ds(pl.multiple_of(j * chunk, chunk), chunk)
        if mode == "plain":
            made = [(low_in, grads[0].at[:, columns]), (low_out, grads[1].at[columns])]
        else:
            made = []
            k_of = zed ^ j
            half_deep = chunk // moves.nf // 2
            for stream in range(2):
                offsets = moves.relative(stream)
                half = len(offsets) // 2
                for number, offset in enumerate(offsets):
                    target = grads[stream * 2 + number // half].at[number % half]
                    owner = flat ^ offset
                    for part in range(2):
                        if stream == 0:
                            for k in range(moves.nz):
                                start = (((zed ^ k) * 2 + part) * moves.nf + owner) * deep
                                place = pl.ds(pl.multiple_of(start, deep), deep)
                                there = target.at[k, pl.ds(part * deep, deep), columns]
                                made.append((low_in.at[place], there))
                        else:
                            start = (owner * 2 + part) * half_deep
                            place = pl.ds(pl.multiple_of(start, half_deep), half_deep)
                            there = target.at[k_of, :, pl.ds(part * width, width)]
                            made.append((low_out.at[place], there))
        return [
            pltpu.make_async_copy(source, target, out_sems.at[n])
            for n, (source, target) in enumerate(made)
        ]

    def chunk_step(j):
        columns = pl.ds(pl.multiple_of(j * chunk, chunk), chunk)
        sum_in[...] = jnp.zeros_like(sum_in)
        sum_out[...] = jnp.zeros_like(sum_out)

        @pl.loop(0, tiles)
        def _(t):
            place = pl.ds(pl.multiple_of(t * TILE, TILE), TILE)
            g_tile = g[place, :]
            inner = dot(x[place, :], win[:, columns])
            grad_active = dot_nt(g_tile, wout[columns, :])
            active, slope = gelu_both(inner)
            active_low = active.astype(BF16)
            grad_inner = (grad_active * slope).astype(BF16)
            branch[place, :] += dot(active_low, wout[columns, :])
            back[place, :] += dot_nt(grad_inner, win[:, columns])
            sum_in[...] += dot(x_turned[:, place], grad_inner)
            sum_out[...] += dot_tn(active_low, g_tile)

        @pl.when(j > 0)
        def _():
            for one in grad_copies(j - 1):
                one.wait()

        low_in[...] = sum_in[...].astype(BF16)
        low_out[...] = sum_out[...].astype(BF16)
        for one in grad_copies(j):
            one.start()

    def run_chunks(start, stop):
        @pl.loop(start, stop)
        def _(j):
            chunk_step(j)

    if mode == "plain":
        run_chunks(0, chunks)
    elif mode == "first":
        run_chunks(0, chunks // 2)
        wait_in(near)
        far += [
            remote.start(
                landing[n].at[other_way[n] - 1],
                landing[n].at[(one_way[n] ^ other_way[n]) - 1],
                hops[one_way[n]],
            )
            for n in range(2)
        ]
        run_chunks(chunks // 2, chunks)
    else:
        run_chunks(0, chunks // 4)
        last = second_hop(0)
        first_hop(1)
        run_chunks(chunks // 4, chunks // 2)
        wait_in([hopped[n, 0, 0] for n in range(2)] + last)
        half_sum(0, 0, up.at[2])
        z_sent = [
            remote.start(up.at[2, n, k], landed_z.at[n, k // 2], others[0])
            for k in (3, 1)
            for n in range(2)
        ]
        own = pltpu.make_async_copy(up.at[2, :, 0], own_z, load_sems.at[0])
        own.start()
        own.wait()
        run_chunks(chunks // 2, chunks - 1)
        last = second_hop(1)
        wait_in(z_sent[:2])
        begun = [
            pltpu.make_async_copy(landed_z.at[n, 1], spare.at[n, 0, 0], load_sems.at[n])
            for n in range(2)
        ]
        for one in begun:
            one.start()
        for one in begun:
            one.wait()
        for n in range(2):
            up[2, n, 2] = sum_low(up[2, n, 2], spare[n, 0, 0]).astype(BF16)
            z_sent.append(remote.start(up.at[2, n, 2], landed_z.at[n, 2], others[1]))
        run_chunks(chunks - 1, chunks)

    @pl.loop(0, tiles)
    def _(t):
        place = pl.ds(pl.multiple_of(t * TILE, TILE), TILE)
        x[place, :] = branch[place, :].astype(BF16)
        g[place, :] = back[place, :].astype(BF16)

    stored = []
    for n, (source, target) in enumerate(
        ((x, rows_own.at[0]), (g, rows_own.at[1]), (x, rows_other.at[0]), (g, rows_other.at[1]))
    ):
        place = pl.ds((n // 2) * capacity, capacity)
        stored.append(pltpu.make_async_copy(source.at[place], target, row_sems.at[n]))
    for one in stored:
        one.start()
    for one in grad_copies(chunks - 1) + stored:
        one.wait()
    if mode == "first":
        wait_in(far)
    elif mode == "second":
        wait_in([hopped[n, 0, 1] for n in range(2)] + last + z_sent[2:] + [crossed])
    if mode != "plain":
        for one in remote.made:
            one.wait_send()


def expert_block(moves, mode, expert, sorted_rows, extra, deep, half_hidden, grad_shapes, landing):
    capacity, width = sorted_rows[0].shape[1:]
    rows = 2 * capacity
    chunks = 4 if mode == "plain" else moves.nz
    chunk = half_hidden // chunks
    anywhere = pl.BlockSpec(memory_space=pl.ANY)
    row_shape = jax.ShapeDtypeStruct((2, capacity, width), BF16)
    outs = [row_shape] * 2 + grad_shapes + landing
    scratch = [
        pltpu.VMEM((width, half_hidden), BF16),
        pltpu.VMEM((half_hidden, width), BF16),
        pltpu.VMEM((rows, width), BF16),
        pltpu.VMEM((width, rows), BF16),
        pltpu.VMEM((rows, width), BF16),
        pltpu.VMEM((rows, width), F32),
        pltpu.VMEM((rows, width), F32),
        pltpu.VMEM((width, chunk), F32),
        pltpu.VMEM((chunk, width), F32),
        pltpu.VMEM((width, chunk), BF16),
        pltpu.VMEM((chunk, width), BF16),
    ]
    copies = 2 if mode == "plain" else 4 * moves.nz * moves.nf
    scratch += [
        pltpu.SemaphoreType.DMA((copies,)),
        pltpu.SemaphoreType.DMA((4,)),
        pltpu.SemaphoreType.DMA((copies,)),
    ]
    options = {}
    if mode == "second":
        block = (moves.nz, deep, half_hidden)
        scratch += [
            pltpu.VMEM((3, 2) + block, BF16),
            pltpu.VMEM((2, 2) + block, BF16),
            pltpu.SemaphoreType.DMA((6,)),
        ]
    if mode != "plain":
        count = 13 + 2 * (moves.nz - 1) if mode == "second" else 6
        scratch += [pltpu.SemaphoreType.DMA((count,))] * 2
        options = {"collective_id": 2 + expert, "has_side_effects": True}
    return pl.pallas_call(
        functools.partial(expert_kernel, moves, mode, expert, deep, chunk, chunks),
        in_specs=[anywhere] * (4 + len(extra)),
        out_specs=[anywhere] * len(outs),
        out_shape=outs,
        scratch_shapes=scratch,
        compiler_params=pltpu.CompilerParams(vmem_limit_bytes=58 * MIB, **options),
        cost_estimate=pl.CostEstimate(
            flops=12 * rows * width * half_hidden,
            bytes_accessed=8 * width * half_hidden + 16 * rows * width,
            transcendentals=rows * half_hidden,
        ),
        name="expert_" + mode,
    )(*sorted_rows, *extra)


def gather_experts_whole(w_expert_in, w_expert_out, core, nz):
    width, hidden = w_expert_out.shape[2], w_expert_in.shape[2]
    all_in = lax.all_gather(w_expert_in, AXES, axis=1, tiled=True)
    all_out = lax.all_gather(w_expert_out, AXES, axis=1, tiled=True)
    all_in = all_in.reshape(EXPERTS, width, nz, 2, hidden // (2 * nz))
    all_in = lax.dynamic_index_in_dim(all_in, core, 3, False)
    all_in = all_in.reshape(EXPERTS, width, hidden // 2)
    all_out = all_out.reshape(EXPERTS, nz, 2, hidden // (2 * nz), width)
    all_out = lax.dynamic_index_in_dim(all_out, core, 2, False)
    all_out = all_out.reshape(EXPERTS, hidden // 2, width)
    return [[all_in[e], all_out[e]] for e in range(EXPERTS)]


def local(
    nd,
    nf,
    tokens,
    seq_lengths,
    expert_ids,
    grad_out,
    ln1_gain,
    ln1_bias,
    w_qkv,
    w_attn_out,
    ln2_gain,
    ln2_bias,
    w_expert_in,
    w_expert_out,
):
    rows, width = tokens.shape
    deep = w_qkv.shape[0]
    moves = Moves(nd, nf)
    staged = deep % 32 == 0 and nf == 4 and moves.nz == 4
    core = lax.rem(lax.axis_index("dp"), 2)
    zed = lax.axis_index("dp") // 2
    flat = lax.axis_index("fsdp")

    positions = jnp.arange(rows, dtype=jnp.int32)
    bounds = jnp.cumsum(seq_lengths[0])
    segment = jnp.sum((positions[:, None] >= bounds[None, :]).astype(jnp.int32), axis=1)
    seg_row = jnp.broadcast_to(segment[None, :], (8, rows))
    seg_col = jnp.broadcast_to(segment[:, None], (rows, BLOCK))
    routed = expert_ids[:, 0]
    rank_second = jnp.cumsum(routed) - routed
    capacity = 3 * rows // 4
    slot = jnp.where(routed == 1, capacity + rank_second, positions - rank_second)

    params = jnp.stack([ln1_gain, ln1_bias, ln2_gain, ln2_bias], axis=1)
    params = jnp.pad(params, ((0, 0), (0, BLOCK - 4)))
    mine = jnp.concatenate([w_qkv, w_attn_out, params], axis=1)
    arguments = (tokens, grad_out, mine, w_expert_in, w_expert_out)
    if staged:
        return staged_block(moves, arguments, seg_row, seg_col, slot, (zed, core, flat))
    return plain_block(moves, arguments, seg_row, seg_col, slot, (zed, core, flat))


def staged_block(moves, arguments, seg_row, seg_col, slot, place):
    tokens, grad_out, mine, w_expert_in, w_expert_out = arguments
    rows, width = tokens.shape
    deep, hidden = w_expert_in.shape[1:]
    half_hidden = hidden // 2
    capacity = 3 * rows // 4
    zed, core, flat = place
    slot_row = jnp.broadcast_to(slot[None, :], (8, rows))
    lane = jnp.arange(BLOCK, dtype=jnp.int32)[None, :]
    marks = jnp.where(lane == 0, seg_col, slot[:, None])
    outs = forward_pass(
        moves, tokens, mine, w_expert_in, w_expert_out, seg_row, seg_col, slot_row, grad_out
    )
    whole_qkv, whole_attn, params, first_in = [one.reshape(-1, one.shape[-1]) for one in outs[:4]]
    first_out = outs[4].reshape(half_hidden, width)
    columns = list(outs[5:7])
    sorted_other, grad_other = outs[7:9]
    normed_one, projected, mixed, stats, hidden_one, sorted_rows, grad_sorted = outs[9:]
    by_expert = lambda value: value.reshape(EXPERTS, capacity, width)
    row_inputs = [by_expert(one) for one in (sorted_rows, sorted_other, grad_sorted, grad_other)]
    shape = lambda *dims: jax.ShapeDtypeStruct(dims, BF16)
    nz, nf = moves.nz, moves.nf
    block = (nz, 2 * deep, half_hidden)
    grad_shapes = [shape(nf // 2, *block)] * 4
    first = expert_block(
        moves,
        "first",
        0,
        row_inputs,
        [first_in, first_out] + columns,
        deep,
        half_hidden,
        grad_shapes,
        [shape(nf - 1, *one.shape) for one in columns],
    )
    second = expert_block(
        moves,
        "second",
        1,
        row_inputs,
        columns + list(first[6:8]) + list(first[2:6]) + [first[1]],
        deep,
        half_hidden,
        grad_shapes,
        [shape(2, *block)] * 2
        + [shape(*block)] * 2
        + [shape(2, capacity, width)]
        + [shape(2, deep, half_hidden), shape(2, nz - 1, deep, half_hidden)],
    )
    landed = second[10]
    results = backward_pass(
        moves,
        deep,
        [projected, whole_qkv, whole_attn, hidden_one, normed_one, tokens, grad_out],
        [first[0], second[0], landed, second[1]],
        [first[2], first[4]] + list(second[6:10]) + list(second[11:13]) + list(second[2:6]),
        stats.T,
        seg_row,
        marks,
        mixed,
        params,
    )
    block_result, grad_input, share_in, share_out, share_qkv, share_attn, vectors = results[:7]
    vectors = vectors[:, :4].T
    return (
        block_result,
        grad_input,
        vectors[0],
        vectors[1],
        share_qkv,
        share_attn,
        vectors[2],
        vectors[3],
        share_in,
        share_out,
    )


def plain_block(moves, arguments, seg_row, seg_col, slot, place):
    tokens, grad_out, mine, w_expert_in, w_expert_out = arguments
    rows, width = tokens.shape
    hidden = w_expert_in.shape[2]
    deep = mine.shape[0]
    nz = moves.nz
    zed, core, flat = place
    capacity = 3 * rows // 4
    whole = lax.all_gather(mine, AXES, axis=0, tiled=True)
    whole_qkv, whole_attn = whole[:, : 3 * width], whole[:, 3 * width : 4 * width]
    params = whole[:, 4 * width :]
    expert_weights = gather_experts_whole(w_expert_in, w_expert_out, core, nz)
    gain_one, bias_one, gain_two, bias_two = [
        params[:, n].astype(F32)[None, :] for n in range(4)
    ]
    tokens_wide = tokens.astype(F32)
    scaled_one, inverse_one = norm_parts(tokens_wide)
    normed_one = (scaled_one * gain_one + bias_one).astype(BF16)
    projected = dot(normed_one, whole_qkv).astype(BF16)
    mixed, stats = attention_forward(projected, seg_row, seg_col, 0, width // BLOCK)
    hidden_one = tokens_wide + dot(mixed, whole_attn)
    scaled_two, inverse_two = norm_parts(hidden_one)
    normed_two = (scaled_two * gain_two + bias_two).astype(BF16)
    slots = jnp.arange(EXPERTS * capacity, dtype=jnp.int32)[:, None]
    spread = (slots == slot[None, :]).astype(BF16)
    by_expert = lambda value: value.reshape(EXPERTS, capacity, width)
    row_inputs = []
    for value in (normed_two, grad_out):
        ordered = dot(spread, value).astype(BF16)
        row_inputs += [by_expert(ordered), by_expert(moves.core(ordered))]
    results, grad_pieces = [], []
    for e in range(EXPERTS):
        weights = expert_weights[e]
        shapes = [jax.ShapeDtypeStruct(one.shape, BF16) for one in weights]
        outs = expert_block(
            moves, "plain", e, row_inputs, weights, deep, hidden // 2, shapes, []
        )
        results.append(add_low(outs[0], moves.core(outs[1])))
        grad_pieces.append(outs[2:])
    both = jnp.concatenate(results, axis=1)
    grad_normed_two = dot_tn(spread, both[1])
    block_result = (hidden_one + dot_tn(spread, both[0])).astype(BF16)
    grad_hidden = grad_out.astype(F32) + norm_back(
        grad_normed_two, scaled_two, inverse_two, gain_two
    )
    grad_branch = grad_hidden.astype(BF16)
    grad_mixed = dot_nt(grad_branch, whole_attn).astype(BF16)
    trio = attention_backward(
        projected, grad_mixed, stats.T, seg_row, seg_col, 0, width // BLOCK
    )
    grad_projected = jnp.concatenate(trio, axis=1)
    grad_normed_one = dot_nt(grad_projected, whole_qkv)
    grad_input = grad_hidden + norm_back(grad_normed_one, scaled_one, inverse_one, gain_one)
    vectors = jnp.stack(
        [
            jnp.sum(grad_normed_one * scaled_one, axis=0),
            jnp.sum(grad_normed_one, axis=0),
            jnp.sum(grad_normed_two * scaled_two, axis=0),
            jnp.sum(grad_normed_two, axis=0),
        ]
    )
    own = lambda value, dim: lax.psum_scatter(value, AXES, scatter_dimension=dim, tiled=True)
    vectors = own(vectors, 1)
    full_in = jnp.stack([pieces[0] for pieces in grad_pieces])
    full_out = jnp.stack([pieces[1] for pieces in grad_pieces])
    full_in = full_in.reshape(EXPERTS, width, nz, 1, -1).astype(F32)
    full_out = full_out.reshape(EXPERTS, nz, 1, -1, width).astype(F32)
    chosen = jnp.arange(2) == core
    full_in = jnp.where(chosen[None, None, None, :, None], full_in, 0.0)
    full_out = jnp.where(chosen[None, None, :, None, None], full_out, 0.0)
    return (
        block_result,
        grad_input,
        vectors[0],
        vectors[1],
        own(dot_tn(normed_one, grad_projected), 0),
        own(dot_tn(mixed, grad_branch), 0),
        vectors[2],
        vectors[3],
        own(full_in.reshape(EXPERTS, width, hidden), 1),
        own(full_out.reshape(EXPERTS, hidden, width), 1),
    )


def solution(mesh):
    rows = P(AXES, None)
    vector = P(AXES)
    expert = P(None, AXES, None)
    return jax.shard_map(
        functools.partial(local, mesh.shape["dp"], mesh.shape["fsdp"]),
        mesh=mesh,
        in_specs=(
            rows, rows, rows, rows, vector, vector, rows, rows, vector, vector, expert, expert
        ),
        out_specs=(
            rows, rows, vector, vector, rows, rows, vector, vector, expert, expert
        ),
        check_vma=False,
    )
```

```python
import functools

import jax
import jax.numpy as jnp
from jax import lax
from jax.experimental import pallas as pl
from jax.experimental.pallas import tpu as pltpu
from jax.sharding import PartitionSpec as P

HEADS = 16
HEAD_DIM = 64
EXPERTS = 2
EPSILON = 1e-05
MASKED = -1000000000.0
AXES = ("dp", "fsdp")
BLOCK = 128
TILE = 256
MIB = 1024 * 1024
PARTS = 4
F32 = jnp.float32
BF16 = jnp.bfloat16
NT = (((1,), (1,)), ((), ()))
TN = (((0,), (0,)), ((), ()))
ROOT_2_PI = 0.7978845608028654
CUBIC = 0.044715


def dot(a, b):
    return jnp.dot(a, b, preferred_element_type=F32)


def dot_nt(a, b):
    return lax.dot_general(a, b, NT, preferred_element_type=F32)


def dot_tn(a, b):
    return lax.dot_general(a, b, TN, preferred_element_type=F32)


def norm_parts(values):
    average = jnp.mean(values, axis=-1, keepdims=True)
    centred = values - average
    variance = jnp.mean(centred * centred, axis=-1, keepdims=True)
    inverse = lax.rsqrt(variance + EPSILON)
    return (centred * inverse, inverse)


def norm_back(grad_normed, scaled, inverse, gain):
    grad_scaled = grad_normed * gain
    middle = jnp.mean(grad_scaled, axis=-1, keepdims=True)
    along = jnp.mean(grad_scaled * scaled, axis=-1, keepdims=True)
    return inverse * (grad_scaled - middle - scaled * along)


class Moves:
    def __init__(self, nd, nf):
        self.nz, self.nf = nd // 2, nf
        bits = []
        bit = 1
        while bit < nf:
            bits.append(bit)
            bit *= 2
        self.orders = (tuple(bits), tuple(reversed(bits)))

    def send(self, value, where):
        pairs = []
        for zed in range(self.nz):
            for core in range(2):
                for flat in range(self.nf):
                    z_to, core_to, f_to = where(zed, core, flat)
                    pairs.append(
                        (
                            (zed * 2 + core) * self.nf + flat,
                            (z_to * 2 + core_to) * self.nf + f_to,
                        )
                    )
        return lax.ppermute(value, AXES, pairs)

    def core(self, value):
        return self.send(value, lambda z, c, f: (z, 1 - c, f))

    def flat(self, value, bit):
        return self.send(value, lambda z, c, f: (z, c, f ^ bit))

    def along(self, value, steps):
        return self.send(value, lambda z, c, f: ((z + steps) % self.nz, c, f))

    def near(self, value, bit):
        return self.send(value, lambda z, c, f: (z ^ bit, c, f))

    def relative(self, stream):
        offsets = [0]
        for bit in reversed(self.orders[stream]):
            offsets = offsets + [one ^ bit for one in offsets]
        return tuple(offsets)

    def gather_z(self, value):
        return [value] + [self.along(value, k) for k in range(1, self.nz)]

    def gather_z_pair(self, value):
        held, bit = value[:, None], 1
        while 2 * bit < self.nz:
            held = jnp.concatenate([held, self.near(held, bit)], axis=1)
            bit *= 2
        got = self.near(held, bit)
        return [jnp.concatenate([held[n], got[n]], axis=0) for n in range(2)], got

    def gather_first(self, value, stream):
        held = value[None]
        for bit in tuple(reversed(self.orders[stream]))[:-1]:
            held = jnp.concatenate([held, self.flat(held, bit)], axis=0)
        return held

    def gather_last(self, held, stream):
        return self.flat(held, self.orders[stream][0])

    def reduce_flat(self, keep, sent, stream):
        order = self.orders[stream]
        now = add_low(keep, self.flat(sent, order[0]))
        for bit in order[1:]:
            half = now.shape[0] // 2
            now = add_low(now[:half], self.flat(now[half:], bit))
        return now[0]

    def reduce_z(self, value):
        total = value[0].astype(F32)
        for k in range(1, self.nz):
            total = total + self.along(value[k], k).astype(F32)
        return total

    def reduce_z_pair(self, value):
        bit = self.nz // 2
        while bit > 1:
            value = add_low(value[:bit], self.near(value[bit:], bit))
            bit //= 2
        return value[0].astype(F32) + self.near(value[1], 1).astype(F32)


def after(value, *others):
    return lax.optimization_barrier((value,) + others)[0]


def add_low(a, b):
    return (a.astype(F32) + b.astype(F32)).astype(BF16)


def attention_forward_kernel(seg_row, seg_col, q, k, v, out, stats, bias):
    rows = q.shape[0]
    pair = pl.program_id(0)
    lane = lax.broadcasted_iota(jnp.int32, (1, BLOCK), 1)

    @pl.when(pair == 0)
    def _():
        stats[...] = jnp.zeros_like(stats)
        for i in range(rows // TILE):
            span = (i + 1) * TILE
            place = slice(i * TILE, span)
            query = lax.broadcasted_iota(jnp.int32, (TILE, span), 0) + i * TILE
            key = lax.broadcasted_iota(jnp.int32, (TILE, span), 1)
            same = seg_col[place, 0:1] == seg_row[0:1, :span]
            bias[place, :span] = jnp.where(same & (key <= query), 0.0, MASKED)

    for i in range(rows // TILE):
        span = (i + 1) * TILE
        place = slice(i * TILE, span)
        query = q[place, :] * jnp.asarray(HEAD_DIM**-0.5, BF16)
        mixed = jnp.zeros((TILE, BLOCK), F32)
        held = stats[place, :]
        for side in range(2):
            mine = (lane // HEAD_DIM) == side
            part = jnp.where(mine, query, jnp.zeros_like(query))
            scores = dot_nt(part, k[:span, :]) + bias[place, :span]
            highest = jnp.max(scores, axis=1, keepdims=True)
            terms = jnp.exp(scores - highest)
            total = jnp.sum(terms, axis=1, keepdims=True)
            attend = (terms * (1.0 / total)).astype(BF16)
            mixed = jnp.where(mine, dot(attend, v[:span, :]), mixed)
            held = jnp.where(lane == 2 * pair + side, highest + jnp.log(total), held)
        stats[place, :] = held
        out[place, :] = mixed.astype(BF16)


def attention_forward(projected, seg_row, seg_col, first, count):
    rows, width = projected.shape[0], projected.shape[1] // 3
    pairs = width // BLOCK
    column = lambda start: pl.BlockSpec((rows, BLOCK), lambda h: (0, start + h))
    whole = lambda shape: pl.BlockSpec(shape, lambda h: (0, 0))
    return pl.pallas_call(
        attention_forward_kernel,
        grid=(count,),
        in_specs=[
            whole((8, rows)),
            whole((rows, BLOCK)),
            column(first),
            column(first + pairs),
            column(first + 2 * pairs),
        ],
        out_specs=[column(0), whole((rows, BLOCK))],
        out_shape=[
            jax.ShapeDtypeStruct((rows, count * BLOCK), BF16),
            jax.ShapeDtypeStruct((rows, BLOCK), F32),
        ],
        scratch_shapes=[pltpu.VMEM((rows, rows), F32)],
        compiler_params=pltpu.CompilerParams(vmem_limit_bytes=40 * MIB),
        cost_estimate=pl.CostEstimate(
            flops=4 * rows * rows * count * BLOCK,
            bytes_accessed=8 * rows * count * BLOCK,
            transcendentals=2 * count * rows * rows,
        ),
        name="attention_forward",
    )(seg_row, seg_col, projected, projected, projected)


def attention_backward_kernel(first, seg_row, seg_col, stats, q, k, v, g, dq, dk, dv, bias, dks, dvs):
    rows = q.shape[0]
    pair = pl.program_id(0)
    lane = lax.broadcasted_iota(jnp.int32, (1, BLOCK), 1)
    row = lax.broadcasted_iota(jnp.int32, (BLOCK, 1), 0)

    @pl.when(pair == 0)
    def _():
        for i in range(rows // TILE):
            span = (i + 1) * TILE
            place = slice(i * TILE, span)
            query = lax.broadcasted_iota(jnp.int32, (span, TILE), 1) + i * TILE
            key = lax.broadcasted_iota(jnp.int32, (span, TILE), 0)
            same = seg_col[:span, 0:1] == seg_row[0:1, place]
            bias[:span, place] = jnp.where(same & (key <= query), 0.0, MASKED)

    dks[...] = jnp.zeros_like(dks)
    dvs[...] = jnp.zeros_like(dvs)
    k_turned = k[...].T
    for i in range(rows // TILE):
        span = (i + 1) * TILE
        place = slice(i * TILE, span)
        query = q[place, :] * jnp.asarray(HEAD_DIM**-0.5, BF16)
        grad = g[place, :]
        turned = jnp.zeros((BLOCK, TILE), F32)
        for side in range(2):
            mine = (lane // HEAD_DIM) == side
            part = jnp.where(mine, query, jnp.zeros_like(query))
            grad_part = jnp.where(mine, grad, jnp.zeros_like(grad))
            level = stats[pl.ds(2 * (first + pair) + side, 1), place]
            scores = dot_nt(k[:span, :], part) + bias[:span, place]
            attend = jnp.exp(scores - level)
            grad_attend = dot_nt(v[:span, :], grad_part)
            inner = jnp.sum(attend * grad_attend, axis=0, keepdims=True)
            grad_scores = (attend * (grad_attend - inner)).astype(BF16)
            dks[:span, :] += dot(grad_scores, part)
            dvs[:span, :] += dot(attend.astype(BF16), grad_part)
            turned = jnp.where(
                (row // HEAD_DIM) == side, dot(k_turned[:, :span], grad_scores), turned
            )
        dq[place, :] = (turned.T * HEAD_DIM**-0.5).astype(BF16)
    dk[...] = dks[...].astype(BF16)
    dv[...] = dvs[...].astype(BF16)


def attention_backward(projected, grad_mixed, stats, seg_row, seg_col, first, count):
    rows, width = projected.shape[0], projected.shape[1] // 3
    pairs = width // BLOCK
    column = lambda start: pl.BlockSpec((rows, BLOCK), lambda h: (0, start + h))
    whole = lambda shape: pl.BlockSpec(shape, lambda h: (0, 0))
    share = jax.ShapeDtypeStruct((rows, count * BLOCK), BF16)
    return pl.pallas_call(
        functools.partial(attention_backward_kernel, first),
        grid=(count,),
        in_specs=[
            whole((8, rows)),
            whole((rows, BLOCK)),
            whole((BLOCK, rows)),
            column(first),
            column(first + pairs),
            column(first + 2 * pairs),
            column(first),
        ],
        out_specs=[column(0), column(0), column(0)],
        out_shape=[share, share, share],
        scratch_shapes=[
            pltpu.VMEM((rows, rows), F32),
            pltpu.VMEM((rows, BLOCK), F32),
            pltpu.VMEM((rows, BLOCK), F32),
        ],
        compiler_params=pltpu.CompilerParams(vmem_limit_bytes=40 * MIB),
        cost_estimate=pl.CostEstimate(
            flops=10 * rows * rows * count * BLOCK,
            bytes_accessed=14 * rows * count * BLOCK,
            transcendentals=2 * count * rows * rows,
        ),
        name="attention_backward",
    )(seg_row, seg_col, stats, projected, projected, projected, grad_mixed)


class Copies:
    def __init__(self, send_sems, recv_sems):
        self.send_sems, self.recv_sems, self.made = send_sems, recv_sems, []

    def start(self, source, target, device):
        n = len(self.made)
        one = pltpu.make_async_remote_copy(
            src_ref=source,
            dst_ref=target,
            send_sem=self.send_sems.at[n],
            recv_sem=self.recv_sems.at[n],
            device_id=device,
            device_id_type=pl.DeviceIdType.MESH,
        )
        one.start()
        self.made.append(one)
        return one


def wait_in(copies):
    for one in copies:
        one.wait_recv()


def forward_kernel(
    moves,
    tokens,
    mine,
    own_in,
    own_out,
    seg_row,
    seg_col,
    slot_row,
    grad_out,
    out_qkv,
    out_attn,
    out_params,
    first_in,
    first_out,
    column_in,
    column_out,
    sorted_other,
    grad_other,
    turned_normed,
    projected,
    turned_mixed,
    turned_stats,
    hidden,
    sorted_rows,
    grad_sorted,
    weights,
    bias,
    normed,
    mixed,
    stats,
    normed_two,
    send_sems,
    recv_sems,
    local_sems,
):
    nz, nf = moves.nz, moves.nf
    dp, flat = lax.axis_index("dp"), lax.axis_index("fsdp")
    zed, core = dp // 2, lax.rem(dp, 2)
    rows, wide = tokens.shape
    sibling = (zed * 2 + 1 - core, flat)
    next_z, across_z = [((zed ^ k) * 2 + core, flat) for k in (1, 2)]
    others = [next_z, across_z]
    hops = {bit: (dp, flat ^ bit) for bit in moves.orders[0]}

    barrier = pltpu.get_barrier_semaphore()
    for device in [sibling] + others + list(hops.values()):
        pl.semaphore_signal(barrier, inc=1, device_id=device, device_id_type=pl.DeviceIdType.MESH)
    pl.semaphore_wait(barrier, 1 + len(others) + len(hops))

    remote = Copies(send_sems, recv_sems)
    local = []

    def local_start(source, target):
        one = pltpu.make_async_copy(source, target, local_sems.at[len(local)])
        one.start()
        local.append(one)
        return one

    own = local_start(mine, weights.at[zed, core, flat])
    stream_columns = (slice(0, 2 * wide), slice(2 * wide, 4 * wide + BLOCK))

    def column_start(source, place):
        return [remote.start(source, place(zed), device) for device in (across_z, next_z)]

    def column_next(column, place):
        wait_in(column[:1])
        column.append(remote.start(place(zed ^ 2), place(zed ^ 2), next_z))

    def column_wait(column):
        wait_in(column[1:])

    def weight_place(stream):
        return lambda z_of: weights.at[z_of, core, flat, :, stream_columns[stream]]

    def weight_column(stream):
        return column_start(mine.at[:, stream_columns[stream]], weight_place(stream))

    columns_a = weight_column(0)
    targets = (first_in.at[zed, core, flat], column_in.at[zed, core])
    cut = own_in.shape[2] // (2 * nz)
    crossed, blocks = [], []
    for e in range(EXPERTS):
        for z_of in range(nz):
            target = targets[e].at[:, pl.ds(z_of * cut, cut)]
            theirs, ours = [
                own_in.at[e, :, pl.ds(pl.multiple_of((2 * z_of + which) * cut, cut), cut)]
                for which in (1 - core, core)
            ]
            crossed.append(remote.start(theirs, target, sibling))
            blocks.append(local_start(ours, target))
    blocks.append(local_start(own_out.at[0], first_out.at[zed, flat]))
    blocks.append(local_start(own_out.at[1], column_out.at[zed]))

    capacity = sorted_rows.shape[0] // EXPERTS

    def sort_rows(source, target, first):
        @pl.loop(0, target.shape[0] // TILE)
        def _(t):
            place = pl.ds(pl.multiple_of(t * TILE, TILE), TILE)
            slot = lax.broadcasted_iota(jnp.int32, (TILE, rows), 0) + t * TILE + first
            chosen = (slot == slot_row[0:1, :]).astype(F32).astype(BF16)
            target[place, :] = dot(chosen, source[...]).astype(BF16)

    def send_weights(stream, owner, device):
        place = weights.at[:, core, owner, :, stream_columns[stream]]
        return remote.start(place, place, device)

    near = [tuple(reversed(moves.orders[n]))[0] for n in range(2)]
    far = [moves.orders[n][0] for n in range(2)]
    hop_near, hop_far, across = [], [], []
    own.wait()
    column_next(columns_a, weight_place(0))
    columns_b = weight_column(1)
    column_wait(columns_a)
    hop_near.append(send_weights(0, flat, hops[near[0]]))
    hop_far.append(send_weights(0, flat, hops[far[0]]))
    across.append(send_weights(0, flat, sibling))

    first_places = (
        lambda z_of: first_in.at[z_of, :, flat],
        lambda z_of: first_out.at[z_of, flat],
    )
    wait_in(crossed)
    for one in blocks:
        one.wait()
    column_next(columns_b, weight_place(1))
    first_a = column_start(first_in.at[zed, :, flat], first_places[0])
    column_wait(columns_b)
    hop_near.append(send_weights(1, flat, hops[near[1]]))
    hop_far.append(send_weights(1, flat, hops[far[1]]))
    across.append(send_weights(1, flat, sibling))
    column_next(first_a, first_places[0])
    first_b = column_start(own_out.at[0], first_places[1])

    sort_rows(grad_out, grad_sorted, 0)
    for i in range(rows // TILE):
        span = (i + 1) * TILE
        place = slice(i * TILE, span)
        query = lax.broadcasted_iota(jnp.int32, (TILE, span), 0) + i * TILE
        key = lax.broadcasted_iota(jnp.int32, (TILE, span), 1)
        same = seg_col[place, 0:1] == seg_row[0:1, :span]
        bias[place, :span] = jnp.where(same & (key <= query), 0.0, MASKED)
    stats[...] = jnp.zeros_like(stats)

    wait_in(hop_near)
    hop_last = [send_weights(n, flat ^ near[n], hops[far[n]]) for n in range(2)]
    across += [send_weights(n, flat ^ near[n], sibling) for n in range(2)]
    exchanged = [remote.start(grad_sorted, grad_other, sibling)]

    def send_first(stream, owner, device):
        place = first_in.at[:, :, owner] if stream == 0 else first_out.at[:, owner]
        return remote.start(place, place, device)

    column_wait(first_a)
    first_near = [send_first(0, flat, hops[near[0]])]
    first_far = [send_first(0, flat, hops[far[0]])]
    column_next(first_b, first_places[1])
    wait_in(hop_far)
    across += [send_weights(n, flat ^ far[n], sibling) for n in range(2)]
    wait_in(hop_last)
    across += [send_weights(n, flat ^ near[n] ^ far[n], sibling) for n in range(2)]

    wait_in(across)
    whole = 2 * nz * nf * mine.shape[0]
    writes = [
        local_start(weights.at[:, :, :, :, pl.ds(0, 3 * wide)], out_qkv),
        local_start(weights.at[:, :, :, :, pl.ds(3 * wide, wide)], out_attn),
        local_start(weights.at[:, :, :, :, pl.ds(4 * wide, BLOCK)], out_params),
    ]
    turned = weights[:, :, :, :, pl.ds(4 * wide, BLOCK)].reshape(whole, BLOCK).astype(F32).T
    gain, shift = turned[0:1, :], turned[1:2, :]

    @pl.loop(0, rows // TILE)
    def _(t):
        place = pl.ds(pl.multiple_of(t * TILE, TILE), TILE)
        scaled, _ = norm_parts(tokens[place, :].astype(F32))
        normed[place, :] = (scaled * gain + shift).astype(BF16)
        for part in range(3):
            columns = pl.ds(part * wide, wide)
            matrix = weights[:, :, :, :, columns].reshape(whole, wide)
            projected[place, columns] = dot(normed[place, :], matrix).astype(BF16)

    lane = lax.broadcasted_iota(jnp.int32, (1, BLOCK), 1)
    pairs = wide // BLOCK

    def attend_pair(pair):
        columns = [
            pl.ds(pl.multiple_of(n * wide + pair * BLOCK, BLOCK), BLOCK) for n in range(3)
        ]
        for i in range(rows // TILE):
            span = (i + 1) * TILE
            place = slice(i * TILE, span)
            query = projected[place, columns[0]] * jnp.asarray(HEAD_DIM**-0.5, BF16)
            result = jnp.zeros((TILE, BLOCK), F32)
            held = stats[place, :]
            for side in range(2):
                ours = (lane // HEAD_DIM) == side
                part = jnp.where(ours, query, jnp.zeros_like(query))
                scores = dot_nt(part, projected[:span, columns[1]]) + bias[place, :span]
                highest = jnp.max(scores, axis=1, keepdims=True)
                terms = jnp.exp(scores - highest)
                total = jnp.sum(terms, axis=1, keepdims=True)
                attend = (terms * (1.0 / total)).astype(BF16)
                result = jnp.where(ours, dot(attend, projected[:span, columns[2]]), result)
                held = jnp.where(lane == 2 * pair + side, highest + jnp.log(total), held)
            stats[place, :] = held
            mixed[place, columns[0]] = result.astype(BF16)

    def attend_pairs(start, stop):
        @pl.loop(start, stop)
        def _(pair):
            attend_pair(pair)

    attend_pairs(0, pairs // 4)
    column_wait(first_b)
    first_near.append(send_first(1, flat, hops[near[1]]))
    first_far.append(send_first(1, flat, hops[far[1]]))

    second_places = (lambda z_of: column_in.at[z_of], lambda z_of: column_out.at[z_of])
    second_a = column_start(column_in.at[zed], second_places[0])

    attend_pairs(pairs // 4, pairs // 2)
    wait_in([first_near[0]])
    first_last = [send_first(0, flat ^ near[0], hops[far[0]])]
    column_next(second_a, second_places[0])
    second_b = column_start(own_out.at[1], second_places[1])
    attend_pairs(pairs // 2, 3 * pairs // 4)
    wait_in([first_near[1]])
    first_last.append(send_first(1, flat ^ near[1], hops[far[1]]))
    column_next(second_b, second_places[1])
    attend_pairs(3 * pairs // 4, pairs)

    gain_two, shift_two = turned[2:3, :], turned[3:4, :]

    @pl.loop(0, rows // TILE)
    def _(t):
        place = pl.ds(pl.multiple_of(t * TILE, TILE), TILE)
        matrix = weights[:, :, :, :, pl.ds(3 * wide, wide)].reshape(whole, wide)
        total = tokens[place, :].astype(F32) + dot(mixed[place, :], matrix)
        hidden[place, :] = total
        scaled, _ = norm_parts(total)
        normed_two[place, :] = (scaled * gain_two + shift_two).astype(BF16)

    sort_rows(normed_two, sorted_rows.at[pl.ds(0, capacity)], 0)
    place = pl.ds(0, capacity)
    exchanged.append(remote.start(sorted_rows.at[place], sorted_other.at[place], sibling))
    sort_rows(normed_two, sorted_rows.at[pl.ds(capacity, capacity)], capacity)
    place = pl.ds(capacity, capacity)
    exchanged.append(remote.start(sorted_rows.at[place], sorted_other.at[place], sibling))
    turned_normed[...] = normed[...].T
    turned_mixed[...] = mixed[...].T
    turned_stats[...] = stats[...].T
    wait_in(first_far)
    wait_in(first_last)
    column_wait(second_a)
    column_wait(second_b)
    wait_in(exchanged)
    for one in remote.made:
        one.wait_send()
    for one in writes:
        one.wait()


def forward_pass(moves, tokens, mine, own_in, own_out, seg_row, seg_col, slot_row, grad_out):
    nz, nf = moves.nz, moves.nf
    rows, wide = tokens.shape
    deep, half = own_in.shape[1], own_in.shape[2] // 2
    part = own_out.shape[1]
    capacity = 3 * rows // 4
    anywhere = pl.BlockSpec(memory_space=pl.ANY)
    inside = pl.BlockSpec(memory_space=pltpu.VMEM)
    shape = jax.ShapeDtypeStruct
    remote = 6 * (nz - 1) + 2 * nz + 26
    return pl.pallas_call(
        functools.partial(forward_kernel, moves),
        in_specs=[inside] * 8,
        out_specs=[anywhere] * 9 + [inside] * 7,
        out_shape=[
            shape((nz, 2, nf, deep, 3 * wide), BF16),
            shape((nz, 2, nf, deep, wide), BF16),
            shape((nz, 2, nf, deep, BLOCK), BF16),
            shape((nz, 2, nf, deep, half), BF16),
            shape((nz, nf, part, wide), BF16),
            shape((nz, 2, deep, half), BF16),
            shape((nz, part, wide), BF16),
            shape((EXPERTS * capacity, wide), BF16),
            shape((EXPERTS * capacity, wide), BF16),
            shape((wide, rows), BF16),
            shape((rows, 3 * wide), BF16),
            shape((wide, rows), BF16),
            shape((BLOCK, rows), F32),
            shape((rows, wide), F32),
            shape((EXPERTS * capacity, wide), BF16),
            shape((EXPERTS * capacity, wide), BF16),
        ],
        scratch_shapes=[
            pltpu.VMEM((nz, 2, nf, deep, 4 * wide + BLOCK), BF16),
            pltpu.VMEM((rows, rows), F32),
            pltpu.VMEM((rows, wide), BF16),
            pltpu.VMEM((rows, wide), BF16),
            pltpu.VMEM((rows, BLOCK), F32),
            pltpu.VMEM((rows, wide), BF16),
            pltpu.SemaphoreType.DMA((remote,)),
            pltpu.SemaphoreType.DMA((remote,)),
            pltpu.SemaphoreType.DMA((2 * nz + 6,)),
        ],
        compiler_params=pltpu.CompilerParams(
            collective_id=0, has_side_effects=True, vmem_limit_bytes=60 * MIB
        ),
        cost_estimate=pl.CostEstimate(
            flops=10 * rows * wide * wide, bytes_accessed=80 * wide * wide, transcendentals=0
        ),
        name="forward_pass",
    )(tokens, mine, own_in, own_out, seg_row, seg_col, slot_row, grad_out)


def sum_low(*values):
    total = values[0].astype(F32)
    for one in values[1:]:
        total = total + one.astype(F32)
    return total


def backward_kernel(
    moves,
    deep,
    projected,
    whole_qkv,
    whole_attn,
    hidden,
    normed_out,
    tokens_in,
    grad_out,
    rows_first,
    rows_second,
    landed_first,
    other_second,
    keep_first_in,
    keep_first_out,
    arrived_in,
    arrived_out,
    first_hop_in,
    first_hop_out,
    first_own,
    first_landed,
    keep_in,
    sent_in,
    keep_out,
    sent_out,
    stats,
    seg_row,
    marks,
    mixed,
    params,
    block_out,
    grad_tokens,
    share_in,
    share_out,
    share_qkv,
    share_attn,
    share_vectors,
    got_in,
    got_out,
    hop_in,
    hop_out,
    landed,
    wide_low,
    wide_f32,
    grad_projected,
    grad_mixed,
    branch,
    normed,
    tokens,
    key_sums,
    value_sums,
    low,
    cross,
    got_q,
    hop_q,
    z_q,
    up_q,
    vec,
    cross_vec,
    got_vec,
    hop_vec,
    z_vec,
    up,
    spare,
    up_first,
    z_first,
    z_second,
    final,
    send_sems,
    recv_sems,
    local_sems,
):
    nz, nf = moves.nz, moves.nf
    dp, flat = lax.axis_index("dp"), lax.axis_index("fsdp")
    zed, core = dp // 2, lax.rem(dp, 2)
    rows, wide = tokens.shape
    share = wide // PARTS
    sibling = (zed * 2 + 1 - core, flat)
    next_z, across_z = [((zed ^ k) * 2 + core, flat) for k in (1, 2)]
    others = [next_z, across_z]
    hops = {bit: (dp, flat ^ bit) for bit in moves.orders[0]}

    barrier = pltpu.get_barrier_semaphore()
    for device in [sibling] + others + list(hops.values()):
        pl.semaphore_signal(barrier, inc=1, device_id=device, device_id_type=pl.DeviceIdType.MESH)
    pl.semaphore_wait(barrier, 1 + len(others) + len(hops))

    remote = Copies(send_sems, recv_sems)
    local = []

    def local_start(source, target):
        one = pltpu.make_async_copy(source, target, local_sems.at[len(local)])
        one.start()
        local.append(one)
        return one

    def load(*pairs):
        for one in [local_start(source, target) for source, target in pairs]:
            one.wait()

    capacity = rows_first.shape[1]
    crossed_rows = [
        remote.start(other_second.at[1], grad_mixed.at[pl.ds(0, capacity)], sibling)
    ]
    crossed_late = [remote.start(other_second.at[0], landed, sibling)]
    row_loads = [
        local_start(source.at[1], grad_projected.at[pl.ds(0, capacity), pl.ds(e * wide, wide)])
        for e, source in enumerate((rows_first, rows_second, landed_first))
    ]
    loaded = local_start(projected, wide_low)
    phase_loads = [
        local_start(hidden, wide_f32),
        local_start(whole_attn, normed),
        local_start(grad_out, tokens),
    ]
    one_way = [moves.orders[n][0] for n in range(2)]
    other_way = [moves.orders[n][1] for n in range(2)]
    keep_first, arrived = (keep_first_in, keep_first_out), (arrived_in, arrived_out)
    first_hop = (first_hop_in, first_hop_out)

    keep, sent = (keep_in, keep_out), (sent_in, sent_out)
    got, hop = (got_in, got_out), (hop_in, hop_out)
    half_rows = [pl.ds(h * deep, deep) for h in range(2)]
    second_got = {}

    def second_start(h):
        for index in (1, 0):
            for n in range(2):
                second_got[n, index, h] = remote.start(
                    sent[n].at[index, :, half_rows[h]],
                    got[n].at[index, :, half_rows[h]],
                    hops[one_way[n]],
                )

    def sum_blocks(target, sources, h):
        pairs = []
        for n in range(2):
            for source, place in zip(sources[n], [target.at[n], spare.at[n, 0], spare.at[n, 1]]):
                pairs.append((source.at[:, half_rows[h]], place))
        load(*pairs)

        @pl.loop(0, nz)
        def _(k):
            for n in range(2):
                arrived = [spare[n, m, k] for m in range(len(sources[n]) - 1)]
                target[n, k] = sum_low(target[n, k], *arrived).astype(BF16)

    def z_first_step(source, landing):
        return [
            remote.start(source.at[n, k], landing.at[n, k // 2], next_z)
            for k in (3, 1)
            for n in range(2)
        ]

    def z_second_step(source, landing, begun):
        wait_in(begun[:2])
        for n in range(2):
            source[n, 2] = sum_low(source[n, 2], landing[n, 1]).astype(BF16)
            begun.append(remote.start(source.at[n, 2], landing.at[n, 2], across_z))
        return begun

    second_start(0)
    sum_blocks(
        up_first,
        [(keep_first[n].at[0], arrived[n].at[0], first_hop[n]) for n in range(2)],
        1,
    )
    first_z = z_first_step(up_first, z_first)

    for one in row_loads + phase_loads:
        one.wait()
    wait_in(crossed_rows)

    def add_rows(target, source, columns):
        @pl.loop(0, capacity // TILE)
        def _(t):
            place = pl.ds(pl.multiple_of(t * TILE, TILE), TILE)
            total = sum_low(grad_projected[place, target], source[place, columns])
            grad_projected[place, target] = total.astype(BF16)

    first_columns, second_columns = pl.ds(0, wide), pl.ds(wide, wide)
    add_rows(first_columns, grad_projected, pl.ds(2 * wide, wide))
    add_rows(second_columns, grad_mixed, first_columns)

    def tokens_order(place):
        total = jnp.zeros((TILE, wide), F32)
        for e in range(EXPERTS):
            slot = lax.broadcasted_iota(jnp.int32, (TILE, capacity), 1) + e * capacity
            chosen = (slot == marks[place, 1:2]).astype(F32).astype(BF16)
            total = total + dot(chosen, grad_projected[pl.ds(0, capacity), pl.ds(e * wide, wide)])
        return total

    turned = params[...].astype(F32).T
    gain_one, gain_two = turned[0:1, :], turned[2:3, :]
    empty = jnp.zeros((1, wide), F32)

    def second_norm_tile(t, sums):
        place = pl.ds(pl.multiple_of(t * TILE, TILE), TILE)
        grad = tokens_order(place)
        scaled, inverse = norm_parts(wide_f32[place, :])
        total = tokens[place, :].astype(F32) + norm_back(grad, scaled, inverse, gain_two)
        wide_f32[place, :] = total
        low_total = total.astype(BF16)
        branch[place, :] = low_total
        grad_mixed[place, :] = dot_nt(low_total, normed[...]).astype(BF16)
        return (
            sums[0] + jnp.sum(grad * scaled, axis=0, keepdims=True),
            sums[1] + jnp.sum(grad, axis=0, keepdims=True),
        )

    sums_two = lax.fori_loop(0, rows // TILE, second_norm_tile, (empty, empty))
    reloads = [local_start(normed_out, normed), local_start(tokens_in, tokens)]
    saved = local_start(wide_f32, grad_tokens)

    def second_next(h):
        wait_in([second_got[n, 1, h] for n in range(2)])
        sum_blocks(up.at[h], [(keep[n].at[1], got[n].at[1]) for n in range(2)], h)
        return [
            remote.start(up.at[h, n], hop[n].at[:, half_rows[h]], hops[other_way[n]])
            for n in range(2)
        ]

    def second_z(h, hopped):
        wait_in([second_got[n, 0, h] for n in range(2)] + hopped)
        for one in hopped:
            one.wait_send()
        sum_blocks(
            up.at[h], [(keep[n].at[0], got[n].at[0], hop[n]) for n in range(2)], h
        )
        return z_first_step(up.at[h], z_second.at[h])

    second_hop = second_next(0)
    second_start(1)
    first_z = z_second_step(up_first, z_first, first_z)
    saved.wait()

    lane = lax.broadcasted_iota(jnp.int32, (1, BLOCK), 1)
    row = lax.broadcasted_iota(jnp.int32, (BLOCK, 1), 0)
    for i in range(rows // TILE):
        span = (i + 1) * TILE
        place = slice(i * TILE, span)
        query = lax.broadcasted_iota(jnp.int32, (span, TILE), 1) + i * TILE
        key = lax.broadcasted_iota(jnp.int32, (span, TILE), 0)
        same = marks[:span, 0:1] == seg_row[0:1, place]
        wide_f32[:span, place] = jnp.where(same & (key <= query), 0.0, MASKED)
    loaded.wait()
    pairs = wide // BLOCK

    def attend_pair(pair):
        columns = [
            pl.ds(pl.multiple_of(n * wide + pair * BLOCK, BLOCK), BLOCK) for n in range(3)
        ]
        key_sums[...] = jnp.zeros_like(key_sums)
        value_sums[...] = jnp.zeros_like(value_sums)
        keys_turned = wide_low[:, columns[1]].T
        for i in range(rows // TILE):
            span = (i + 1) * TILE
            place = slice(i * TILE, span)
            query = wide_low[place, columns[0]] * jnp.asarray(HEAD_DIM**-0.5, BF16)
            grad = grad_mixed[place, columns[0]]
            turned = jnp.zeros((BLOCK, TILE), F32)
            for side in range(2):
                ours = (lane // HEAD_DIM) == side
                part = jnp.where(ours, query, jnp.zeros_like(query))
                grad_part = jnp.where(ours, grad, jnp.zeros_like(grad))
                level = stats[pl.ds(2 * pair + side, 1), place]
                scores = dot_nt(wide_low[:span, columns[1]], part) + wide_f32[:span, place]
                attend = jnp.exp(scores - level)
                grad_attend = dot_nt(wide_low[:span, columns[2]], grad_part)
                inner = jnp.sum(attend * grad_attend, axis=0, keepdims=True)
                grad_scores = (attend * (grad_attend - inner)).astype(BF16)
                key_sums[:span, :] += dot(grad_scores, part)
                value_sums[:span, :] += dot(attend.astype(BF16), grad_part)
                turned = jnp.where(
                    (row // HEAD_DIM) == side, dot(keys_turned[:, :span], grad_scores), turned
                )
            grad_projected[place, columns[0]] = (turned.T * HEAD_DIM**-0.5).astype(BF16)
        grad_projected[:, columns[1]] = key_sums[...].astype(BF16)
        grad_projected[:, columns[2]] = value_sums[...].astype(BF16)

    def attend_pairs(start, stop):
        @pl.loop(start, stop)
        def _(pair):
            attend_pair(pair)

    def weight_grads(n):
        @pl.loop(0, nz)
        def _(z_of):
            span = 2 * nf * deep
            place = pl.ds(pl.multiple_of(z_of * span, span), span)
            turned = normed[place, :]
            mixed_turned = mixed[place, :]
            for part in range(4):
                if part < 3:
                    columns = pl.ds(part * wide + n * share, share)
                    made = dot(turned, grad_projected[:, columns])
                else:
                    made = dot(mixed_turned, branch[:, pl.ds(n * share, share)])
                made = made.astype(BF16).reshape(2, nf, deep, share)
                low[n, z_of, :, :, :, pl.ds(part * share, share)] = made

    def cross_start(source, target):
        return remote.start(source.at[:, 1 - core], target, sibling)

    def cross_add(source, target):
        @pl.loop(0, nz)
        def _(k):
            source[k, core] = sum_low(source[k, core], target[k]).astype(source.dtype)

    def hop_start(source, target, n):
        bits = one_way[n], other_way[n]
        return [
            remote.start(
                source.at[:, core, flat ^ bits[0] ^ (bits[1] * index)],
                target.at[index],
                hops[bits[0]],
            )
            for index in (1, 0)
        ]

    def hop_next(source, arrived, target, landing, n):
        @pl.loop(0, nz)
        def _(k):
            mine = source[k, core, flat ^ other_way[n]]
            target[k] = sum_low(mine, arrived[1, k]).astype(target.dtype)

        return remote.start(target, landing, hops[other_way[n]])

    def z_start(source, arrived, landing, z_landing):
        @pl.loop(0, nz)
        def _(k):
            total = sum_low(source[k, core, flat], arrived[0, k], landing[k])
            source[k, core, flat] = total.astype(source.dtype)

        return [
            remote.start(source.at[zed ^ k, core, flat], z_landing.at[k // 2], next_z)
            for k in (3, 1)
        ]

    def z_next(source, z_landing, begun):
        wait_in(begun[:1])
        total = sum_low(source[zed ^ 2, core, flat], z_landing[1])
        source[zed ^ 2, core, flat] = total.astype(source.dtype)
        begun.append(remote.start(source.at[zed ^ 2, core, flat], z_landing.at[2], across_z))

    def z_total(source, z_landing):
        return sum_low(source[zed, core, flat], z_landing[0], z_landing[2])

    def finish_half(e, h, own, landing):
        for n in range(2):
            total = sum_low(own[n], landing[n, 0], landing[n, 2])
            final[2 * e + n, half_rows[h]] = total

    def finish_expert(e, writes):
        cut = share_in.shape[2] // (2 * nz)
        for z_of in range(nz):
            place = pl.ds(pl.multiple_of((z_of * 2 + core) * cut, cut), cut)
            target = share_in.at[e, :, place]
            source = final.at[2 * e]
            there = source.at[pl.ds(pl.multiple_of((1 - core) * deep, deep), deep)]
            here = source.at[pl.ds(pl.multiple_of(core * deep, deep), deep)]
            writes.append(remote.start(there.at[:, pl.ds(z_of * cut, cut)], target, sibling))
            stored.append(local_start(here.at[:, pl.ds(z_of * cut, cut)], target))
        part = share_out.shape[1] // 2
        for index in range(2):
            stored.append(
                local_start(
                    final.at[2 * e + 1, :, pl.ds(index * wide, wide)],
                    share_out.at[e, pl.ds(index * part, part)],
                )
            )

    def put_share(n, total):
        for part in range(4):
            piece = total[:, part * share : (part + 1) * share]
            if part < 3:
                share_qkv[:, pl.ds(part * wide + n * share, share)] = piece
            else:
                share_attn[:, pl.ds(n * share, share)] = piece

    def norm_tile(t, sums):
        place = pl.ds(pl.multiple_of(t * TILE, TILE), TILE)
        grad = dot_nt(grad_projected[place, :], wide_low[...])
        scaled, inverse = norm_parts(tokens[place, :].astype(F32))
        wide_f32[place, :] += norm_back(grad, scaled, inverse, gain_one)
        return (
            sums[0] + jnp.sum(grad * scaled, axis=0, keepdims=True),
            sums[1] + jnp.sum(grad, axis=0, keepdims=True),
        )

    stored, writes = [], []
    step = pairs // PARTS
    crossed, hopped, went, turned_z = {}, {}, {}, {}

    def part_attend(n):
        attend_pairs(n * step, (n + 1) * step)

    def part_begin(n):
        weight_grads(n)
        crossed[n] = cross_start(low.at[n], cross.at[n])

    def part_hop(n):
        wait_in([crossed[n]])
        cross_add(low.at[n], cross.at[n])
        hopped[n] = hop_start(low.at[n], got_q.at[n], n % 2)

    def part_next(n):
        wait_in([hopped[n][0]])
        went[n] = hop_next(low.at[n], got_q.at[n], up_q.at[n], hop_q.at[n], n % 2)

    def part_z(n):
        wait_in([hopped[n][1], went[n]])
        turned_z[n] = z_start(low.at[n], got_q.at[n], hop_q.at[n], z_q.at[n])

    def part_z_next(n):
        z_next(low.at[n], z_q.at[n], turned_z[n])

    def part_end(n):
        wait_in(turned_z[n][1:])
        put_share(n, z_total(low.at[n], z_q.at[n]))

    part_attend(0)
    for one in reloads:
        one.wait()
    part_begin(0)
    second_z_0 = second_z(0, second_hop)
    part_attend(1)
    part_hop(0)
    part_begin(1)
    z_second_step(up.at[0], z_second.at[0], second_z_0)
    second_hop_late = second_next(1)
    part_attend(2)
    part_hop(1)
    part_next(0)
    part_begin(2)
    second_z_1 = second_z(1, second_hop_late)
    part_attend(3)
    reload = local_start(whole_qkv, wide_low)
    restore = local_start(grad_tokens, wide_f32)
    part_hop(2)
    part_next(1)
    part_z(0)
    part_begin(3)
    z_second_step(up.at[1], z_second.at[1], second_z_1)
    reload.wait()
    restore.wait()
    sums = lax.fori_loop(0, 1, norm_tile, (empty, empty))
    part_hop(3)
    part_next(2)
    sums = lax.fori_loop(1, 3, norm_tile, sums)
    part_z(1)
    part_z_next(0)
    part_next(3)
    sums = lax.fori_loop(3, rows // TILE, norm_tile, sums)
    result = local_start(wide_f32, grad_tokens)
    index = lax.broadcasted_iota(jnp.int32, (BLOCK, 1), 0)
    stacked = jnp.zeros((BLOCK, wide), F32)
    for n, one in enumerate(sums + sums_two):
        stacked = jnp.where(index == n, one, stacked)
    vec[...] = stacked.T.reshape(nz, 2, nf, deep, BLOCK)
    crossed_v = [cross_start(vec, cross_vec)]
    wait_in(first_z[2:])
    load(
        (first_own, spare.at[0, 0, pl.ds(0, 2)]),
        *[(first_landed.at[n], spare.at[n, 1, pl.ds(0, nz - 1)]) for n in range(2)],
    )
    finish_half(0, 0, [spare[0, 0, n] for n in range(2)], spare.at[:, 1])
    finish_half(0, 1, [up_first[n, 0] for n in range(2)], z_first)
    finish_expert(0, writes)
    wait_in(crossed_v)
    cross_add(vec, cross_vec)
    hops_v = hop_start(vec, got_vec, 0)
    part_z(2)
    part_z_next(1)

    result.wait()
    wait_in(crossed_late)
    late = [
        local_start(source, target)
        for source, target in [(hidden, wide_f32), (landed, grad_mixed.at[pl.ds(0, capacity)])]
        + [
            (source.at[0], grad_projected.at[pl.ds(0, capacity), pl.ds(e * wide, wide)])
            for e, source in enumerate((rows_first, rows_second, landed_first))
        ]
    ]
    part_z(3)
    part_z_next(2)
    wait_in(hops_v)
    next_v = hop_next(vec, got_vec, hop_vec.at[1], hop_vec.at[0], 0)
    for one in late:
        one.wait()
    add_rows(first_columns, grad_projected, pl.ds(2 * wide, wide))
    add_rows(second_columns, grad_mixed, first_columns)
    wait_in([next_v])
    z_v = z_start(vec, got_vec, hop_vec.at[0], z_vec)
    part_z_next(3)

    def output_tiles(start, stop):
        @pl.loop(start, stop)
        def _(t):
            place = pl.ds(pl.multiple_of(t * TILE, TILE), TILE)
            branch[place, :] = (wide_f32[place, :] + tokens_order(place)).astype(BF16)

    output_tiles(0, rows // TILE // 2)
    z_next(vec, z_vec, z_v)
    for n in range(PARTS - 1):
        part_end(n)
    output_tiles(rows // TILE // 2, rows // TILE)
    stored.append(local_start(branch, block_out))
    wait_in(second_z_0[2:] + second_z_1[2:])
    for h in range(2):
        finish_half(1, h, [up[h, n, 0] for n in range(2)], z_second.at[h])
    finish_expert(1, writes)
    part_end(PARTS - 1)
    wait_in(z_v[1:])
    share_vectors[...] = z_total(vec, z_vec)
    wait_in(writes)
    for one in remote.made:
        if not any(one is other for other in second_hop + second_hop_late):
            one.wait_send()
    for one in stored:
        one.wait()


def backward_pass(moves, deep, big, row_parts, sums, stats, seg_row, marks, mixed, params):
    nz, nf = moves.nz, moves.nf
    rows, wide = mixed.shape
    share = wide // PARTS
    block = sums[0].shape[2:]
    half_block = (deep, block[1])
    capacity = row_parts[0].shape[1]
    anywhere = pl.BlockSpec(memory_space=pl.ANY)
    inside = pl.BlockSpec(memory_space=pltpu.VMEM)
    shape = jax.ShapeDtypeStruct
    landing = (2, nz) + block
    remote = 24 + 5 * PARTS + (PARTS + 7) * (nz - 1) + 2 * nz
    inputs = list(big) + list(row_parts) + list(sums)
    return pl.pallas_call(
        functools.partial(backward_kernel, moves, deep),
        in_specs=[anywhere] * len(inputs) + [inside] * 5,
        out_specs=[anywhere] * 4 + [inside] * 3 + [anywhere] * 5,
        out_shape=[
            shape((rows, wide), BF16),
            shape((rows, wide), F32),
            shape((EXPERTS, deep, 2 * block[1]), F32),
            shape((EXPERTS, block[0] * block[1] // wide, wide), F32),
            shape((deep, 3 * wide), F32),
            shape((deep, wide), F32),
            shape((deep, BLOCK), F32),
            shape(landing, BF16),
            shape(landing, BF16),
            shape(landing[1:], BF16),
            shape(landing[1:], BF16),
            shape((capacity, wide), BF16),
        ],
        scratch_shapes=[
            pltpu.VMEM((rows, 3 * wide), BF16),
            pltpu.VMEM((rows, rows), F32),
            pltpu.VMEM((rows, 3 * wide), BF16),
            pltpu.VMEM((rows, wide), BF16),
            pltpu.VMEM((rows, wide), BF16),
            pltpu.VMEM((rows, wide), BF16),
            pltpu.VMEM((rows, wide), BF16),
            pltpu.VMEM((rows, BLOCK), F32),
            pltpu.VMEM((rows, BLOCK), F32),
            pltpu.VMEM((PARTS, nz, 2, nf, deep, 4 * share), BF16),
            pltpu.VMEM((PARTS, nz, nf, deep, 4 * share), BF16),
            pltpu.VMEM((PARTS, 2, nz, deep, 4 * share), BF16),
            pltpu.VMEM((PARTS, nz, deep, 4 * share), BF16),
            pltpu.VMEM((PARTS, nz - 1, deep, 4 * share), BF16),
            pltpu.VMEM((PARTS, nz, deep, 4 * share), BF16),
            pltpu.VMEM((nz, 2, nf, deep, BLOCK), F32),
            pltpu.VMEM((nz, nf, deep, BLOCK), F32),
            pltpu.VMEM((2, nz, deep, BLOCK), F32),
            pltpu.VMEM((2, nz, deep, BLOCK), F32),
            pltpu.VMEM((nz - 1, deep, BLOCK), F32),
            pltpu.VMEM((2, 2, nz) + half_block, BF16),
            pltpu.VMEM((2, 2, nz) + half_block, BF16),
            pltpu.VMEM((2, nz) + half_block, BF16),
            pltpu.VMEM((2, nz - 1) + half_block, BF16),
            pltpu.VMEM((2, 2, nz - 1) + half_block, BF16),
            pltpu.VMEM((4,) + block, F32),
            pltpu.SemaphoreType.DMA((remote,)),
            pltpu.SemaphoreType.DMA((remote,)),
            pltpu.SemaphoreType.DMA((60 + 2 * nz,)),
        ],
        compiler_params=pltpu.CompilerParams(
            collective_id=1, has_side_effects=True, vmem_limit_bytes=63 * MIB
        ),
        cost_estimate=pl.CostEstimate(
            flops=30 * rows * wide * wide, bytes_accessed=80 * wide * wide, transcendentals=0
        ),
        name="backward_pass",
    )(*inputs, stats, seg_row, marks, mixed, params)


def gelu_both(value):
    square = value * value
    bent = jnp.tanh(ROOT_2_PI * value * (1.0 + CUBIC * square))
    half = 0.5 + 0.5 * bent
    slope = half + (0.5 * ROOT_2_PI) * value * (1.0 - bent * bent) * (1.0 + 3.0 * CUBIC * square)
    return (value * half, slope)


def expert_kernel(moves, mode, expert, deep, chunk, chunks, x_own, x_other, g_own, g_other, *refs):
    refs = list(refs)

    def take(count):
        taken, refs[:] = refs[:count], refs[count:]
        return taken

    if mode == "first":
        weights, columns_own = take(2), take(2)
    elif mode == "second":
        columns_own, pieces = take(2), take(2)
        first_grads, first_other = take(4), take(1)[0]
    else:
        weights = take(2)
    rows_own, rows_other = take(2)
    grads = take(2 if mode == "plain" else 4)
    if mode == "first":
        landing = take(2)
    elif mode == "second":
        got, hop, landed, own_z, landed_z = take(2), take(2), take(1)[0], *take(2)
    (win, wout, x, x_turned, g, branch, back, sum_in, sum_out, low_in, low_out) = take(11)
    w_sems, row_sems, out_sems = take(3)
    width = x.shape[1]
    rows = x.shape[0]
    capacity = rows // 2
    tiles = rows // TILE

    if mode != "plain":
        dp, flat = lax.axis_index("dp"), lax.axis_index("fsdp")
        zed, core = dp // 2, lax.rem(dp, 2)
        one_way = [moves.orders[n][0] for n in range(2)]
        other_way = [moves.orders[n][1] for n in range(2)]
        hops = {bit: (dp, flat ^ bit) for bit in moves.orders[0]}
        sibling = (zed * 2 + 1 - core, flat)
        devices = list(hops.values())
        if mode == "second":
            others = [((zed ^ k) * 2 + core, flat) for k in (1, 2)]
            devices += [sibling] + others
            up, spare, load_sems = take(3)
            half_rows = [pl.ds(h * deep, deep) for h in range(2)]
        barrier = pltpu.get_barrier_semaphore()
        for device in devices:
            pl.semaphore_signal(
                barrier, inc=1, device_id=device, device_id_type=pl.DeviceIdType.MESH
            )
        pl.semaphore_wait(barrier, len(devices))
        remote = Copies(*take(2))

    if mode == "first":
        near = [
            remote.start(columns_own[n], landing[n].at[other_way[n] - 1], hops[other_way[n]])
            for n in range(2)
        ]
        far = [
            remote.start(columns_own[n], landing[n].at[one_way[n] - 1], hops[one_way[n]])
            for n in range(2)
        ]
    elif mode == "second":
        hopped = {}

        def first_hop(h):
            for index in (1, 0):
                for n in range(2):
                    hopped[n, index, h] = remote.start(
                        first_grads[2 * n + 1].at[index, :, half_rows[h]],
                        got[n].at[index, :, half_rows[h]],
                        hops[one_way[n]],
                    )

        def half_sum(index, h, target):
            count = 2 if index else 3
            pairs = []
            for n in range(2):
                sources = [first_grads[2 * n].at[index], got[n].at[index], hop[n]][:count]
                places = [target.at[n], spare.at[n, 0], spare.at[n, 1]]
                for source, there in zip(sources, places):
                    pairs.append((source.at[:, half_rows[h]], there))
            begun = [
                pltpu.make_async_copy(source, there, load_sems.at[m])
                for m, (source, there) in enumerate(pairs)
            ]
            for one in begun:
                one.start()
            for one in begun:
                one.wait()

            @pl.loop(0, moves.nz)
            def _(k):
                for n in range(2):
                    arrived = [spare[n, m, k] for m in range(count - 1)]
                    target[n, k] = sum_low(target[n, k], *arrived).astype(BF16)

        def second_hop(h):
            wait_in([hopped[n, 1, h] for n in range(2)])
            half_sum(1, h, up.at[h])
            return [
                remote.start(up.at[h, n], hop[n].at[:, half_rows[h]], hops[other_way[n]])
                for n in range(2)
            ]

        first_hop(0)
        crossed = remote.start(first_other, landed, sibling)

    loads = []
    for n, (source, target) in enumerate(((x_own, x), (g_own, g), (x_other, x), (g_other, g))):
        place = pl.ds((n // 2) * capacity, capacity)
        loads.append(pltpu.make_async_copy(source.at[expert], target.at[place], row_sems.at[n]))
    copies = []
    if mode == "second":
        part_rows = chunk // moves.nf
        for offset in range(moves.nf):
            owner = flat ^ offset
            for k in range(moves.nz):
                sources = [
                    own.at[k] if offset == 0 else piece.at[offset - 1, k]
                    for own, piece in zip(columns_own, pieces)
                ]
                for part in range(2):
                    start = ((k * 2 + part) * moves.nf + owner) * deep
                    place = pl.ds(pl.multiple_of(start, deep), deep)
                    copies.append((sources[0].at[part], win.at[place]))
                start = (k * moves.nf + owner) * part_rows
                place = pl.ds(pl.multiple_of(start, part_rows), part_rows)
                copies.append((sources[1], wout.at[place]))
    else:
        copies = [(weights[0], win), (weights[1], wout)]
    loads += [
        pltpu.make_async_copy(source, target, w_sems.at[n])
        for n, (source, target) in enumerate(copies)
    ]
    for one in loads:
        one.start()
    branch[...] = jnp.zeros_like(branch)
    back[...] = jnp.zeros_like(back)
    for one in loads[:4]:
        one.wait()

    @pl.loop(0, tiles)
    def _(t):
        place = pl.ds(pl.multiple_of(t * TILE, TILE), TILE)
        x_turned[:, place] = x[place, :].T

    for one in loads[4:]:
        one.wait()

    def grad_copies(j):
        columns = pl.ds(pl.multiple_of(j * chunk, chunk), chunk)
        if mode == "plain":
            made = [(low_in, grads[0].at[:, columns]), (low_out, grads[1].at[columns])]
        else:
            made = []
            k_of = zed ^ j
            half_deep = chunk // moves.nf // 2
            for stream in range(2):
                offsets = moves.relative(stream)
                half = len(offsets) // 2
                for number, offset in enumerate(offsets):
                    target = grads[stream * 2 + number // half].at[number % half]
                    owner = flat ^ offset
                    for part in range(2):
                        if stream == 0:
                            for k in range(moves.nz):
                                start = (((zed ^ k) * 2 + part) * moves.nf + owner) * deep
                                place = pl.ds(pl.multiple_of(start, deep), deep)
                                there = target.at[k, pl.ds(part * deep, deep), columns]
                                made.append((low_in.at[place], there))
                        else:
                            start = (owner * 2 + part) * half_deep
                            place = pl.ds(pl.multiple_of(start, half_deep), half_deep)
                            there = target.at[k_of, :, pl.ds(part * width, width)]
                            made.append((low_out.at[place], there))
        return [
            pltpu.make_async_copy(source, target, out_sems.at[n])
            for n, (source, target) in enumerate(made)
        ]

    def chunk_step(j):
        columns = pl.ds(pl.multiple_of(j * chunk, chunk), chunk)
        sum_in[...] = jnp.zeros_like(sum_in)
        sum_out[...] = jnp.zeros_like(sum_out)

        @pl.loop(0, tiles)
        def _(t):
            place = pl.ds(pl.multiple_of(t * TILE, TILE), TILE)
            g_tile = g[place, :]
            inner = dot(x[place, :], win[:, columns])
            grad_active = dot_nt(g_tile, wout[columns, :])
            active, slope = gelu_both(inner)
            active_low = active.astype(BF16)
            grad_inner = (grad_active * slope).astype(BF16)
            branch[place, :] += dot(active_low, wout[columns, :])
            back[place, :] += dot_nt(grad_inner, win[:, columns])
            sum_in[...] += dot(x_turned[:, place], grad_inner)
            sum_out[...] += dot_tn(active_low, g_tile)

        @pl.when(j > 0)
        def _():
            for one in grad_copies(j - 1):
                one.wait()

        low_in[...] = sum_in[...].astype(BF16)
        low_out[...] = sum_out[...].astype(BF16)
        for one in grad_copies(j):
            one.start()

    def run_chunks(start, stop):
        @pl.loop(start, stop)
        def _(j):
            chunk_step(j)

    if mode == "plain":
        run_chunks(0, chunks)
    elif mode == "first":
        run_chunks(0, chunks // 2)
        wait_in(near)
        far += [
            remote.start(
                landing[n].at[other_way[n] - 1],
                landing[n].at[(one_way[n] ^ other_way[n]) - 1],
                hops[one_way[n]],
            )
            for n in range(2)
        ]
        run_chunks(chunks // 2, chunks)
    else:
        run_chunks(0, chunks // 4)
        last = second_hop(0)
        first_hop(1)
        run_chunks(chunks // 4, chunks // 2)
        wait_in([hopped[n, 0, 0] for n in range(2)] + last)
        half_sum(0, 0, up.at[2])
        z_sent = [
            remote.start(up.at[2, n, k], landed_z.at[n, k // 2], others[0])
            for k in (3, 1)
            for n in range(2)
        ]
        own = pltpu.make_async_copy(up.at[2, :, 0], own_z, load_sems.at[0])
        own.start()
        own.wait()
        run_chunks(chunks // 2, chunks - 1)
        last = second_hop(1)
        wait_in(z_sent[:2])
        begun = [
            pltpu.make_async_copy(landed_z.at[n, 1], spare.at[n, 0, 0], load_sems.at[n])
            for n in range(2)
        ]
        for one in begun:
            one.start()
        for one in begun:
            one.wait()
        for n in range(2):
            up[2, n, 2] = sum_low(up[2, n, 2], spare[n, 0, 0]).astype(BF16)
            z_sent.append(remote.start(up.at[2, n, 2], landed_z.at[n, 2], others[1]))
        run_chunks(chunks - 1, chunks)

    @pl.loop(0, tiles)
    def _(t):
        place = pl.ds(pl.multiple_of(t * TILE, TILE), TILE)
        x[place, :] = branch[place, :].astype(BF16)
        g[place, :] = back[place, :].astype(BF16)

    stored = []
    for n, (source, target) in enumerate(
        ((x, rows_own.at[0]), (g, rows_own.at[1]), (x, rows_other.at[0]), (g, rows_other.at[1]))
    ):
        place = pl.ds((n // 2) * capacity, capacity)
        stored.append(pltpu.make_async_copy(source.at[place], target, row_sems.at[n]))
    for one in stored:
        one.start()
    for one in grad_copies(chunks - 1) + stored:
        one.wait()
    if mode == "first":
        wait_in(far)
    elif mode == "second":
        wait_in([hopped[n, 0, 1] for n in range(2)] + last + z_sent[2:] + [crossed])
    if mode != "plain":
        for one in remote.made:
            one.wait_send()


def expert_block(moves, mode, expert, sorted_rows, extra, deep, half_hidden, grad_shapes, landing):
    capacity, width = sorted_rows[0].shape[1:]
    rows = 2 * capacity
    chunks = 4 if mode == "plain" else moves.nz
    chunk = half_hidden // chunks
    anywhere = pl.BlockSpec(memory_space=pl.ANY)
    row_shape = jax.ShapeDtypeStruct((2, capacity, width), BF16)
    outs = [row_shape] * 2 + grad_shapes + landing
    scratch = [
        pltpu.VMEM((width, half_hidden), BF16),
        pltpu.VMEM((half_hidden, width), BF16),
        pltpu.VMEM((rows, width), BF16),
        pltpu.VMEM((width, rows), BF16),
        pltpu.VMEM((rows, width), BF16),
        pltpu.VMEM((rows, width), F32),
        pltpu.VMEM((rows, width), F32),
        pltpu.VMEM((width, chunk), F32),
        pltpu.VMEM((chunk, width), F32),
        pltpu.VMEM((width, chunk), BF16),
        pltpu.VMEM((chunk, width), BF16),
    ]
    copies = 2 if mode == "plain" else 4 * moves.nz * moves.nf
    scratch += [
        pltpu.SemaphoreType.DMA((copies,)),
        pltpu.SemaphoreType.DMA((4,)),
        pltpu.SemaphoreType.DMA((copies,)),
    ]
    options = {}
    if mode == "second":
        block = (moves.nz, deep, half_hidden)
        scratch += [
            pltpu.VMEM((3, 2) + block, BF16),
            pltpu.VMEM((2, 2) + block, BF16),
            pltpu.SemaphoreType.DMA((6,)),
        ]
    if mode != "plain":
        count = 13 + 2 * (moves.nz - 1) if mode == "second" else 6
        scratch += [pltpu.SemaphoreType.DMA((count,))] * 2
        options = {"collective_id": 2 + expert, "has_side_effects": True}
    return pl.pallas_call(
        functools.partial(expert_kernel, moves, mode, expert, deep, chunk, chunks),
        in_specs=[anywhere] * (4 + len(extra)),
        out_specs=[anywhere] * len(outs),
        out_shape=outs,
        scratch_shapes=scratch,
        compiler_params=pltpu.CompilerParams(vmem_limit_bytes=58 * MIB, **options),
        cost_estimate=pl.CostEstimate(
            flops=12 * rows * width * half_hidden,
            bytes_accessed=8 * width * half_hidden + 16 * rows * width,
            transcendentals=rows * half_hidden,
        ),
        name="expert_" + mode,
    )(*sorted_rows, *extra)


def gather_experts_whole(w_expert_in, w_expert_out, core, nz):
    width, hidden = w_expert_out.shape[2], w_expert_in.shape[2]
    all_in = lax.all_gather(w_expert_in, AXES, axis=1, tiled=True)
    all_out = lax.all_gather(w_expert_out, AXES, axis=1, tiled=True)
    all_in = all_in.reshape(EXPERTS, width, nz, 2, hidden // (2 * nz))
    all_in = lax.dynamic_index_in_dim(all_in, core, 3, False)
    all_in = all_in.reshape(EXPERTS, width, hidden // 2)
    all_out = all_out.reshape(EXPERTS, nz, 2, hidden // (2 * nz), width)
    all_out = lax.dynamic_index_in_dim(all_out, core, 2, False)
    all_out = all_out.reshape(EXPERTS, hidden // 2, width)
    return [[all_in[e], all_out[e]] for e in range(EXPERTS)]


def local(
    nd,
    nf,
    tokens,
    seq_lengths,
    expert_ids,
    grad_out,
    ln1_gain,
    ln1_bias,
    w_qkv,
    w_attn_out,
    ln2_gain,
    ln2_bias,
    w_expert_in,
    w_expert_out,
):
    rows, width = tokens.shape
    deep = w_qkv.shape[0]
    moves = Moves(nd, nf)
    staged = deep % 32 == 0 and nf == 4 and moves.nz == 4
    core = lax.rem(lax.axis_index("dp"), 2)
    zed = lax.axis_index("dp") // 2
    flat = lax.axis_index("fsdp")

    positions = jnp.arange(rows, dtype=jnp.int32)
    bounds = jnp.cumsum(seq_lengths[0])
    segment = jnp.sum((positions[:, None] >= bounds[None, :]).astype(jnp.int32), axis=1)
    seg_row = jnp.broadcast_to(segment[None, :], (8, rows))
    seg_col = jnp.broadcast_to(segment[:, None], (rows, BLOCK))
    routed = expert_ids[:, 0]
    rank_second = jnp.cumsum(routed) - routed
    capacity = 3 * rows // 4
    slot = jnp.where(routed == 1, capacity + rank_second, positions - rank_second)

    params = jnp.stack([ln1_gain, ln1_bias, ln2_gain, ln2_bias], axis=1)
    params = jnp.pad(params, ((0, 0), (0, BLOCK - 4)))
    mine = jnp.concatenate([w_qkv, w_attn_out, params], axis=1)
    arguments = (tokens, grad_out, mine, w_expert_in, w_expert_out)
    if staged:
        return staged_block(moves, arguments, seg_row, seg_col, slot, (zed, core, flat))
    return plain_block(moves, arguments, seg_row, seg_col, slot, (zed, core, flat))


def staged_block(moves, arguments, seg_row, seg_col, slot, place):
    tokens, grad_out, mine, w_expert_in, w_expert_out = arguments
    rows, width = tokens.shape
    deep, hidden = w_expert_in.shape[1:]
    half_hidden = hidden // 2
    capacity = 3 * rows // 4
    zed, core, flat = place
    slot_row = jnp.broadcast_to(slot[None, :], (8, rows))
    lane = jnp.arange(BLOCK, dtype=jnp.int32)[None, :]
    marks = jnp.where(lane == 0, seg_col, slot[:, None])
    outs = forward_pass(
        moves, tokens, mine, w_expert_in, w_expert_out, seg_row, marks, slot_row, grad_out
    )
    whole_qkv, whole_attn, params, first_in = [one.reshape(-1, one.shape[-1]) for one in outs[:4]]
    first_out = outs[4].reshape(half_hidden, width)
    columns = list(outs[5:7])
    sorted_other, grad_other = outs[7:9]
    normed_one, projected, mixed, stats, hidden_one, sorted_rows, grad_sorted = outs[9:]
    by_expert = lambda value: value.reshape(EXPERTS, capacity, width)
    row_inputs = [by_expert(one) for one in (sorted_rows, sorted_other, grad_sorted, grad_other)]
    shape = lambda *dims: jax.ShapeDtypeStruct(dims, BF16)
    nz, nf = moves.nz, moves.nf
    block = (nz, 2 * deep, half_hidden)
    grad_shapes = [shape(nf // 2, *block)] * 4
    first = expert_block(
        moves,
        "first",
        0,
        row_inputs,
        [first_in, first_out] + columns,
        deep,
        half_hidden,
        grad_shapes,
        [shape(nf - 1, *one.shape) for one in columns],
    )
    second = expert_block(
        moves,
        "second",
        1,
        row_inputs,
        columns + list(first[6:8]) + list(first[2:6]) + [first[1]],
        deep,
        half_hidden,
        grad_shapes,
        [shape(2, *block)] * 2
        + [shape(*block)] * 2
        + [shape(2, capacity, width)]
        + [shape(2, deep, half_hidden), shape(2, nz - 1, deep, half_hidden)],
    )
    landed = second[10]
    results = backward_pass(
        moves,
        deep,
        [projected, whole_qkv, whole_attn, hidden_one, normed_one, tokens, grad_out],
        [first[0], second[0], landed, second[1]],
        [first[2], first[4]] + list(second[6:10]) + list(second[11:13]) + list(second[2:6]),
        stats,
        seg_row,
        marks,
        mixed,
        params,
    )
    block_result, grad_input, share_in, share_out, share_qkv, share_attn, vectors = results[:7]
    vectors = vectors[:, :4].T
    return (
        block_result,
        grad_input,
        vectors[0],
        vectors[1],
        share_qkv,
        share_attn,
        vectors[2],
        vectors[3],
        share_in,
        share_out,
    )


def plain_block(moves, arguments, seg_row, seg_col, slot, place):
    tokens, grad_out, mine, w_expert_in, w_expert_out = arguments
    rows, width = tokens.shape
    hidden = w_expert_in.shape[2]
    deep = mine.shape[0]
    nz = moves.nz
    zed, core, flat = place
    capacity = 3 * rows // 4
    whole = lax.all_gather(mine, AXES, axis=0, tiled=True)
    whole_qkv, whole_attn = whole[:, : 3 * width], whole[:, 3 * width : 4 * width]
    params = whole[:, 4 * width :]
    expert_weights = gather_experts_whole(w_expert_in, w_expert_out, core, nz)
    gain_one, bias_one, gain_two, bias_two = [
        params[:, n].astype(F32)[None, :] for n in range(4)
    ]
    tokens_wide = tokens.astype(F32)
    scaled_one, inverse_one = norm_parts(tokens_wide)
    normed_one = (scaled_one * gain_one + bias_one).astype(BF16)
    projected = dot(normed_one, whole_qkv).astype(BF16)
    mixed, stats = attention_forward(projected, seg_row, seg_col, 0, width // BLOCK)
    hidden_one = tokens_wide + dot(mixed, whole_attn)
    scaled_two, inverse_two = norm_parts(hidden_one)
    normed_two = (scaled_two * gain_two + bias_two).astype(BF16)
    slots = jnp.arange(EXPERTS * capacity, dtype=jnp.int32)[:, None]
    spread = (slots == slot[None, :]).astype(BF16)
    by_expert = lambda value: value.reshape(EXPERTS, capacity, width)
    row_inputs = []
    for value in (normed_two, grad_out):
        ordered = dot(spread, value).astype(BF16)
        row_inputs += [by_expert(ordered), by_expert(moves.core(ordered))]
    results, grad_pieces = [], []
    for e in range(EXPERTS):
        weights = expert_weights[e]
        shapes = [jax.ShapeDtypeStruct(one.shape, BF16) for one in weights]
        outs = expert_block(
            moves, "plain", e, row_inputs, weights, deep, hidden // 2, shapes, []
        )
        results.append(add_low(outs[0], moves.core(outs[1])))
        grad_pieces.append(outs[2:])
    both = jnp.concatenate(results, axis=1)
    grad_normed_two = dot_tn(spread, both[1])
    block_result = (hidden_one + dot_tn(spread, both[0])).astype(BF16)
    grad_hidden = grad_out.astype(F32) + norm_back(
        grad_normed_two, scaled_two, inverse_two, gain_two
    )
    grad_branch = grad_hidden.astype(BF16)
    grad_mixed = dot_nt(grad_branch, whole_attn).astype(BF16)
    trio = attention_backward(
        projected, grad_mixed, stats.T, seg_row, seg_col, 0, width // BLOCK
    )
    grad_projected = jnp.concatenate(trio, axis=1)
    grad_normed_one = dot_nt(grad_projected, whole_qkv)
    grad_input = grad_hidden + norm_back(grad_normed_one, scaled_one, inverse_one, gain_one)
    vectors = jnp.stack(
        [
            jnp.sum(grad_normed_one * scaled_one, axis=0),
            jnp.sum(grad_normed_one, axis=0),
            jnp.sum(grad_normed_two * scaled_two, axis=0),
            jnp.sum(grad_normed_two, axis=0),
        ]
    )
    own = lambda value, dim: lax.psum_scatter(value, AXES, scatter_dimension=dim, tiled=True)
    vectors = own(vectors, 1)
    full_in = jnp.stack([pieces[0] for pieces in grad_pieces])
    full_out = jnp.stack([pieces[1] for pieces in grad_pieces])
    full_in = full_in.reshape(EXPERTS, width, nz, 1, -1).astype(F32)
    full_out = full_out.reshape(EXPERTS, nz, 1, -1, width).astype(F32)
    chosen = jnp.arange(2) == core
    full_in = jnp.where(chosen[None, None, None, :, None], full_in, 0.0)
    full_out = jnp.where(chosen[None, None, :, None, None], full_out, 0.0)
    return (
        block_result,
        grad_input,
        vectors[0],
        vectors[1],
        own(dot_tn(normed_one, grad_projected), 0),
        own(dot_tn(mixed, grad_branch), 0),
        vectors[2],
        vectors[3],
        own(full_in.reshape(EXPERTS, width, hidden), 1),
        own(full_out.reshape(EXPERTS, hidden, width), 1),
    )


def solution(mesh):
    rows = P(AXES, None)
    vector = P(AXES)
    expert = P(None, AXES, None)
    return jax.shard_map(
        functools.partial(local, mesh.shape["dp"], mesh.shape["fsdp"]),
        mesh=mesh,
        in_specs=(
            rows, rows, rows, rows, vector, vector, rows, rows, vector, vector, expert, expert
        ),
        out_specs=(
            rows, rows, vector, vector, rows, rows, vector, vector, expert, expert
        ),
        check_vma=False,
    )
```
